32 devices in a mesh: pods: 2 (over y), inst: 4 (over z), tp: 4 (over x, core).
Axes of the slice: x: 2, y: 2, z: 4, core: 2. Of those that a mesh axis runs over, the one named last changes fastest.
Arguments:
- queries: bfloat16 [2048, 4096], P(('pods', 'inst'), 'tp'), parts along dimension 0, may hold values from -62 to 62
- cache_store: bfloat16 [2, 2048, 16, 512], P(None, ('pods', 'inst'), None, 'tp'), parts along dimension 1, may hold values from -6 to 6
- span_cache: bfloat16 [2, 2048, 512], P(None, ('pods', 'inst'), 'tp'), parts along dimension 1, may hold values from -6 to 6
- out_weight: bfloat16 [4096, 4096], P('tp'), may hold values from -0.5 to 0.5
- prefix_blocks: int32 [8], P(('pods', 'inst')), parts along dimension 0, may hold values from 1 to 512, 1280 in all
- span_lengths: int32 [8], P(('pods', 'inst')), parts along dimension 0, may hold values from 1 to 256, 768 in all
- hit_holders: int32 [8, 512, 1], P(('pods', 'inst')), parts along dimension 0, may hold values from 0 to 3; in each aligned block of 512 rows (0 to 511, 512 to 1023, ..., all dimensions but the last counted through in order) at most 160 rows name the same one
- hit_slots: int32 [8, 512], P(('pods', 'inst')), parts along dimension 0, may hold values from 0 to 255
- store_owners: int32 [8, 16, 1], P(('pods', 'inst')), parts along dimension 0, may hold values from 0 to 3; in each aligned block of 16 rows (0 to 15, 16 to 31, ..., all dimensions but the last counted through in order) at most 8 rows name the same one
Outputs:
- projected: bfloat16 [2048, 4096], P(('pods', 'inst', 'tp')), parts along dimension 0
- pushed_blocks: bfloat16 [2, 256, 16, 512], P(None, ('pods', 'inst'), None, 'tp'), parts along dimension 1
The draws below stay inside these ranges and needn't reach their ends.
There are 2 independent parts, one for each index of `pods`. The reference program is written for one: setup_inputs(seed, part) draws one part's arguments, and reference() takes and returns one part's arrays. A program takes and returns all parts, laid end to end along the dimension named above; an argument that names none is the same for every part. Nothing has to cross between parts.
Inputs may be any that keep to these rules, and one draw needn't show every extreme that they name: `prefix_blocks`: the largest equals 512; they sum to 1280. `span_lengths`: the largest equals 256; they sum to 768. `hit_holders`: among the 512 entries of one instance no holder appears more than 160 times, and some instance names some holder exactly 160 times. Entries past the live prefix are present too. `store_owners`: among the 16 blocks of one instance no owner appears more than 8 times, and some instance names some owner exactly 8 times.
All inputs are finite; a program needn't handle non-finite values. No bound on the sum of `prefix_blocks` or of `span_lengths` on one device may be relied on, other than what follows from the above.
Results may differ from the reference program's by a relative error of at most 0.013.
Values may be sent and summed in bfloat16 or wider, within the bound.
No kernel may reach another device: no remote copies, remote signals or barrier semaphores. Data moves between devices by JAX's collectives and lax.ppermute only.
A program may use at most 128 MiB of HBM per device.

```python
import math
from functools import partial
import jax
import jax.numpy as jnp
import numpy as np
from jax import lax

HD = 128
HPK = 8
DW = 4096
BS = 16
SPAN = 256
MAXB = 512
SLOTS = 256
HEADS = 32
KV_HEADS = 4
TOKENS = 1024
NB = 16
PULLCAP = 160
PUSHCAP = 8
N_INST = 4


def draw_queries(key, part):
    key = jax.random.fold_in(key, 7)
    noise_key = jax.random.fold_in(key, 0)
    full_shape = (TOKENS, HEADS * HD)
    values = jnp.clip(1.5 * jax.random.normal(noise_key, full_shape, jnp.float32), -9.0, 9.0)
    return values.astype(jnp.bfloat16)


def place_ends(entries, rng, least, top_value):
    longest = entries.shape.index(max(entries.shape))
    spots = []
    for shift in (0, 1):
        where = [jax.random.randint(jax.random.fold_in(rng, axis), (), 0, length) for axis, length in enumerate(entries.shape)]
        where[longest] = (where[longest] + shift) % entries.shape[longest]
        spots.append(tuple(where))
    return entries.at[spots[0]].set(least).at[spots[1]].set(top_value)


def block_levels(stream_key, dims, cuts, smallest, largest):
    level, own = 1.0, jax.random.fold_in(stream_key, 6)
    for dim, blocks in cuts:
        heights = jnp.exp(jax.random.uniform(jax.random.fold_in(own, dim), (blocks,), jnp.float32, smallest / len(cuts), largest / len(cuts)))
        level = level * jnp.repeat(heights, dims[dim] // blocks).reshape([-1 if axis == dim else 1 for axis in range(len(dims))])
    return level


def length_profile(amount, total, bound, slope):
    loads = [(1 << 20) // math.isqrt(standing ** slope) + 1 for standing in range(2, amount + 1)]
    spare, counts = total - bound - (amount - 1), [1] * (amount - 1)
    while spare > 0:
        free = [i for i in range(amount - 1) if counts[i] < bound]
        mass, remaining = sum([loads[i] for i in free]), spare
        for i in free:
            addition = min(bound - counts[i], max(1, remaining * loads[i] // mass), spare)
            counts[i] = counts[i] + addition
            spare = spare - addition
    return np.array([bound] + counts)


def uneven(stream_key, number_of, total, most, lean):
    if number_of == 2:
        one = jax.random.randint(stream_key, (), max(1, total - most), min(most, total - 1) + 1)
        return jnp.stack([one, total - one])
    sizes = jnp.asarray(length_profile(number_of, total, most, lean), jnp.int32)
    couples = (number_of - 1) // 2
    giver, sink = sizes[1:1 + 2 * couples:2], sizes[2:2 + 2 * couples:2]
    slack = jnp.minimum(giver - 1, most - sink)
    shifted = jax.random.randint(jax.random.fold_in(stream_key, 1), (couples,), 0, 1 << 20) % (slack + 1)
    sizes = sizes.at[1:1 + 2 * couples:2].set(giver - shifted).at[2:2 + 2 * couples:2].set(sink + shifted)
    return sizes[jax.random.permutation(jax.random.fold_in(stream_key, 2), number_of)]


def routed_block(own_key, own, number, rows, amount, top, most, lean):
    order = jax.random.permutation(own_key, amount)
    crowded, common = shares(amount, rows * top, most, lean, True), shares(amount, rows * top, most, lean, False)
    places = jnp.arange(amount)

    def named(tallies, rotation):
        used = int((tallies > 0).sum())
        fixed = max(1, used // 4)
        moved = fixed + (places - fixed + rotation * (used - fixed)) % max(1, amount - fixed)
        return jnp.zeros((amount,), jnp.int32).at[order[jnp.where(places < fixed, places, moved)]].set(jnp.asarray(tallies, jnp.int32))

    tallies = jnp.where(number % 4 == 0, named(crowded, number // 4), named(common, number - number // 4 - 1))
    mixed = jax.random.permutation(jax.random.fold_in(own, 3), amount)
    source_of, receiver = mixed[0:amount // 2 * 2:2], mixed[1:amount // 2 * 2:2]
    slack = jnp.minimum(tallies[source_of] - 1, most - tallies[receiver]) // 2
    slack = jnp.where((source_of == order[0]) | (receiver == order[0]) | (tallies[receiver] == 0), 0, jnp.maximum(slack, 0))
    moved = jax.random.randint(jax.random.fold_in(own, 4), (amount // 2,), 0, 1 << 20) % (slack + 1)
    tallies = tallies.at[source_of].add(-moved).at[receiver].add(moved)
    members = jnp.searchsorted(jnp.cumsum(tallies), jnp.arange(rows * top), side="right").astype(jnp.int32)
    grid = members.reshape(top, rows).T
    grid = grid[jax.random.permutation(jax.random.fold_in(own, 1), rows)]
    rotation = jax.random.randint(jax.random.fold_in(own, 2), (rows, 1), 0, top)
    return jnp.take_along_axis(grid, (jnp.arange(top)[None, :] + rotation) % top, axis=1)


def shares(number_of, total, reach, skew, full):
    weights = [(1 << 20) // math.isqrt(rank ** skew) + 1 for rank in range(1, number_of + 1)]
    largest = reach if full else min(reach, max(-(-total // number_of), total * weights[0] // sum(weights)))
    least = 1 if total - largest >= number_of - 1 else 0
    given, surplus = [largest] + [least] * (number_of - 1), total - largest - least * (number_of - 1)
    while surplus > 0:
        movable = [i for i in range(1, number_of) if given[i] < largest] or [i for i in range(1, number_of) if given[i] < reach]
        mass, left = sum([weights[i] for i in movable]), surplus
        for i in movable:
            addition = min(reach - given[i], max(1, left * weights[i] // mass), surplus)
            given[i] = given[i] + addition
            surplus = surplus - addition
    return np.array(given)


def noise(rng, dims, scale, limit, cuts=(), held_as=jnp.bfloat16):
    loudness = block_levels(rng, dims, cuts, -0.22, 0.18) if cuts else 1.0
    entries = jax.random.normal(rng, dims, jnp.float32) * scale * loudness
    return jnp.minimum(jnp.maximum(entries, -limit), limit).astype(held_as)


def setup_inputs(seed: int = 0, part: int = 0) -> dict:
    keys = jax.random.split(jax.random.key(seed), 10)
    part_splits = jax.random.split(jax.random.fold_in(keys[9], part), 10)
    queries = draw_queries(jax.random.fold_in(jax.random.fold_in(keys[9], part), 71), part)
    cache_store = noise(part_splits[1], (2, N_INST * SLOTS, BS, KV_HEADS * HD), 1.0, 6.0, ((1, 4), (3, 4)))
    span_cache = noise(part_splits[2], (2, TOKENS, KV_HEADS * HD), 1.0, 6.0, ((1, 4), (2, 4)))
    out_weight = noise(keys[3], (HEADS * HD, DW), HD ** -0.5, 0.5, ((0, 4),))
    prefix_blocks = uneven(part_splits[4], N_INST, N_INST * MAXB * 5 // 8, MAXB, 1).astype(jnp.int32)
    span_lengths = uneven(part_splits[5], N_INST, N_INST * SPAN * 3 // 4, SPAN, 1).astype(jnp.int32)
    hit_holders_keys = jax.random.split(jax.random.fold_in(part_splits[6], 1), N_INST * MAXB // MAXB)
    hit_holders_turns = jax.random.permutation(jax.random.fold_in(part_splits[6], 3), N_INST * MAXB // MAXB)
    hit_holders = jax.vmap(lambda own, number: routed_block(jax.random.fold_in(part_splits[6], 2), own, number, MAXB, N_INST, 1, PULLCAP, 2))(hit_holders_keys, hit_holders_turns).reshape((N_INST, MAXB, 1))
    hit_slots = place_ends(jax.random.randint(part_splits[7], (N_INST, MAXB), 0, SLOTS), jax.random.fold_in(part_splits[7], 1), 0, SLOTS - 1).astype(jnp.int32)
    store_owners_keys = jax.random.split(jax.random.fold_in(part_splits[8], 1), N_INST * NB // NB)
    store_owners_turns = jax.random.permutation(jax.random.fold_in(part_splits[8], 3), N_INST * NB // NB)
    store_owners = jax.vmap(lambda own, number: routed_block(jax.random.fold_in(part_splits[8], 2), own, number, NB, N_INST, 1, PUSHCAP, 1))(store_owners_keys, store_owners_turns).reshape((N_INST, NB, 1))
    return {"queries": queries, "cache_store": cache_store, "span_cache": span_cache, "out_weight": out_weight, "prefix_blocks": prefix_blocks, "span_lengths": span_lengths, "hit_holders": hit_holders, "hit_slots": hit_slots, "store_owners": store_owners}


def slot_ranks(labels, number):
    onehot = (labels[:, None] == jnp.arange(number, dtype=jnp.int32)[None, :]).astype(jnp.int32)
    before = jnp.cumsum(onehot, axis=0) - onehot
    return lax.optimization_barrier(jnp.sum(before * onehot, axis=1)).astype(jnp.int32)

def attend_group(query_group, key_rows, value_rows, usable):
    scores = jnp.einsum('thd,kd->htk', query_group, key_rows) / math.sqrt(HD)
    row_max = lax.optimization_barrier(jnp.max(jnp.where(usable[None], scores, -1e+30), axis=-1, keepdims=True))
    weights = jnp.where(usable[None], jnp.exp(scores - row_max), 0.0)
    total_weight = lax.optimization_barrier(jnp.sum(weights, axis=-1))
    rounded = lax.optimization_barrier(weights.astype(jnp.bfloat16)).astype(query_group.dtype)
    summed = jnp.einsum('htk,kd->thd', rounded, value_rows)
    return summed / jnp.transpose(total_weight)[:, :, None]

def reference(queries, cache_store, span_cache, out_weight, prefix_blocks, span_lengths, hit_holders, hit_slots, store_owners):
    head_cols = KV_HEADS * HD
    query_sets = queries.reshape(N_INST, SPAN, HEADS * HD)
    span_sets = jnp.transpose(span_cache.reshape(2, N_INST, SPAN, head_cols), (1, 0, 2, 3))

    def one_member(packed):
        query_set, span_set, prefix_count, span_count, holder_row, slot_row = packed
        rows = (holder_row[:, 0] * SLOTS + slot_row).astype(jnp.int32)
        prefix_vals = jnp.take(cache_store, rows, axis=1).reshape(2, MAXB * BS, head_cols)
        keys_all = jnp.concatenate([prefix_vals, span_set], axis=1).astype(jnp.float32)
        prefix_ok = jnp.arange(MAXB * BS, dtype=jnp.int32) < prefix_count * BS
        column = jnp.arange(SPAN, dtype=jnp.int32)
        span_ok = (column[None, :] <= column[:, None]) & (column[None, :] < span_count)
        usable = jnp.concatenate([jnp.broadcast_to(prefix_ok[None, :], (SPAN, MAXB * BS)), span_ok], axis=1)
        query_full = query_set.astype(jnp.float32).reshape(SPAN, HEADS, HD)

        def one_group(group):
            query_group = lax.dynamic_slice_in_dim(query_full, group * HPK, HPK, 1)
            key_rows = lax.dynamic_slice_in_dim(keys_all[0], group * HD, HD, 1)
            value_rows = lax.dynamic_slice_in_dim(keys_all[1], group * HD, HD, 1)
            return attend_group(query_group, key_rows, value_rows, usable)
        grouped = lax.map(one_group, jnp.arange(KV_HEADS, dtype=jnp.int32))
        return jnp.transpose(grouped, (1, 0, 2, 3)).reshape(SPAN, HEADS * HD).astype(jnp.bfloat16)
    attended = lax.map(one_member, (query_sets, span_sets, prefix_blocks, span_lengths, hit_holders, hit_slots))
    attended = attended.reshape(TOKENS, HEADS * HD)
    projected = jnp.dot(attended, out_weight, preferred_element_type=jnp.float32)
    token_pos = jnp.arange(TOKENS, dtype=jnp.int32) % SPAN
    member = jnp.arange(TOKENS, dtype=jnp.int32) // SPAN
    live = token_pos < jnp.take(span_lengths, member)
    projected = jnp.where(live[:, None], projected, 0.0).astype(jnp.bfloat16)
    fresh = jnp.where(live[None, :, None], span_cache, jnp.zeros_like(span_cache))
    fresh = fresh.reshape(2, N_INST * NB, BS, head_cols)
    targets = store_owners[:, :, 0]
    ranks = jax.vmap(partial(slot_ranks, number=N_INST))(targets)
    senders = jnp.arange(N_INST, dtype=jnp.int32)[:, None]
    destination = (targets * (N_INST * PUSHCAP) + senders * PUSHCAP + ranks).reshape(-1).astype(jnp.int32)
    pushed_blocks = jnp.zeros((2, N_INST * N_INST * PUSHCAP, BS, head_cols), jnp.bfloat16).at[:, destination].set(fresh)
    return (projected, pushed_blocks)
```

```python
import functools
import math

import jax
import jax.numpy as jnp
from jax import lax
from jax.experimental import pallas as pl
from jax.experimental.pallas import tpu as pltpu
from jax.sharding import PartitionSpec as P

LOW = -1e30
TILE = 16
VMEM_LIMIT = 48 * 1024 * 1024

SMEM = pl.BlockSpec(memory_space=pltpu.SMEM)
VMEM = pl.BlockSpec(memory_space=pltpu.VMEM)


def round_up(number, step):
    return -(-number // step) * step


def route_kernel(peers, me_ref, live_ref, holders_ref, slots_ref, lists_ref):
    last = lists_ref.shape[1] - 1
    me = me_ref[0]
    for k in range(peers):
        lists_ref[k, last] = 0

    def step(j, carry):
        away = holders_ref[j] - me
        away = jnp.where(away < 0, away + peers, away)
        count = lists_ref[away, last]
        lists_ref[away, count] = slots_ref[j]
        lists_ref[away, last] = count + 1
        return carry

    lax.fori_loop(0, live_ref[0], step, 0)


def route(me, live, holders, slots, peers, cap):
    width = round_up(cap + 1, 128)
    return pl.pallas_call(
        functools.partial(route_kernel, peers),
        out_shape=jax.ShapeDtypeStruct((peers, width), jnp.int32),
        in_specs=[SMEM] * 4,
        out_specs=SMEM,
        name="route",
    )(me, live, holders, slots)


def absorb_tile(keys, values_ref, q_ref, max_ref, acc_ref, scale, mask=None):
    heads, _, rows = max_ref.shape
    head_dim = keys.shape[1]
    values = values_ref[...]
    for g in range(heads):
        q = q_ref[:, g * head_dim : (g + 1) * head_dim]
        s = lax.dot_general(
            keys, q, (((1,), (1,)), ((), ())), preferred_element_type=jnp.float32
        )
        if mask is not None:
            s = jnp.where(mask, s, LOW)
        old = max_ref[g]
        new = jnp.maximum(old, jnp.max(s, axis=0, keepdims=True))
        p = jnp.exp2((s - new) * scale).astype(jnp.bfloat16)
        update = jnp.dot(values, p, preferred_element_type=jnp.float32)
        acc_ref[g] = acc_ref[g] * jnp.exp2((old - new) * scale) + update
        max_ref[g] = new


def put_values(values, valid_keys, vt_ref):
    head_dim = values.shape[1]
    keys = values.shape[0]
    vt_ref[:head_dim, :] = values.T
    row = lax.broadcasted_iota(jnp.int32, (16, keys), 0)
    col = lax.broadcasted_iota(jnp.int32, (16, keys), 1)
    vt_ref[head_dim:, :] = jnp.where((row == 0) & (col < valid_keys), 1.0, 0.0).astype(
        jnp.bfloat16
    )


def absorb_blocks(list_ref, q_ref, store_ref, k_ref, v_ref, vt_ref, max_ref, acc_ref, scale):
    block_rows = store_ref.shape[2]
    count = list_ref[list_ref.shape[0] - 1]

    def step(tile, carry):
        for j in range(TILE):
            index = tile * TILE + j
            slot = list_ref[jnp.minimum(index, count - 1)]
            k_ref[j * block_rows : (j + 1) * block_rows, :] = store_ref[0, slot]
            block = store_ref[1, slot]
            v_ref[j * block_rows : (j + 1) * block_rows, :] = jnp.where(
                index < count, block, jnp.zeros_like(block)
            )
        put_values(v_ref[...], (count - tile * TILE) * block_rows, vt_ref)
        absorb_tile(k_ref[...], vt_ref, q_ref, max_ref, acc_ref, scale)
        return carry

    lax.fori_loop(0, (count + TILE - 1) // TILE, step, 0)


def reset(max_ref, acc_ref):
    max_ref[...] = jnp.full_like(max_ref, LOW)
    acc_ref[...] = jnp.zeros_like(acc_ref)


def finish(out_ref, max_ref, acc_ref, scale):
    heads, _, rows = max_ref.shape
    head_dim = acc_ref.shape[1] - 16
    logs = []
    for g in range(heads):
        total = acc_ref[g, head_dim : head_dim + 8, :][:1]
        some = total > 0.0
        inverse = jnp.where(some, 1.0 / jnp.where(some, total, 1.0), 0.0)
        out_ref[g * head_dim : (g + 1) * head_dim, :] = (
            acc_ref[g, :head_dim, :] * inverse
        ).astype(jnp.bfloat16)
        logs.append(
            jnp.where(some, max_ref[g] * scale + jnp.log2(jnp.where(some, total, 1.0)), LOW)
        )
    logs = jnp.concatenate(logs, axis=0)
    first = logs.astype(jnp.bfloat16).astype(jnp.float32)
    rest = logs - first
    second = rest.astype(jnp.bfloat16).astype(jnp.float32)
    third = rest - second
    pieces = jnp.concatenate([first, second, third, jnp.zeros_like(first)], axis=0)
    out_ref[heads * head_dim :, :] = pieces.astype(jnp.bfloat16)


def own_kernel(
    scale, span_live_ref, list_ref, q_ref, store_ref, span_ref, out_ref,
    k_ref, v_ref, vt_ref, max_ref, acc_ref,
):
    reset(max_ref, acc_ref)
    rows = q_ref.shape[0]
    keys = span_ref.shape[1]
    key = lax.broadcasted_iota(jnp.int32, (keys, rows), 0)
    row = lax.broadcasted_iota(jnp.int32, (keys, rows), 1)
    put_values(span_ref[1], keys, vt_ref)
    absorb_tile(
        span_ref[0], vt_ref, q_ref, max_ref, acc_ref, scale,
        (key <= row) & (key < span_live_ref[0]),
    )
    absorb_blocks(list_ref, q_ref, store_ref, k_ref, v_ref, vt_ref, max_ref, acc_ref, scale)
    finish(out_ref, max_ref, acc_ref, scale)


def guest_kernel(
    scale, list_a_ref, list_b_ref, q_a_ref, q_b_ref, store_ref, out_a_ref, out_b_ref,
    k_ref, v_ref, vt_ref, max_ref, acc_ref,
):
    for list_ref, q_ref, out_ref in (
        (list_a_ref, q_a_ref, out_a_ref),
        (list_b_ref, q_b_ref, out_b_ref),
    ):
        reset(max_ref, acc_ref)
        absorb_blocks(list_ref, q_ref, store_ref, k_ref, v_ref, vt_ref, max_ref, acc_ref, scale)
        finish(out_ref, max_ref, acc_ref, scale)


def attention_scratch(heads, rows, head_dim, block_rows):
    keys = TILE * block_rows
    return [
        pltpu.VMEM((keys, head_dim), jnp.bfloat16),
        pltpu.VMEM((keys, head_dim), jnp.bfloat16),
        pltpu.VMEM((head_dim + 16, keys), jnp.bfloat16),
        pltpu.VMEM((heads, 1, rows), jnp.float32),
        pltpu.VMEM((heads, head_dim + 16, rows), jnp.float32),
    ]


def attention_cost(rows, keys, head_dim, heads):
    return pl.CostEstimate(
        flops=4 * rows * keys * head_dim * heads,
        bytes_accessed=4 * 1024 * 1024,
        transcendentals=rows * keys * heads,
    )


def project_kernel(
    peers, me_ref, span_live_ref, *refs
):
    parts = refs[: 2 * peers - 1]
    weight_ref, out_ref, att_ref = refs[2 * peers - 1 :]
    rows, features = att_ref.shape

    @pl.when(pl.program_id(0) == 0)
    def _():
        heads = 8 * ((parts[0].shape[0] - features) // 32)
        head_dim = features // heads
        me = me_ref[0]
        logs = []
        for index, part in enumerate(parts):
            pieces = part[features:, :].astype(jnp.float32)
            log = pieces[:heads] + pieces[heads : 2 * heads] + pieces[2 * heads : 3 * heads]
            if index:
                away = (index + 1) // 2
                valid = me >= away if index % 2 else me + away < peers
                log = jnp.where(valid, log, LOW)
            logs.append(log)
        top = functools.reduce(jnp.maximum, logs)
        weights = [jnp.exp2(log - top) for log in logs]
        inverse = 1.0 / functools.reduce(jnp.add, weights)
        row = lax.broadcasted_iota(jnp.int32, (heads, rows), 1)
        inverse = jnp.where(row < span_live_ref[0], inverse, 0.0)
        weights = [weight * inverse for weight in weights]
        for g in range(heads):
            total = jnp.zeros((head_dim, rows), jnp.float32)
            for part, weight in zip(parts, weights):
                total += part[g * head_dim : (g + 1) * head_dim, :].astype(jnp.float32) * weight[
                    g : g + 1
                ]
            att_ref[:, g * head_dim : (g + 1) * head_dim] = total.T.astype(jnp.bfloat16)

    out_ref[...] = jnp.dot(
        att_ref[...], weight_ref[...], preferred_element_type=jnp.float32
    ).astype(jnp.bfloat16)


def project(me, span_live, parts, out_weight, peers):
    features, outputs = out_weight.shape
    rows = parts[0].shape[1]
    width = 512
    whole = lambda i, *_: (0, 0)
    return pl.pallas_call(
        functools.partial(project_kernel, peers),
        out_shape=jax.ShapeDtypeStruct((rows, outputs), jnp.bfloat16),
        grid_spec=pltpu.PrefetchScalarGridSpec(
            num_scalar_prefetch=2,
            grid=(outputs // width,),
            in_specs=[pl.BlockSpec(part.shape, whole) for part in parts]
            + [pl.BlockSpec((features, width), lambda i, *_: (0, i))],
            out_specs=pl.BlockSpec((rows, width), lambda i, *_: (0, i)),
            scratch_shapes=[pltpu.VMEM((rows, features), jnp.bfloat16)],
        ),
        compiler_params=pltpu.CompilerParams(vmem_limit_bytes=VMEM_LIMIT),
        cost_estimate=pl.CostEstimate(
            flops=2 * rows * features * outputs,
            bytes_accessed=2 * (features + rows) * outputs,
            transcendentals=0,
        ),
        name="project",
    )(me, span_live, *parts, out_weight)


def pack_kernel(span_live_ref, owners_ref, span_ref, out_ref, counts_ref):
    peers = out_ref.shape[1]
    block_rows, head_dim = out_ref.shape[3:]
    out_ref[...] = jnp.zeros_like(out_ref)
    for k in range(peers):
        counts_ref[k] = 0
    row = lax.broadcasted_iota(jnp.int32, (block_rows, head_dim), 0)
    for b in range(span_ref.shape[1] // block_rows):
        owner = owners_ref[b]
        rank = counts_ref[owner]
        counts_ref[owner] = rank + 1
        keep = row + b * block_rows < span_live_ref[0]
        for side in range(2):
            block = span_ref[side, b * block_rows : (b + 1) * block_rows, :]
            out_ref[side, owner, rank] = jnp.where(keep, block, jnp.zeros_like(block))


def shards(
    queries,
    cache_store,
    span_cache,
    out_weight,
    prefix_blocks,
    span_lengths,
    hit_holders,
    hit_slots,
    store_owners,
):
    peers = lax.axis_size("inst")
    block_rows, head_dim = cache_store.shape[2:]
    rows = queries.shape[0]
    heads = queries.shape[1] // head_dim
    block_max = hit_slots.shape[1]
    cap = max(2, block_max * 5 // (4 * peers))
    new_count = rows // block_rows
    push_cap = max(2, 2 * new_count // peers)
    scale = math.log2(math.e) / math.sqrt(head_dim)
    me = lax.axis_index("inst").reshape(1)
    part_shape = jax.ShapeDtypeStruct((heads * head_dim + 4 * heads, rows), jnp.bfloat16)

    def shift(value, by):
        pairs = [(i, i + by) for i in range(peers) if 0 <= i + by < peers]
        return lax.ppermute(value, "inst", pairs)

    lists = route(me, prefix_blocks, hit_holders.reshape(-1), hit_slots.reshape(-1), peers, cap)

    from_left, from_right = [queries], [queries]
    for away in range(1, peers):
        from_left.append(shift(from_left[-1], 1))
        from_right.append(shift(from_right[-1], -1))

    own = pl.pallas_call(
        functools.partial(own_kernel, scale),
        out_shape=part_shape,
        in_specs=[SMEM, SMEM, VMEM, VMEM, VMEM],
        out_specs=VMEM,
        scratch_shapes=attention_scratch(heads, rows, head_dim, block_rows),
        compiler_params=pltpu.CompilerParams(vmem_limit_bytes=VMEM_LIMIT),
        cost_estimate=attention_cost(rows, 4 * rows, head_dim, heads),
        name="own_attention",
    )(span_lengths, lists[0], queries, cache_store, span_cache)

    parts = [own]
    for away in range(1, peers):
        list_a = shift(lists[away], away)
        list_b = shift(lists[peers - away], -away)
        part_a, part_b = pl.pallas_call(
            functools.partial(guest_kernel, scale),
            out_shape=(part_shape, part_shape),
            in_specs=[SMEM, SMEM, VMEM, VMEM, VMEM],
            out_specs=(VMEM, VMEM),
            scratch_shapes=attention_scratch(heads, rows, head_dim, block_rows),
            compiler_params=pltpu.CompilerParams(vmem_limit_bytes=VMEM_LIMIT),
            cost_estimate=attention_cost(rows, 6 * rows, head_dim, heads),
            name="guest_attention",
        )(list_a, list_b, from_left[away], from_right[away], cache_store)
        parts.append(shift(part_b, away))
        parts.append(shift(part_a, -away))

    partial = project(me, span_lengths, parts, out_weight, peers)
    projected = lax.psum_scatter(partial, "tp", scatter_dimension=0, tiled=True)

    outgoing = pl.pallas_call(
        pack_kernel,
        out_shape=jax.ShapeDtypeStruct(
            (2, peers, push_cap, block_rows, head_dim), jnp.bfloat16
        ),
        in_specs=[SMEM, SMEM, VMEM],
        out_specs=VMEM,
        scratch_shapes=[pltpu.SMEM((peers,), jnp.int32)],
        compiler_params=pltpu.CompilerParams(vmem_limit_bytes=VMEM_LIMIT),
        name="pack_blocks",
    )(span_lengths, store_owners.reshape(-1), span_cache)
    incoming = lax.all_to_all(outgoing, "inst", split_axis=1, concat_axis=1, tiled=True)
    pushed_blocks = incoming.reshape(2, peers * push_cap, block_rows, head_dim)
    return (projected, pushed_blocks)


def solution(mesh):
    return jax.shard_map(
        shards,
        mesh=mesh,
        in_specs=(
            P(("pods", "inst"), "tp"),
            P(None, ("pods", "inst"), None, "tp"),
            P(None, ("pods", "inst"), "tp"),
            P("tp", None),
            P(("pods", "inst")),
            P(("pods", "inst")),
            P(("pods", "inst"), None, None),
            P(("pods", "inst"), None),
            P(("pods", "inst"), None, None),
        ),
        out_specs=(P(("pods", "inst", "tp"), None), P(None, ("pods", "inst"), None, "tp")),
        check_vma=False,
    )
```

```python
import functools
import math

import jax
import jax.numpy as jnp
from jax import lax
from jax.experimental import pallas as pl
from jax.experimental.pallas import tpu as pltpu
from jax.sharding import PartitionSpec as P

LOW = -1e30
TILE = 16
VMEM_LIMIT = 48 * 1024 * 1024

SMEM = pl.BlockSpec(memory_space=pltpu.SMEM)
VMEM = pl.BlockSpec(memory_space=pltpu.VMEM)


def round_up(number, step):
    return -(-number // step) * step


def route_kernel(live_ref, holders_ref, slots_ref, lists_ref):
    peers, width = lists_ref.shape
    number = holders_ref.shape[1]
    padded = round_up(peers, 16)
    holder = lax.broadcasted_iota(jnp.int32, (padded, number), 0)
    entry = lax.broadcasted_iota(jnp.int32, (padded, number), 1)
    hot = (holders_ref[...] == holder) & (entry < live_ref[0])
    ones = jnp.where(hot, 1.0, 0.0)
    earlier = lax.broadcasted_iota(jnp.int32, (number, number), 0) < lax.broadcasted_iota(
        jnp.int32, (number, number), 1
    )
    ranks = jnp.dot(
        ones.astype(jnp.bfloat16),
        jnp.where(earlier, 1.0, 0.0).astype(jnp.bfloat16),
        preferred_element_type=jnp.float32,
    )
    rank = jnp.sum(ranks * ones, axis=0, keepdims=True)
    rank = jnp.broadcast_to(rank, (8, number)).T[:, :1].astype(jnp.int32)
    place = lax.broadcasted_iota(jnp.int32, (number, width), 1) == rank
    slots = jnp.where(hot, slots_ref[...], 0).astype(jnp.float32)
    lists = jnp.dot(
        slots.astype(jnp.bfloat16),
        jnp.where(place, 1.0, 0.0).astype(jnp.bfloat16),
        preferred_element_type=jnp.float32,
    )
    counts = jnp.sum(ones, axis=1, keepdims=True)
    last = lax.broadcasted_iota(jnp.int32, (padded, width), 1) == width - 1
    lists_ref[...] = jnp.where(last, counts, lists)[:peers].astype(jnp.int32)


def route(live, holders, slots, peers, cap):
    width = round_up(cap + 1, 128)
    return pl.pallas_call(
        route_kernel,
        out_shape=jax.ShapeDtypeStruct((peers, width), jnp.int32),
        in_specs=[SMEM, VMEM, VMEM],
        out_specs=VMEM,
        name="route",
    )(live, holders, slots)


def score(keys, qt_ref, g):
    return jnp.dot(keys, qt_ref[g], preferred_element_type=jnp.float32)


def absorb_tile(keys, values, qt_ref, max_ref, acc_ref, scale, s, tail=None, middle=None, mask=None):
    heads = max_ref.shape[0]
    for g in range(heads):
        if g + 1 < heads:
            following = score(keys, qt_ref, g + 1)
        elif tail is not None:
            tail()
        if mask is not None:
            s = jnp.where(mask, s, LOW)
        old = max_ref[g]
        new = jnp.maximum(old, jnp.max(s, axis=0, keepdims=True))
        p = jnp.exp2((s - new) * scale).astype(jnp.bfloat16)
        update = jnp.dot(values, p, preferred_element_type=jnp.float32)
        acc_ref[g] = acc_ref[g] * jnp.exp2((old - new) * scale) + update
        max_ref[g] = new
        if middle is not None and g == heads // 2:
            middle()
        s = following


def transposed_values(values, valid_keys):
    keys = values.shape[0]
    row = lax.broadcasted_iota(jnp.int32, (16, keys), 0)
    col = lax.broadcasted_iota(jnp.int32, (16, keys), 1)
    marks = jnp.where((row == 0) & (col < valid_keys), 1.0, 0.0).astype(jnp.bfloat16)
    return jnp.concatenate([values.T, marks], axis=0)


def absorb_blocks(slot, count, store_ref, qt_ref, k_ref, v_ref, vt_ref, s_ref, max_ref, acc_ref, scale):
    block_rows = store_ref.shape[2]

    def fetch(tile, into):
        for j in range(TILE):
            index = tile * TILE + j
            here = slot(jnp.maximum(jnp.minimum(index, count - 1), 0))
            k_ref[into, j * block_rows : (j + 1) * block_rows, :] = store_ref[0, here]
            block = store_ref[1, here]
            v_ref[j * block_rows : (j + 1) * block_rows, :] = jnp.where(
                index < count, block, jnp.zeros_like(block)
            )
        vt_ref[into] = transposed_values(v_ref[...], (count - tile * TILE) * block_rows)

    @pl.when(count > 0)
    def _():
        fetch(0, 0)
        s_ref[...] = score(k_ref[0], qt_ref, 0)

        def step(tile, carry):
            now = lax.rem(tile, 2)
            later = 1 - now

            def tail():
                s_ref[...] = score(k_ref[later], qt_ref, 0)

            absorb_tile(
                k_ref[now], vt_ref[now], qt_ref, max_ref, acc_ref, scale, s_ref[...],
                tail=tail, middle=lambda: fetch(tile + 1, later),
            )
            return carry

        lax.fori_loop(0, (count + TILE - 1) // TILE, step, 0)


def begin(q_ref, qt_ref, max_ref, acc_ref):
    heads = max_ref.shape[0]
    head_dim = qt_ref.shape[1]
    max_ref[...] = jnp.full_like(max_ref, LOW)
    acc_ref[...] = jnp.zeros_like(acc_ref)
    for g in range(heads):
        qt_ref[g] = q_ref[:, g * head_dim : (g + 1) * head_dim].T


def finish(out_ref, max_ref, acc_ref, scale):
    heads = max_ref.shape[0]
    head_dim = acc_ref.shape[1] - 16
    logs = []
    for g in range(heads):
        total = acc_ref[g, head_dim : head_dim + 8, :][:1]
        some = total > 0.0
        inverse = jnp.where(some, 1.0 / jnp.where(some, total, 1.0), 0.0)
        out_ref[g * head_dim : (g + 1) * head_dim, :] = (
            acc_ref[g, :head_dim, :] * inverse
        ).astype(jnp.bfloat16)
        logs.append(
            jnp.where(some, max_ref[g] * scale + jnp.log2(jnp.where(some, total, 1.0)), LOW)
        )
    logs = jnp.concatenate(logs, axis=0)
    first = logs.astype(jnp.bfloat16).astype(jnp.float32)
    rest = logs - first
    second = rest.astype(jnp.bfloat16).astype(jnp.float32)
    third = rest - second
    pieces = jnp.concatenate([first, second, third, jnp.zeros_like(first)], axis=0)
    out_ref[heads * head_dim :, :] = pieces.astype(jnp.bfloat16)


def own_kernel(
    scale, me_ref, span_live_ref, list_ref, q_ref, store_ref, span_ref, out_ref,
    qt_ref, k_ref, v_ref, vt_ref, s_ref, max_ref, acc_ref,
):
    me = me_ref[0]
    begin(q_ref, qt_ref, max_ref, acc_ref)
    rows = q_ref.shape[0]
    keys = span_ref.shape[1]
    key = lax.broadcasted_iota(jnp.int32, (keys, rows), 0)
    row = lax.broadcasted_iota(jnp.int32, (keys, rows), 1)
    absorb_tile(
        span_ref[0], transposed_values(span_ref[1], keys), qt_ref, max_ref, acc_ref, scale,
        score(span_ref[0], qt_ref, 0), mask=(key <= row) & (key < span_live_ref[0]),
    )
    absorb_blocks(
        lambda index: list_ref[me, index], list_ref[me, list_ref.shape[1] - 1],
        store_ref, qt_ref, k_ref, v_ref, vt_ref, s_ref, max_ref, acc_ref, scale,
    )
    finish(out_ref.at[0], max_ref, acc_ref, scale)


def guest_kernel(
    scale, me_ref, lists_ref, q_ref, store_ref, kept_ref, out_ref,
    qt_ref, k_ref, v_ref, vt_ref, s_ref, max_ref, acc_ref,
):
    me = me_ref[0]
    peers = lists_ref.shape[0]
    guest = lax.rem(me + 1 + pl.program_id(0), peers)
    begin(q_ref.at[0], qt_ref, max_ref, acc_ref)
    absorb_blocks(
        lambda index: lists_ref[guest, me, index], lists_ref[guest, me, lists_ref.shape[2] - 1],
        store_ref, qt_ref, k_ref, v_ref, vt_ref, s_ref, max_ref, acc_ref, scale,
    )
    finish(out_ref.at[0], max_ref, acc_ref, scale)


def attention_scratch(heads, rows, head_dim, block_rows):
    keys = TILE * block_rows
    return [
        pltpu.VMEM((heads, head_dim, rows), jnp.bfloat16),
        pltpu.VMEM((2, keys, head_dim), jnp.bfloat16),
        pltpu.VMEM((keys, head_dim), jnp.bfloat16),
        pltpu.VMEM((2, head_dim + 16, keys), jnp.bfloat16),
        pltpu.VMEM((keys, rows), jnp.float32),
        pltpu.VMEM((heads, 1, rows), jnp.float32),
        pltpu.VMEM((heads, head_dim + 16, rows), jnp.float32),
    ]


def attention_cost(rows, keys, head_dim, heads):
    return pl.CostEstimate(
        flops=4 * rows * keys * head_dim * heads,
        bytes_accessed=4 * 1024 * 1024,
        transcendentals=rows * keys * heads,
    )


def project_kernel(span_live_ref, parts_ref, weight_ref, out_ref, att_ref):
    rows, features = att_ref.shape
    peers = parts_ref.shape[0]

    @pl.when(pl.program_id(0) == 0)
    def _():
        heads = (parts_ref.shape[1] - features) // 4
        head_dim = features // heads
        logs = []
        for h in range(peers):
            pieces = parts_ref[h, features:, :].astype(jnp.float32)
            logs.append(pieces[:heads] + pieces[heads : 2 * heads] + pieces[2 * heads : 3 * heads])
        top = functools.reduce(jnp.maximum, logs)
        weights = [jnp.exp2(log - top) for log in logs]
        inverse = 1.0 / functools.reduce(jnp.add, weights)
        row = lax.broadcasted_iota(jnp.int32, (heads, rows), 1)
        inverse = jnp.where(row < span_live_ref[0], inverse, 0.0)
        weights = [weight * inverse for weight in weights]
        for g in range(heads):
            total = jnp.zeros((head_dim, rows), jnp.float32)
            for h in range(peers):
                part = parts_ref[h, g * head_dim : (g + 1) * head_dim, :]
                total += part.astype(jnp.float32) * weights[h][g : g + 1]
            att_ref[:, g * head_dim : (g + 1) * head_dim] = total.T.astype(jnp.bfloat16)

    out_ref[...] = jnp.dot(
        att_ref[...], weight_ref[...], preferred_element_type=jnp.float32
    ).astype(jnp.bfloat16)


def project(span_live, parts, out_weight):
    features, outputs = out_weight.shape
    rows = parts.shape[2]
    width = 512
    return pl.pallas_call(
        project_kernel,
        out_shape=jax.ShapeDtypeStruct((rows, outputs), jnp.bfloat16),
        grid_spec=pltpu.PrefetchScalarGridSpec(
            num_scalar_prefetch=1,
            grid=(outputs // width,),
            in_specs=[
                pl.BlockSpec(parts.shape, lambda i, *_: (0, 0, 0)),
                pl.BlockSpec((features, width), lambda i, *_: (0, i)),
            ],
            out_specs=pl.BlockSpec((rows, width), lambda i, *_: (0, i)),
            scratch_shapes=[pltpu.VMEM((rows, features), jnp.bfloat16)],
        ),
        compiler_params=pltpu.CompilerParams(vmem_limit_bytes=VMEM_LIMIT),
        cost_estimate=pl.CostEstimate(
            flops=2 * rows * features * outputs,
            bytes_accessed=2 * (features + rows) * outputs,
            transcendentals=0,
        ),
        name="project",
    )(span_live, parts, out_weight)


def pack_kernel(span_live_ref, owners_ref, span_ref, out_ref, counts_ref):
    peers = out_ref.shape[1]
    block_rows, head_dim = out_ref.shape[3:]
    out_ref[...] = jnp.zeros_like(out_ref)
    for k in range(peers):
        counts_ref[k] = 0
    row = lax.broadcasted_iota(jnp.int32, (block_rows, head_dim), 0)
    for b in range(span_ref.shape[1] // block_rows):
        owner = owners_ref[b]
        rank = counts_ref[owner]
        counts_ref[owner] = rank + 1
        keep = row + b * block_rows < span_live_ref[0]
        for side in range(2):
            block = span_ref[side, b * block_rows : (b + 1) * block_rows, :]
            out_ref[side, owner, rank] = jnp.where(keep, block, jnp.zeros_like(block))


def shards(
    queries,
    cache_store,
    span_cache,
    out_weight,
    prefix_blocks,
    span_lengths,
    hit_holders,
    hit_slots,
    store_owners,
):
    peers = lax.axis_size("inst")
    block_rows, head_dim = cache_store.shape[2:]
    rows, columns = queries.shape
    heads = columns // head_dim
    block_max = hit_slots.shape[1]
    cap = max(2, block_max * 5 // (4 * peers))
    new_count = rows // block_rows
    push_cap = max(2, 2 * new_count // peers)
    scale = math.log2(math.e) / math.sqrt(head_dim)
    me = lax.axis_index("inst").reshape(1)
    part_rows = heads * head_dim + 4 * heads
    parts_shape = jax.ShapeDtypeStruct((peers, part_rows, rows), jnp.bfloat16)

    all_queries = lax.all_gather(queries, "inst")
    lists = route(prefix_blocks, hit_holders.reshape(1, -1), hit_slots, peers, cap)
    all_lists = lax.all_gather(lists, "inst")

    whole_store = pl.BlockSpec(cache_store.shape, lambda i, *_: (0, 0, 0, 0))
    own = pl.pallas_call(
        functools.partial(own_kernel, scale),
        out_shape=parts_shape,
        grid_spec=pltpu.PrefetchScalarGridSpec(
            num_scalar_prefetch=3,
            grid=(1,),
            in_specs=[
                pl.BlockSpec((rows, columns), lambda i, *_: (0, 0)),
                whole_store,
                pl.BlockSpec(span_cache.shape, lambda i, *_: (0, 0, 0)),
            ],
            out_specs=pl.BlockSpec((1, part_rows, rows), lambda i, at, *_: (at[0], 0, 0)),
            scratch_shapes=attention_scratch(heads, rows, head_dim, block_rows),
        ),
        compiler_params=pltpu.CompilerParams(vmem_limit_bytes=VMEM_LIMIT),
        cost_estimate=attention_cost(rows, 8 * rows, head_dim, heads),
        name="own_attention",
    )(me, span_lengths, lists, queries, cache_store, span_cache)

    parts = pl.pallas_call(
        functools.partial(guest_kernel, scale),
        out_shape=parts_shape,
        grid_spec=pltpu.PrefetchScalarGridSpec(
            num_scalar_prefetch=2,
            grid=(peers - 1,),
            in_specs=[
                pl.BlockSpec(
                    (1, rows, columns), lambda i, at, *_: (lax.rem(at[0] + 1 + i, peers), 0, 0)
                ),
                whole_store,
                pl.BlockSpec(memory_space=pl.ANY),
            ],
            out_specs=pl.BlockSpec(
                (1, part_rows, rows), lambda i, at, *_: (lax.rem(at[0] + 1 + i, peers), 0, 0)
            ),
            scratch_shapes=attention_scratch(heads, rows, head_dim, block_rows),
        ),
        input_output_aliases={4: 0},
        compiler_params=pltpu.CompilerParams(vmem_limit_bytes=VMEM_LIMIT),
        cost_estimate=attention_cost(rows, 16 * rows, head_dim, heads),
        name="guest_attention",
    )(me, all_lists, all_queries, cache_store, own)

    parts = lax.all_to_all(parts, "inst", split_axis=0, concat_axis=0, tiled=True)
    partial = project(span_lengths, parts, out_weight)
    projected = lax.psum_scatter(partial, "tp", scatter_dimension=0, tiled=True)

    outgoing = pl.pallas_call(
        pack_kernel,
        out_shape=jax.ShapeDtypeStruct(
            (2, peers, push_cap, block_rows, head_dim), jnp.bfloat16
        ),
        in_specs=[SMEM, SMEM, VMEM],
        out_specs=VMEM,
        scratch_shapes=[pltpu.SMEM((peers,), jnp.int32)],
        compiler_params=pltpu.CompilerParams(vmem_limit_bytes=VMEM_LIMIT),
        name="pack_blocks",
    )(span_lengths, store_owners.reshape(-1), span_cache)
    incoming = lax.all_to_all(outgoing, "inst", split_axis=1, concat_axis=1, tiled=True)
    pushed_blocks = incoming.reshape(2, peers * push_cap, block_rows, head_dim)
    return (projected, pushed_blocks)


def solution(mesh):
    return jax.shard_map(
        shards,
        mesh=mesh,
        in_specs=(
            P(("pods", "inst"), "tp"),
            P(None, ("pods", "inst"), None, "tp"),
            P(None, ("pods", "inst"), "tp"),
            P("tp", None),
            P(("pods", "inst")),
            P(("pods", "inst")),
            P(("pods", "inst"), None, None),
            P(("pods", "inst"), None),
            P(("pods", "inst"), None, None),
        ),
        out_specs=(P(("pods", "inst", "tp"), None), P(None, ("pods", "inst"), None, "tp")),
        check_vma=False,
    )
```

```python
import functools
import math

import jax
import jax.numpy as jnp
from jax import lax
from jax.experimental import pallas as pl
from jax.experimental.pallas import tpu as pltpu
from jax.sharding import PartitionSpec as P

LOW = -1e30
TOP = 2.0**100
TILE = 16
VMEM_LIMIT = 60 * 1024 * 1024

SMEM = pl.BlockSpec(memory_space=pltpu.SMEM)
VMEM = pl.BlockSpec(memory_space=pltpu.VMEM)


def round_up(number, step):
    return -(-number // step) * step


def route_kernel(live_ref, holders_ref, slots_ref, q_ref, lists_ref, out_ref):
    peers, width = lists_ref.shape
    number = holders_ref.shape[1]
    padded = round_up(peers, 16)
    holder = lax.broadcasted_iota(jnp.int32, (padded, number), 0)
    entry = lax.broadcasted_iota(jnp.int32, (padded, number), 1)
    hot = (holders_ref[...] == holder) & (entry < live_ref[0])
    ones = jnp.where(hot, 1.0, 0.0)
    earlier = lax.broadcasted_iota(jnp.int32, (number, number), 0) < lax.broadcasted_iota(
        jnp.int32, (number, number), 1
    )
    ranks = jnp.dot(
        ones.astype(jnp.bfloat16),
        jnp.where(earlier, 1.0, 0.0).astype(jnp.bfloat16),
        preferred_element_type=jnp.float32,
    )
    rank = jnp.sum(ranks * ones, axis=0, keepdims=True)
    rank = jnp.broadcast_to(rank, (8, number)).T[:, :1].astype(jnp.int32)
    place = lax.broadcasted_iota(jnp.int32, (number, width), 1) == rank
    slots = jnp.where(hot, slots_ref[...], 0).astype(jnp.float32)
    lists = jnp.dot(
        slots.astype(jnp.bfloat16),
        jnp.where(place, 1.0, 0.0).astype(jnp.bfloat16),
        preferred_element_type=jnp.float32,
    )
    counts = jnp.sum(ones, axis=1, keepdims=True)
    last = lax.broadcasted_iota(jnp.int32, (padded, width), 1) == width - 1
    lists = jnp.where(last, counts, lists)[:peers]
    lists_ref[...] = lists.astype(jnp.int32)

    rows, columns = q_ref.shape
    out_ref[:rows, :] = q_ref[...]
    each = columns // width
    riders = out_ref.shape[0] - rows
    row = lax.broadcasted_iota(jnp.int32, (riders, columns), 0)
    tail = jnp.zeros((riders, columns), jnp.float32)
    for r in range(-(-peers // each)):
        line = [lists[h : h + 1] for h in range(r * each, min(peers, (r + 1) * each))]
        line += [jnp.zeros((1, width), jnp.float32)] * (each - len(line))
        tail = jnp.where(row == r, jnp.concatenate(line, axis=1), tail)
    out_ref[rows:, :] = tail.astype(jnp.bfloat16)


def route(live, holders, slots, queries, peers, width):
    rows, columns = queries.shape
    riders = round_up(-(-peers // (columns // width)), 16)
    return pl.pallas_call(
        route_kernel,
        out_shape=(
            jax.ShapeDtypeStruct((peers, width), jnp.int32),
            jax.ShapeDtypeStruct((rows + riders, columns), jnp.bfloat16),
        ),
        in_specs=[SMEM, VMEM, VMEM, VMEM],
        out_specs=(VMEM, VMEM),
        compiler_params=pltpu.CompilerParams(vmem_limit_bytes=VMEM_LIMIT),
        name="route",
    )(live, holders, slots, queries)


def score(keys, qt_ref, g):
    return jnp.dot(keys, qt_ref[g], preferred_element_type=jnp.float32)


def absorb_tile(keys, values, qt_ref, max_ref, acc_ref, scale, mask=None):
    for g in range(max_ref.shape[0]):
        s = score(keys, qt_ref, g)
        if mask is not None:
            s = jnp.where(mask, s, LOW)
        old = max_ref[g]
        new = jnp.maximum(old, jnp.max(s, axis=0, keepdims=True))
        p = jnp.exp2((s - new) * scale).astype(jnp.bfloat16)
        update = jnp.dot(values, p, preferred_element_type=jnp.float32)
        acc_ref[g] = acc_ref[g] * jnp.exp2((old - new) * scale) + update
        max_ref[g] = new


def add_tile(keys, values, qt_ref, max_ref, acc_ref, scale, s, middle, tail):
    heads = max_ref.shape[0]
    for g in range(heads):
        if g + 1 < heads:
            following = score(keys, qt_ref, g + 1)
        else:
            tail()
        p = jnp.exp2((s - max_ref[g]) * scale).astype(jnp.bfloat16)
        acc_ref[g] += jnp.dot(values, p, preferred_element_type=jnp.float32)
        if g == heads // 2:
            middle()
        s = following


def transposed_values(values, valid_keys):
    keys = values.shape[0]
    row = lax.broadcasted_iota(jnp.int32, (16, keys), 0)
    col = lax.broadcasted_iota(jnp.int32, (16, keys), 1)
    marks = jnp.where((row == 0) & (col < valid_keys), 1.0, 0.0).astype(jnp.bfloat16)
    return jnp.concatenate([values.T, marks], axis=0)


def attend(
    slot, count, store_ref, span_ref, span_live, qt_ref, k_ref, v_ref, vt_ref, s_ref, max_ref,
    acc_ref, scale,
):
    block_rows = store_ref.shape[2]
    heads, head_dim, rows = qt_ref.shape
    tiles = (count + TILE - 1) // TILE

    def fetch(tile, into):
        for j in range(TILE):
            index = tile * TILE + j
            here = slot(jnp.maximum(jnp.minimum(index, count - 1), 0))
            k_ref[into, j * block_rows : (j + 1) * block_rows, :] = store_ref[0, here]
            block = store_ref[1, here]
            v_ref[j * block_rows : (j + 1) * block_rows, :] = jnp.where(
                index < count, block, jnp.zeros_like(block)
            )
        vt_ref[into] = transposed_values(v_ref[...], (count - tile * TILE) * block_rows)

    def start():
        acc_ref[...] = jnp.zeros_like(acc_ref)
        if span_ref is not None:
            max_ref[...] = jnp.full_like(max_ref, LOW)
            keys = span_ref.shape[1]
            key = lax.broadcasted_iota(jnp.int32, (keys, rows), 0)
            row = lax.broadcasted_iota(jnp.int32, (keys, rows), 1)
            absorb_tile(
                span_ref[0], transposed_values(span_ref[1], keys), qt_ref, max_ref, acc_ref,
                scale, (key <= row) & (key < span_live),
            )

    start()

    @pl.when(count > 0)
    def _():
        fetch(0, 0)
        if span_ref is None:
            for g in range(heads):
                few = score(k_ref[0, : 4 * block_rows, :], qt_ref, g)
                max_ref[g] = jnp.max(few, axis=0, keepdims=True)
        s_ref[...] = score(k_ref[0], qt_ref, 0)

        def step(tile, carry):
            now = lax.rem(tile, 2)
            later = 1 - now

            def tail():
                s_ref[...] = score(k_ref[later], qt_ref, 0)

            add_tile(
                k_ref[now], vt_ref[now], qt_ref, max_ref, acc_ref, scale, s_ref[...],
                lambda: fetch(tile + 1, later), tail,
            )
            return carry

        lax.fori_loop(0, tiles, step, 0)
        totals = jnp.concatenate(
            [acc_ref[g, head_dim : head_dim + 8, :][:1] for g in range(heads)], axis=0
        )
        beyond = jnp.max(jnp.where(totals < TOP, 0, 1))

        @pl.when(beyond > 0)
        def _():
            start()
            if span_ref is None:
                max_ref[...] = jnp.full_like(max_ref, LOW)

            def careful(tile, carry):
                fetch(tile, 0)
                absorb_tile(k_ref[0], vt_ref[0], qt_ref, max_ref, acc_ref, scale)
                return carry

            lax.fori_loop(0, tiles, careful, 0)


def turn(q_ref, qt_ref):
    heads, head_dim, rows = qt_ref.shape
    for g in range(heads):
        qt_ref[g] = q_ref[:rows, g * head_dim : (g + 1) * head_dim].T


def write_logs(out_ref, logs):
    first = logs.astype(jnp.bfloat16).astype(jnp.float32)
    rest = logs - first
    second = rest.astype(jnp.bfloat16).astype(jnp.float32)
    third = rest - second
    pieces = jnp.concatenate([first, second, third, jnp.zeros_like(first)], axis=0)
    out_ref[out_ref.shape[0] - pieces.shape[0] :, :] = pieces.astype(jnp.bfloat16)


def finish(out_ref, max_ref, acc_ref, scale):
    heads = max_ref.shape[0]
    head_dim = acc_ref.shape[1] - 16
    logs = []
    for g in range(heads):
        total = acc_ref[g, head_dim : head_dim + 8, :][:1]
        out_ref[g * head_dim : (g + 1) * head_dim, :] = (
            acc_ref[g, :head_dim, :] * (1.0 / total)
        ).astype(jnp.bfloat16)
        logs.append(max_ref[g] * scale + jnp.log2(total))
    write_logs(out_ref, jnp.concatenate(logs, axis=0))


def own_kernel(
    scale, me_ref, span_live_ref, lists_ref, q_ref, store_ref, span_ref, out_ref,
    qt_ref, k_ref, v_ref, vt_ref, s_ref, max_ref, acc_ref,
):
    me = me_ref[0]
    turn(q_ref, qt_ref)
    attend(
        lambda index: lists_ref[me, index], lists_ref[me, lists_ref.shape[1] - 1], store_ref,
        span_ref, span_live_ref[0], qt_ref, k_ref, v_ref, vt_ref, s_ref, max_ref, acc_ref, scale,
    )
    finish(out_ref, max_ref, acc_ref, scale)


def guest_kernel(
    scale, width, me_ref, q_a_ref, q_b_ref, store_ref, after_ref, out_a_ref, out_b_ref,
    wide_ref, list_ref, qt_ref, k_ref, v_ref, vt_ref, s_ref, max_ref, acc_ref,
):
    rows = out_a_ref.shape[1]
    each = q_a_ref.shape[1] // width
    me = me_ref[0]
    lane = pl.multiple_of(lax.rem(me, each) * width, 128)
    for which, (q_ref, out_ref) in enumerate(((q_a_ref, out_a_ref), (q_b_ref, out_b_ref))):
        riders = q_ref[rows:, pl.ds(lane, width)].astype(jnp.float32)
        row = lax.broadcasted_iota(jnp.int32, riders.shape, 0)
        mine = jnp.sum(jnp.where(row == me // each, riders, 0.0), axis=0, keepdims=True)
        wide_ref[which : which + 1, :] = mine.astype(jnp.int32)
    pltpu.sync_copy(wide_ref, list_ref)
    for which, (q_ref, out_ref) in enumerate(((q_a_ref, out_a_ref), (q_b_ref, out_b_ref))):
        count = list_ref[which, width - 1]

        @pl.when(count > 0)
        def _():
            turn(q_ref, qt_ref)
            attend(
                lambda index: list_ref[which, index], count, store_ref, None, None,
                qt_ref, k_ref, v_ref, vt_ref, s_ref, max_ref, acc_ref, scale,
            )
            finish(out_ref, max_ref, acc_ref, scale)

        @pl.when(count == 0)
        def _():
            out_ref[...] = jnp.zeros_like(out_ref)
            write_logs(out_ref, jnp.full((max_ref.shape[0], rows), LOW, jnp.float32))


def attention_scratch(heads, rows, head_dim, block_rows):
    keys = TILE * block_rows
    return [
        pltpu.VMEM((heads, head_dim, rows), jnp.bfloat16),
        pltpu.VMEM((2, keys, head_dim), jnp.bfloat16),
        pltpu.VMEM((keys, head_dim), jnp.bfloat16),
        pltpu.VMEM((2, head_dim + 16, keys), jnp.bfloat16),
        pltpu.VMEM((keys, rows), jnp.float32),
        pltpu.VMEM((heads, 1, rows), jnp.float32),
        pltpu.VMEM((heads, head_dim + 16, rows), jnp.float32),
    ]


def attention_cost(rows, keys, head_dim, heads):
    return pl.CostEstimate(
        flops=4 * rows * keys * head_dim * heads,
        bytes_accessed=4 * 1024 * 1024,
        transcendentals=rows * keys * heads,
    )


def project_kernel(
    peers, me_ref, span_live_ref, *refs
):
    parts = refs[: 2 * peers - 1]
    weight_ref, out_ref, att_ref = refs[2 * peers - 1 :]
    rows, features = att_ref.shape

    @pl.when(pl.program_id(0) == 0)
    def _():
        heads = 8 * ((parts[0].shape[0] - features) // 32)
        head_dim = features // heads
        me = me_ref[0]
        logs = []
        for index, part in enumerate(parts):
            pieces = part[features:, :].astype(jnp.float32)
            log = pieces[:heads] + pieces[heads : 2 * heads] + pieces[2 * heads : 3 * heads]
            if index:
                away = (index + 1) // 2
                valid = me >= away if index % 2 else me + away < peers
                log = jnp.where(valid, log, LOW)
            logs.append(log)
        top = functools.reduce(jnp.maximum, logs)
        weights = [jnp.exp2(log - top) for log in logs]
        inverse = 1.0 / functools.reduce(jnp.add, weights)
        row = lax.broadcasted_iota(jnp.int32, (heads, rows), 1)
        inverse = jnp.where(row < span_live_ref[0], inverse, 0.0)
        weights = [weight * inverse for weight in weights]
        for g in range(heads):
            total = jnp.zeros((head_dim, rows), jnp.float32)
            for part, weight in zip(parts, weights):
                total += part[g * head_dim : (g + 1) * head_dim, :].astype(jnp.float32) * weight[
                    g : g + 1
                ]
            att_ref[:, g * head_dim : (g + 1) * head_dim] = total.T.astype(jnp.bfloat16)

    out_ref[...] = jnp.dot(
        att_ref[...], weight_ref[...], preferred_element_type=jnp.float32
    ).astype(jnp.bfloat16)


def project(me, span_live, parts, out_weight, peers):
    features, outputs = out_weight.shape
    rows = parts[0].shape[1]
    width = 512
    whole = lambda i, *_: (0, 0)
    return pl.pallas_call(
        functools.partial(project_kernel, peers),
        out_shape=jax.ShapeDtypeStruct((rows, outputs), jnp.bfloat16),
        grid_spec=pltpu.PrefetchScalarGridSpec(
            num_scalar_prefetch=2,
            grid=(outputs // width,),
            in_specs=[pl.BlockSpec(part.shape, whole) for part in parts]
            + [pl.BlockSpec((features, width), lambda i, *_: (0, i))],
            out_specs=pl.BlockSpec((rows, width), lambda i, *_: (0, i)),
            scratch_shapes=[pltpu.VMEM((rows, features), jnp.bfloat16)],
        ),
        compiler_params=pltpu.CompilerParams(vmem_limit_bytes=VMEM_LIMIT),
        cost_estimate=pl.CostEstimate(
            flops=2 * rows * features * outputs,
            bytes_accessed=2 * (features + rows) * outputs,
            transcendentals=0,
        ),
        name="project",
    )(me, span_live, *parts, out_weight)


def pack_kernel(span_live_ref, owners_ref, span_ref, out_ref, counts_ref):
    peers = out_ref.shape[1]
    block_rows, head_dim = out_ref.shape[3:]
    out_ref[...] = jnp.zeros_like(out_ref)
    for k in range(peers):
        counts_ref[k] = 0
    row = lax.broadcasted_iota(jnp.int32, (block_rows, head_dim), 0)
    for b in range(span_ref.shape[1] // block_rows):
        owner = owners_ref[b]
        rank = counts_ref[owner]
        counts_ref[owner] = rank + 1
        keep = row + b * block_rows < span_live_ref[0]
        for side in range(2):
            block = span_ref[side, b * block_rows : (b + 1) * block_rows, :]
            out_ref[side, owner, rank] = jnp.where(keep, block, jnp.zeros_like(block))


def shards(
    queries,
    cache_store,
    span_cache,
    out_weight,
    prefix_blocks,
    span_lengths,
    hit_holders,
    hit_slots,
    store_owners,
):
    peers = lax.axis_size("inst")
    block_rows, head_dim = cache_store.shape[2:]
    rows, columns = queries.shape
    heads = columns // head_dim
    block_max = hit_slots.shape[1]
    cap = max(2, block_max * 5 // (4 * peers))
    new_count = rows // block_rows
    push_cap = max(2, 2 * new_count // peers)
    scale = math.log2(math.e) / math.sqrt(head_dim)
    me = lax.axis_index("inst").reshape(1)
    width = round_up(cap + 1, 128)
    part_shape = jax.ShapeDtypeStruct((heads * head_dim + 4 * heads, rows), jnp.bfloat16)
    scratch = attention_scratch(heads, rows, head_dim, block_rows)
    params = pltpu.CompilerParams(vmem_limit_bytes=VMEM_LIMIT)

    def shift(value, by):
        pairs = [(i, i + by) for i in range(peers) if 0 <= i + by < peers]
        return lax.ppermute(value, "inst", pairs)

    lists, loaded = route(
        prefix_blocks, hit_holders.reshape(1, -1), hit_slots, queries, peers, width
    )
    from_left, from_right = shift(loaded, 1), shift(loaded, -1)
    own = pl.pallas_call(
        functools.partial(own_kernel, scale),
        out_shape=part_shape,
        in_specs=[SMEM, SMEM, SMEM, VMEM, VMEM, VMEM],
        out_specs=VMEM,
        scratch_shapes=scratch,
        compiler_params=params,
        cost_estimate=attention_cost(rows, 8 * rows, head_dim, heads),
        name="own_attention",
    )(me, span_lengths, lists, queries, cache_store, span_cache)

    parts, after = [own], own
    for away in range(1, peers):
        guests = (from_left, from_right)
        if away + 1 < peers:
            from_left, from_right, after = lax.optimization_barrier((*guests, after))
            from_left, from_right = shift(from_left, 1), shift(from_right, -1)
        part_a, part_b = pl.pallas_call(
            functools.partial(guest_kernel, scale, width),
            out_shape=(part_shape, part_shape),
            in_specs=[SMEM, VMEM, VMEM, VMEM, pl.BlockSpec(memory_space=pl.ANY)],
            out_specs=(VMEM, VMEM),
            scratch_shapes=[pltpu.VMEM((2, width), jnp.int32), pltpu.SMEM((2, width), jnp.int32)]
            + scratch,
            compiler_params=params,
            cost_estimate=attention_cost(rows, 8 * rows, head_dim, heads),
            name="guest_attention",
        )(me, *guests, cache_store, after)
        after = part_a
        parts.append(shift(part_b, away))
        parts.append(shift(part_a, -away))

    partial = project(me, span_lengths, parts, out_weight, peers)
    projected = lax.psum_scatter(partial, "tp", scatter_dimension=0, tiled=True)

    outgoing = pl.pallas_call(
        pack_kernel,
        out_shape=jax.ShapeDtypeStruct(
            (2, peers, push_cap, block_rows, head_dim), jnp.bfloat16
        ),
        in_specs=[SMEM, SMEM, VMEM],
        out_specs=VMEM,
        scratch_shapes=[pltpu.SMEM((peers,), jnp.int32)],
        compiler_params=pltpu.CompilerParams(vmem_limit_bytes=VMEM_LIMIT),
        name="pack_blocks",
    )(span_lengths, store_owners.reshape(-1), span_cache)
    incoming = lax.all_to_all(outgoing, "inst", split_axis=1, concat_axis=1, tiled=True)
    pushed_blocks = incoming.reshape(2, peers * push_cap, block_rows, head_dim)
    return (projected, pushed_blocks)


def solution(mesh):
    return jax.shard_map(
        shards,
        mesh=mesh,
        in_specs=(
            P(("pods", "inst"), "tp"),
            P(None, ("pods", "inst"), None, "tp"),
            P(None, ("pods", "inst"), "tp"),
            P("tp", None),
            P(("pods", "inst")),
            P(("pods", "inst")),
            P(("pods", "inst"), None, None),
            P(("pods", "inst"), None),
            P(("pods", "inst"), None, None),
        ),
        out_specs=(P(("pods", "inst", "tp"), None), P(None, ("pods", "inst"), None, "tp")),
        check_vma=False,
    )
```

```python
import functools
import math

import jax
import jax.numpy as jnp
from jax import lax
from jax.experimental import pallas as pl
from jax.experimental.pallas import tpu as pltpu
from jax.sharding import PartitionSpec as P

LOW = -1e30
TOP = 2.0**100
TILE = 16
STACK = 4
VMEM_LIMIT = 32 * 1024 * 1024

SMEM = pl.BlockSpec(memory_space=pltpu.SMEM)
VMEM = pl.BlockSpec(memory_space=pltpu.VMEM)


def round_up(number, step):
    return -(-number // step) * step


def route_kernel(live_ref, holders_ref, slots_ref, q_ref, lists_ref, out_ref):
    peers, width = lists_ref.shape
    number = holders_ref.shape[1]
    padded = round_up(peers, 16)
    holder = lax.broadcasted_iota(jnp.int32, (padded, number), 0)
    entry = lax.broadcasted_iota(jnp.int32, (padded, number), 1)
    hot = (holders_ref[...] == holder) & (entry < live_ref[0])
    ones = jnp.where(hot, 1.0, 0.0)
    earlier = lax.broadcasted_iota(jnp.int32, (number, number), 0) < lax.broadcasted_iota(
        jnp.int32, (number, number), 1
    )
    ranks = jnp.dot(
        ones.astype(jnp.bfloat16),
        jnp.where(earlier, 1.0, 0.0).astype(jnp.bfloat16),
        preferred_element_type=jnp.float32,
    )
    rank = jnp.sum(ranks * ones, axis=0, keepdims=True)
    rank = jnp.broadcast_to(rank, (8, number)).T[:, :1].astype(jnp.int32)
    place = lax.broadcasted_iota(jnp.int32, (number, width), 1) == rank
    slots = jnp.where(hot, slots_ref[...], 0).astype(jnp.float32)
    lists = jnp.dot(
        slots.astype(jnp.bfloat16),
        jnp.where(place, 1.0, 0.0).astype(jnp.bfloat16),
        preferred_element_type=jnp.float32,
    )
    counts = jnp.sum(ones, axis=1, keepdims=True)
    last = lax.broadcasted_iota(jnp.int32, (padded, width), 1) == width - 1
    lists = jnp.where(last, counts, lists)[:peers]
    lists_ref[...] = lists.astype(jnp.int32)

    rows, columns = q_ref.shape
    out_ref[:rows, :] = q_ref[...]
    each = columns // width
    riders = out_ref.shape[0] - rows
    row = lax.broadcasted_iota(jnp.int32, (riders, columns), 0)
    tail = jnp.zeros((riders, columns), jnp.float32)
    for r in range(-(-peers // each)):
        line = [lists[h : h + 1] for h in range(r * each, min(peers, (r + 1) * each))]
        line += [jnp.zeros((1, width), jnp.float32)] * (each - len(line))
        tail = jnp.where(row == r, jnp.concatenate(line, axis=1), tail)
    out_ref[rows:, :] = tail.astype(jnp.bfloat16)


def route(live, holders, slots, queries, peers, width):
    rows, columns = queries.shape
    riders = round_up(-(-peers // (columns // width)), 16)
    return pl.pallas_call(
        route_kernel,
        out_shape=(
            jax.ShapeDtypeStruct((peers, width), jnp.int32),
            jax.ShapeDtypeStruct((rows + riders, columns), jnp.bfloat16),
        ),
        in_specs=[SMEM, VMEM, VMEM, VMEM],
        out_specs=(VMEM, VMEM),
        compiler_params=pltpu.CompilerParams(vmem_limit_bytes=VMEM_LIMIT),
        name="route",
    )(live, holders, slots, queries)


def score(q, keys):
    return lax.dot_general(q, keys, (((1,), (1,)), ((), ())), preferred_element_type=jnp.float32)


def twice(value):
    return jnp.concatenate([value, value], axis=1)


def attend(
    slot, count, store_ref, span_ref, span_live, q_ref, k_ref, v_ref, s_ref, ref_ref, acc_ref, rows,
    scale,
):
    block_rows, head_dim = store_ref.shape[2:]
    heads = q_ref.shape[0] // rows
    stack = rows * math.gcd(heads, STACK)
    stacks = q_ref.shape[0] // stack
    tiles = (count + TILE - 1) // TILE

    def fetch(tile, into):
        for j in range(TILE):
            index = tile * TILE + j
            here = slot(jnp.maximum(jnp.minimum(index, count - 1), 0))
            at = slice(j * block_rows, (j + 1) * block_rows)
            k_ref[into, at, :] = store_ref[0, here]
            block = store_ref[1, here]
            v_ref[into, at, :head_dim] = jnp.where(index < count, block, jnp.zeros_like(block))
            v_ref[into, at, head_dim:] = jnp.where(
                index < count, jnp.ones_like(block), jnp.zeros_like(block)
            )

    def start():
        if span_ref is None:
            acc_ref[...] = jnp.zeros_like(acc_ref)
            return
        keys = span_ref.shape[1]
        key = lax.broadcasted_iota(jnp.int32, (rows, keys), 1)
        row = lax.broadcasted_iota(jnp.int32, (rows, keys), 0)
        mask = (key <= row) & (key < span_live)
        values = jnp.concatenate(
            [span_ref[1], jnp.ones((keys, head_dim), jnp.bfloat16)], axis=1
        )
        s = score(q_ref[:rows, :], span_ref[0])
        for g in range(heads):
            at = slice(g * rows, (g + 1) * rows)
            if g + 1 < heads:
                following = score(q_ref[(g + 1) * rows : (g + 2) * rows, :], span_ref[0])
            s = jnp.where(mask, s, LOW)
            top = jnp.max(s, axis=1, keepdims=True)
            ref_ref[at, :] = jnp.broadcast_to(top, (rows, head_dim))
            p = jnp.exp2((s - top) * scale).astype(jnp.bfloat16)
            acc_ref[at, :] = jnp.dot(p, values, preferred_element_type=jnp.float32)
            s = following

    start()

    @pl.when(count > 0)
    def _():
        fetch(0, 0)
        if span_ref is None:
            few = score(q_ref[...], k_ref[0, : 8 * block_rows, :])
            ref_ref[...] = jnp.broadcast_to(
                jnp.max(few, axis=1, keepdims=True), ref_ref.shape
            )
        s_ref[...] = score(q_ref[:stack, :], k_ref[0])

        def step(tile, carry):
            now = lax.rem(tile, 2)
            later = 1 - now
            keys, values = k_ref[now], v_ref[now]
            s = s_ref[...]
            fetch(tile + 1, later)
            for c in range(stacks):
                at = slice(c * stack, (c + 1) * stack)
                if c + 1 < stacks:
                    following = score(q_ref[(c + 1) * stack : (c + 2) * stack, :], keys)
                else:
                    s_ref[...] = score(q_ref[:stack, :], k_ref[later])
                p = jnp.exp2((s - twice(ref_ref[at, :])) * scale).astype(jnp.bfloat16)
                acc_ref[at, :] += jnp.dot(p, values, preferred_element_type=jnp.float32)
                s = following
            return carry

        lax.fori_loop(0, tiles, step, 0)
        beyond = jnp.max(jnp.where(acc_ref[:, head_dim:] < TOP, 0.0, 1.0))

        @pl.when(beyond > 0.0)
        def _():
            start()
            if span_ref is None:
                ref_ref[...] = jnp.full_like(ref_ref, LOW)

            def careful(tile, carry):
                fetch(tile, 0)

                def head(g, inner):
                    at = pl.ds(pl.multiple_of(g * rows, rows), rows)
                    s = score(q_ref[at, :], k_ref[0])
                    old = ref_ref[at, :]
                    new = jnp.maximum(old, jnp.max(s, axis=1, keepdims=True))
                    p = jnp.exp2((s - twice(new)) * scale).astype(jnp.bfloat16)
                    update = jnp.dot(p, v_ref[0], preferred_element_type=jnp.float32)
                    acc_ref[at, :] = (
                        acc_ref[at, :] * twice(jnp.exp2((old - new) * scale)) + update
                    )
                    ref_ref[at, :] = new
                    return inner

                return lax.fori_loop(0, heads, head, carry)

            lax.fori_loop(0, tiles, careful, 0)


def stack_heads(queries_ref, q_ref, rows):
    head_dim = q_ref.shape[1]
    for g in range(q_ref.shape[0] // rows):
        q_ref[g * rows : (g + 1) * rows, :] = queries_ref[
            :rows, g * head_dim : (g + 1) * head_dim
        ]


def write_logs(out_ref, logs):
    heads, rows = logs.shape
    first = logs.astype(jnp.bfloat16).astype(jnp.float32)
    rest = logs - first
    second = rest.astype(jnp.bfloat16).astype(jnp.float32)
    third = rest - second
    spare = jnp.zeros((heads, out_ref.shape[1] - 3 * rows), jnp.float32)
    line = jnp.concatenate([first, second, third, spare], axis=1)
    padding = jnp.zeros((16 - heads, out_ref.shape[1]), jnp.float32)
    out_ref[rows:, :] = jnp.concatenate([line, padding], axis=0).astype(jnp.bfloat16)


def finish(out_ref, ref_ref, acc_ref, rows, scale):
    head_dim = ref_ref.shape[1]
    heads = ref_ref.shape[0] // rows
    lane = lax.broadcasted_iota(jnp.int32, (rows, head_dim), 1)
    logs = jnp.zeros((rows, head_dim), jnp.float32)
    for g in range(heads):
        at = slice(g * rows, (g + 1) * rows)
        total = acc_ref[at, head_dim:]
        out_ref[:rows, g * head_dim : (g + 1) * head_dim] = (
            acc_ref[at, :head_dim] / total
        ).astype(jnp.bfloat16)
        logs = jnp.where(lane == g, ref_ref[at, :] * scale + jnp.log2(total), logs)
    write_logs(out_ref, logs.T[:heads])


def own_kernel(
    scale, me_ref, span_live_ref, lists_ref, queries_ref, store_ref, span_ref, out_ref,
    q_ref, k_ref, v_ref, s_ref, ref_ref, acc_ref,
):
    me = me_ref[0]
    rows = queries_ref.shape[0]
    stack_heads(queries_ref, q_ref, rows)
    attend(
        lambda index: lists_ref[me, index], lists_ref[me, lists_ref.shape[1] - 1], store_ref,
        span_ref, span_live_ref[0], q_ref, k_ref, v_ref, s_ref, ref_ref, acc_ref, rows, scale,
    )
    finish(out_ref, ref_ref, acc_ref, rows, scale)


def guest_kernel(
    scale, width, rows, me_ref, a_ref, b_ref, store_ref, after_ref, out_a_ref, out_b_ref,
    wide_ref, list_ref, sem_ref, q_ref, k_ref, v_ref, s_ref, ref_ref, acc_ref,
):
    each = a_ref.shape[1] // width
    me = me_ref[0]
    lane = pl.multiple_of(lax.rem(me, each) * width, 128)
    for which, loaded_ref in enumerate((a_ref, b_ref)):
        riders = loaded_ref[rows:, pl.ds(lane, width)].astype(jnp.float32)
        row = lax.broadcasted_iota(jnp.int32, riders.shape, 0)
        mine = jnp.sum(jnp.where(row == me // each, riders, 0.0), axis=0, keepdims=True)
        wide_ref[which : which + 1, :] = mine.astype(jnp.int32)
    copy = pltpu.make_async_copy(wide_ref, list_ref, sem_ref)
    copy.start()
    stack_heads(a_ref, q_ref, rows)
    copy.wait()
    for which, (loaded_ref, out_ref) in enumerate(((a_ref, out_a_ref), (b_ref, out_b_ref))):
        count = list_ref[which, width - 1]

        @pl.when(count > 0)
        def _():
            if which:
                stack_heads(loaded_ref, q_ref, rows)
            attend(
                lambda index: list_ref[which, index], count, store_ref, None, None,
                q_ref, k_ref, v_ref, s_ref, ref_ref, acc_ref, rows, scale,
            )
            finish(out_ref, ref_ref, acc_ref, rows, scale)

        @pl.when(count == 0)
        def _():
            out_ref[...] = jnp.zeros_like(out_ref)
            write_logs(out_ref, jnp.full((q_ref.shape[0] // rows, rows), LOW, jnp.float32))


def attention_scratch(heads, rows, head_dim, block_rows):
    keys = TILE * block_rows
    return [
        pltpu.VMEM((heads * rows, head_dim), jnp.bfloat16),
        pltpu.VMEM((2, keys, head_dim), jnp.bfloat16),
        pltpu.VMEM((2, keys, 2 * head_dim), jnp.bfloat16),
        pltpu.VMEM((rows * math.gcd(heads, STACK), keys), jnp.float32),
        pltpu.VMEM((heads * rows, head_dim), jnp.float32),
        pltpu.VMEM((heads * rows, 2 * head_dim), jnp.float32),
    ]


def attention_cost(rows, keys, head_dim, heads):
    return pl.CostEstimate(
        flops=4 * rows * keys * head_dim * heads,
        bytes_accessed=4 * 1024 * 1024,
        transcendentals=rows * keys * heads,
    )


def project_kernel(peers, heads, me_ref, span_live_ref, *refs):
    parts = refs[: 2 * peers - 1]
    weight_ref, out_ref, held_ref, att_ref, sem_ref = refs[2 * peers - 1 :]
    rows, features = att_ref.shape
    chunks, _, width = held_ref.shape
    head_dim = features // heads
    copies = [
        pltpu.make_async_copy(
            weight_ref.at[:, pl.ds(i * width, width)], held_ref.at[i], sem_ref.at[i]
        )
        for i in range(chunks)
    ]
    for copy in copies:
        copy.start()

    me = me_ref[0]
    logs = []
    for index, part in enumerate(parts):
        pieces = part[rows:, :].astype(jnp.float32)[:heads]
        log = pieces[:, :rows] + pieces[:, rows : 2 * rows] + pieces[:, 2 * rows : 3 * rows]
        if index:
            away = (index + 1) // 2
            valid = me >= away if index % 2 else me + away < peers
            log = jnp.where(valid, log, LOW)
        logs.append(log)
    top = functools.reduce(jnp.maximum, logs)
    weights = [jnp.exp2(log - top) for log in logs]
    inverse = 1.0 / functools.reduce(jnp.add, weights)
    row = lax.broadcasted_iota(jnp.int32, (heads, rows), 1)
    inverse = jnp.where(row < span_live_ref[0], inverse, 0.0)
    weights = [(weight * inverse).T for weight in weights]
    for g in range(heads):
        at = slice(g * head_dim, (g + 1) * head_dim)
        total = jnp.zeros((rows, head_dim), jnp.float32)
        for part, weight in zip(parts, weights):
            total += part[:rows, at].astype(jnp.float32) * weight[:, g : g + 1]
        att_ref[:, at] = total.astype(jnp.bfloat16)

    for i in range(chunks):
        copies[i].wait()
        out_ref[:, i * width : (i + 1) * width] = jnp.dot(
            att_ref[...], held_ref[i], preferred_element_type=jnp.float32
        ).astype(jnp.bfloat16)


def project(me, span_live, parts, out_weight, peers, heads):
    features, outputs = out_weight.shape
    rows = parts[0].shape[0] - 16
    width = 512
    chunks = outputs // width
    return pl.pallas_call(
        functools.partial(project_kernel, peers, heads),
        out_shape=jax.ShapeDtypeStruct((rows, outputs), jnp.bfloat16),
        in_specs=[SMEM, SMEM]
        + [VMEM] * len(parts)
        + [pl.BlockSpec(memory_space=pl.ANY)],
        out_specs=VMEM,
        scratch_shapes=[
            pltpu.VMEM((chunks, features, width), jnp.bfloat16),
            pltpu.VMEM((rows, features), jnp.bfloat16),
            pltpu.SemaphoreType.DMA((chunks,)),
        ],
        compiler_params=pltpu.CompilerParams(vmem_limit_bytes=VMEM_LIMIT),
        cost_estimate=pl.CostEstimate(
            flops=2 * rows * features * outputs,
            bytes_accessed=2 * (features + rows) * outputs,
            transcendentals=0,
        ),
        name="project",
    )(me, span_live, *parts, out_weight)


def pack_kernel(span_live_ref, owners_ref, span_ref, out_ref, counts_ref):
    peers = out_ref.shape[1]
    block_rows, head_dim = out_ref.shape[3:]
    out_ref[...] = jnp.zeros_like(out_ref)
    for k in range(peers):
        counts_ref[k] = 0
    row = lax.broadcasted_iota(jnp.int32, (block_rows, head_dim), 0)
    for b in range(span_ref.shape[1] // block_rows):
        owner = owners_ref[b]
        rank = counts_ref[owner]
        counts_ref[owner] = rank + 1
        keep = row + b * block_rows < span_live_ref[0]
        for side in range(2):
            block = span_ref[side, b * block_rows : (b + 1) * block_rows, :]
            out_ref[side, owner, rank] = jnp.where(keep, block, jnp.zeros_like(block))


def shards(
    queries,
    cache_store,
    span_cache,
    out_weight,
    prefix_blocks,
    span_lengths,
    hit_holders,
    hit_slots,
    store_owners,
):
    peers = lax.axis_size("inst")
    block_rows, head_dim = cache_store.shape[2:]
    rows, columns = queries.shape
    heads = columns // head_dim
    block_max = hit_slots.shape[1]
    cap = max(2, block_max * 5 // (4 * peers))
    new_count = rows // block_rows
    push_cap = max(2, 2 * new_count // peers)
    scale = math.log2(math.e) / math.sqrt(head_dim)
    me = lax.axis_index("inst").reshape(1)
    width = round_up(cap + 1, 128)
    part_shape = jax.ShapeDtypeStruct((rows + 16, columns), jnp.bfloat16)
    scratch = attention_scratch(heads, rows, head_dim, block_rows)
    params = pltpu.CompilerParams(vmem_limit_bytes=VMEM_LIMIT)

    def shift(value, by):
        pairs = [(i, i + by) for i in range(peers) if 0 <= i + by < peers]
        return lax.ppermute(value, "inst", pairs)

    lists, loaded = route(
        prefix_blocks, hit_holders.reshape(1, -1), hit_slots, queries, peers, width
    )
    from_left, from_right = shift(loaded, 1), shift(loaded, -1)
    own = pl.pallas_call(
        functools.partial(own_kernel, scale),
        out_shape=part_shape,
        in_specs=[SMEM, SMEM, SMEM, VMEM, VMEM, VMEM],
        out_specs=VMEM,
        scratch_shapes=scratch,
        compiler_params=params,
        cost_estimate=attention_cost(rows, 8 * rows, head_dim, heads),
        name="own_attention",
    )(me, span_lengths, lists, queries, cache_store, span_cache)

    parts, after = [own], own
    for away in range(1, peers):
        guests = (from_left, from_right)
        if away + 1 < peers:
            from_left, from_right, after = lax.optimization_barrier((*guests, after))
            from_left, from_right = shift(from_left, 1), shift(from_right, -1)
        part_a, part_b = pl.pallas_call(
            functools.partial(guest_kernel, scale, width, rows),
            out_shape=(part_shape, part_shape),
            in_specs=[SMEM, VMEM, VMEM, VMEM, pl.BlockSpec(memory_space=pl.ANY)],
            out_specs=(VMEM, VMEM),
            scratch_shapes=[
                pltpu.VMEM((2, width), jnp.int32),
                pltpu.SMEM((2, width), jnp.int32),
                pltpu.SemaphoreType.DMA,
                *scratch,
            ],
            compiler_params=params,
            cost_estimate=attention_cost(rows, 8 * rows, head_dim, heads),
            name="guest_attention",
        )(me, *guests, cache_store, after)
        after = part_a
        parts.append(shift(part_b, away))
        parts.append(shift(part_a, -away))

    partial = project(me, span_lengths, parts, out_weight, peers, heads)
    projected = lax.psum_scatter(partial, "tp", scatter_dimension=0, tiled=True)

    outgoing = pl.pallas_call(
        pack_kernel,
        out_shape=jax.ShapeDtypeStruct(
            (2, peers, push_cap, block_rows, head_dim), jnp.bfloat16
        ),
        in_specs=[SMEM, SMEM, VMEM],
        out_specs=VMEM,
        scratch_shapes=[pltpu.SMEM((peers,), jnp.int32)],
        compiler_params=pltpu.CompilerParams(vmem_limit_bytes=VMEM_LIMIT),
        name="pack_blocks",
    )(span_lengths, store_owners.reshape(-1), span_cache)
    incoming = lax.all_to_all(outgoing, "inst", split_axis=1, concat_axis=1, tiled=True)
    pushed_blocks = incoming.reshape(2, peers * push_cap, block_rows, head_dim)
    return (projected, pushed_blocks)


def solution(mesh):
    return jax.shard_map(
        shards,
        mesh=mesh,
        in_specs=(
            P(("pods", "inst"), "tp"),
            P(None, ("pods", "inst"), None, "tp"),
            P(None, ("pods", "inst"), "tp"),
            P("tp", None),
            P(("pods", "inst")),
            P(("pods", "inst")),
            P(("pods", "inst"), None, None),
            P(("pods", "inst"), None),
            P(("pods", "inst"), None, None),
        ),
        out_specs=(P(("pods", "inst", "tp"), None), P(None, ("pods", "inst"), None, "tp")),
        check_vma=False,
    )
```

```python
import functools
import math

import jax
import jax.numpy as jnp
from jax import lax
from jax.experimental import pallas as pl
from jax.experimental.pallas import tpu as pltpu
from jax.sharding import PartitionSpec as P

LOW = -1e30
TOP = 2.0**100
TILE = 16
STACK = 4
VMEM_LIMIT = 32 * 1024 * 1024

SMEM = pl.BlockSpec(memory_space=pltpu.SMEM)
VMEM = pl.BlockSpec(memory_space=pltpu.VMEM)
HBM = pl.BlockSpec(memory_space=pltpu.HBM)


def round_up(number, step):
    return -(-number // step) * step


def route_kernel(
    live_ref, holders_in, slots_in, q_in, lists_ref, out_ref, holders_ref, slots_ref, tail_ref, sems
):
    rows, columns = q_in.shape
    loading = [
        pltpu.make_async_copy(holders_in, holders_ref, sems.at[0]),
        pltpu.make_async_copy(slots_in, slots_ref, sems.at[1]),
    ]
    passing = pltpu.make_async_copy(q_in, out_ref.at[pl.ds(0, rows)], sems.at[2])
    for copy in loading:
        copy.start()
    passing.start()
    for copy in loading:
        copy.wait()
    peers, width = lists_ref.shape
    number = holders_ref.shape[1]
    padded = round_up(peers, 16)
    holder = lax.broadcasted_iota(jnp.int32, (padded, number), 0)
    entry = lax.broadcasted_iota(jnp.int32, (padded, number), 1)
    hot = (holders_ref[...] == holder) & (entry < live_ref[0])
    ones = jnp.where(hot, 1.0, 0.0)
    earlier = lax.broadcasted_iota(jnp.int32, (number, number), 0) < lax.broadcasted_iota(
        jnp.int32, (number, number), 1
    )
    ranks = jnp.dot(
        ones.astype(jnp.bfloat16),
        jnp.where(earlier, 1.0, 0.0).astype(jnp.bfloat16),
        preferred_element_type=jnp.float32,
    )
    rank = jnp.sum(ranks * ones, axis=0, keepdims=True)
    rank = jnp.broadcast_to(rank, (8, number)).T[:, :1].astype(jnp.int32)
    place = lax.broadcasted_iota(jnp.int32, (number, width), 1) == rank
    slots = jnp.where(hot, slots_ref[...], 0).astype(jnp.float32)
    lists = jnp.dot(
        slots.astype(jnp.bfloat16),
        jnp.where(place, 1.0, 0.0).astype(jnp.bfloat16),
        preferred_element_type=jnp.float32,
    )
    counts = jnp.sum(ones, axis=1, keepdims=True)
    last = lax.broadcasted_iota(jnp.int32, (padded, width), 1) == width - 1
    lists = jnp.where(last, counts, lists)[:peers]
    lists_ref[...] = lists.astype(jnp.int32)

    each = columns // width
    riders = tail_ref.shape[0]
    row = lax.broadcasted_iota(jnp.int32, (riders, columns), 0)
    tail = jnp.zeros((riders, columns), jnp.float32)
    for r in range(-(-peers // each)):
        line = [lists[h : h + 1] for h in range(r * each, min(peers, (r + 1) * each))]
        line += [jnp.zeros((1, width), jnp.float32)] * (each - len(line))
        tail = jnp.where(row == r, jnp.concatenate(line, axis=1), tail)
    tail_ref[...] = tail.astype(jnp.bfloat16)
    riding = pltpu.make_async_copy(tail_ref, out_ref.at[pl.ds(rows, riders)], sems.at[3])
    riding.start()
    passing.wait()
    riding.wait()


def route(live, holders, slots, queries, peers, width):
    rows, columns = queries.shape
    riders = round_up(-(-peers // (columns // width)), 16)
    return pl.pallas_call(
        route_kernel,
        out_shape=(
            jax.ShapeDtypeStruct((peers, width), jnp.int32),
            jax.ShapeDtypeStruct((rows + riders, columns), jnp.bfloat16),
        ),
        in_specs=[SMEM, HBM, HBM, HBM],
        out_specs=(VMEM, HBM),
        scratch_shapes=[
            pltpu.VMEM(holders.shape, jnp.int32),
            pltpu.VMEM(slots.shape, jnp.int32),
            pltpu.VMEM((riders, columns), jnp.bfloat16),
            pltpu.SemaphoreType.DMA((4,)),
        ],
        compiler_params=pltpu.CompilerParams(vmem_limit_bytes=62 * 1024 * 1024),
        name="route",
    )(live, holders, slots, queries)


def score(q, keys):
    return lax.dot_general(q, keys, (((1,), (1,)), ((), ())), preferred_element_type=jnp.float32)


def twice(value):
    return jnp.concatenate([value, value], axis=1)


def attend(
    slot, count, store_ref, span_ref, span_live, q_ref, k_ref, v_ref, s_ref, ref_ref, acc_ref, rows,
    scale, stored=None,
):
    block_rows, head_dim = store_ref.shape[2:]
    heads = q_ref.shape[0] // rows
    stack = rows * math.gcd(heads, STACK)
    stacks = q_ref.shape[0] // stack
    tiles = (count + TILE - 1) // TILE

    def fetch(tile, into):
        for j in range(TILE):
            index = tile * TILE + j
            here = slot(jnp.maximum(jnp.minimum(index, count - 1), 0))
            at = slice(j * block_rows, (j + 1) * block_rows)
            k_ref[into, at, :] = store_ref[0, here]
            block = store_ref[1, here]
            v_ref[into, at, :head_dim] = jnp.where(index < count, block, jnp.zeros_like(block))
            v_ref[into, at, head_dim:] = jnp.where(
                index < count, jnp.ones_like(block), jnp.zeros_like(block)
            )

    def start():
        if span_ref is None:
            acc_ref[...] = jnp.zeros_like(acc_ref)
            return
        keys = span_ref.shape[1]
        key = lax.broadcasted_iota(jnp.int32, (rows, keys), 1)
        row = lax.broadcasted_iota(jnp.int32, (rows, keys), 0)
        mask = (key <= row) & (key < span_live)
        values = jnp.concatenate(
            [span_ref[1], jnp.ones((keys, head_dim), jnp.bfloat16)], axis=1
        )
        s = score(q_ref[:rows, :], span_ref[0])
        for g in range(heads):
            at = slice(g * rows, (g + 1) * rows)
            if g + 1 < heads:
                following = score(q_ref[(g + 1) * rows : (g + 2) * rows, :], span_ref[0])
            s = jnp.where(mask, s, LOW)
            top = jnp.max(s, axis=1, keepdims=True)
            ref_ref[at, :] = jnp.broadcast_to(top, (rows, head_dim))
            p = jnp.exp2((s - top) * scale).astype(jnp.bfloat16)
            acc_ref[at, :] = jnp.dot(p, values, preferred_element_type=jnp.float32)
            s = following

    start()
    if stored is not None:
        stored()

    @pl.when(count > 0)
    def _():
        fetch(0, 0)
        if span_ref is None:
            few = score(q_ref[...], k_ref[0, : 8 * block_rows, :])
            ref_ref[...] = jnp.broadcast_to(
                jnp.max(few, axis=1, keepdims=True), ref_ref.shape
            )
        s_ref[...] = score(q_ref[:stack, :], k_ref[0])

        def step(tile, carry):
            now = lax.rem(tile, 2)
            later = 1 - now
            keys, values = k_ref[now], v_ref[now]
            s = s_ref[...]
            fetch(tile + 1, later)
            for c in range(stacks):
                at = slice(c * stack, (c + 1) * stack)
                if c + 1 < stacks:
                    following = score(q_ref[(c + 1) * stack : (c + 2) * stack, :], keys)
                else:
                    s_ref[...] = score(q_ref[:stack, :], k_ref[later])
                p = jnp.exp2((s - twice(ref_ref[at, :])) * scale).astype(jnp.bfloat16)
                acc_ref[at, :] += jnp.dot(p, values, preferred_element_type=jnp.float32)
                s = following
            return carry

        lax.fori_loop(0, tiles, step, 0)
        beyond = jnp.max(jnp.where(acc_ref[:, head_dim:] < TOP, 0.0, 1.0))

        @pl.when(beyond > 0.0)
        def _():
            start()
            if span_ref is None:
                ref_ref[...] = jnp.full_like(ref_ref, LOW)

            def careful(tile, carry):
                fetch(tile, 0)

                def head(g, inner):
                    at = pl.ds(pl.multiple_of(g * rows, rows), rows)
                    s = score(q_ref[at, :], k_ref[0])
                    old = ref_ref[at, :]
                    new = jnp.maximum(old, jnp.max(s, axis=1, keepdims=True))
                    p = jnp.exp2((s - twice(new)) * scale).astype(jnp.bfloat16)
                    update = jnp.dot(p, v_ref[0], preferred_element_type=jnp.float32)
                    acc_ref[at, :] = (
                        acc_ref[at, :] * twice(jnp.exp2((old - new) * scale)) + update
                    )
                    ref_ref[at, :] = new
                    return inner

                return lax.fori_loop(0, heads, head, carry)

            lax.fori_loop(0, tiles, careful, 0)


def stack_heads(queries_ref, q_ref, rows):
    head_dim = q_ref.shape[1]
    for g in range(q_ref.shape[0] // rows):
        q_ref[g * rows : (g + 1) * rows, :] = queries_ref[
            :rows, g * head_dim : (g + 1) * head_dim
        ]


def write_logs(out_ref, logs):
    heads, rows = logs.shape
    first = logs.astype(jnp.bfloat16).astype(jnp.float32)
    rest = logs - first
    second = rest.astype(jnp.bfloat16).astype(jnp.float32)
    third = rest - second
    spare = jnp.zeros((heads, out_ref.shape[1] - 3 * rows), jnp.float32)
    line = jnp.concatenate([first, second, third, spare], axis=1)
    padding = jnp.zeros((16 - heads, out_ref.shape[1]), jnp.float32)
    out_ref[rows:, :] = jnp.concatenate([line, padding], axis=0).astype(jnp.bfloat16)


def finish(out_ref, ref_ref, acc_ref, rows, scale):
    head_dim = ref_ref.shape[1]
    heads = ref_ref.shape[0] // rows
    lane = lax.broadcasted_iota(jnp.int32, (rows, head_dim), 1)
    logs = jnp.zeros((rows, head_dim), jnp.float32)
    for g in range(heads):
        at = slice(g * rows, (g + 1) * rows)
        total = acc_ref[at, head_dim:]
        out_ref[:rows, g * head_dim : (g + 1) * head_dim] = (
            acc_ref[at, :head_dim] / total
        ).astype(jnp.bfloat16)
        logs = jnp.where(lane == g, ref_ref[at, :] * scale + jnp.log2(total), logs)
    write_logs(out_ref, logs.T[:heads])


def own_kernel(
    scale, me_ref, span_live_ref, lists_ref, queries_in, store_in, span_in, out_ref,
    queries_ref, store_ref, span_ref, sems, q_ref, k_ref, v_ref, s_ref, ref_ref, acc_ref,
):
    me = me_ref[0]
    rows = queries_ref.shape[0]
    copies = [
        pltpu.make_async_copy(source, target, sems.at[i])
        for i, (source, target) in enumerate(
            ((queries_in, queries_ref), (span_in, span_ref), (store_in, store_ref))
        )
    ]
    for copy in copies:
        copy.start()
    copies[0].wait()
    stack_heads(queries_ref, q_ref, rows)
    copies[1].wait()
    attend(
        lambda index: lists_ref[me, index], lists_ref[me, lists_ref.shape[1] - 1], store_ref,
        span_ref, span_live_ref[0], q_ref, k_ref, v_ref, s_ref, ref_ref, acc_ref, rows, scale,
        copies[2].wait,
    )
    finish(out_ref, ref_ref, acc_ref, rows, scale)


def guest_kernel(
    scale, width, rows, me_ref, a_ref, b_ref, store_ref, after_ref, out_a_ref, out_b_ref,
    wide_ref, list_ref, sem_ref, q_ref, k_ref, v_ref, s_ref, ref_ref, acc_ref,
):
    each = a_ref.shape[1] // width
    me = me_ref[0]
    lane = pl.multiple_of(lax.rem(me, each) * width, 128)
    for which, loaded_ref in enumerate((a_ref, b_ref)):
        riders = loaded_ref[rows:, pl.ds(lane, width)].astype(jnp.float32)
        row = lax.broadcasted_iota(jnp.int32, riders.shape, 0)
        mine = jnp.sum(jnp.where(row == me // each, riders, 0.0), axis=0, keepdims=True)
        wide_ref[which : which + 1, :] = mine.astype(jnp.int32)
    copy = pltpu.make_async_copy(wide_ref, list_ref, sem_ref)
    copy.start()
    stack_heads(a_ref, q_ref, rows)
    copy.wait()
    for which, (loaded_ref, out_ref) in enumerate(((a_ref, out_a_ref), (b_ref, out_b_ref))):
        count = list_ref[which, width - 1]

        @pl.when(count > 0)
        def _():
            if which:
                stack_heads(loaded_ref, q_ref, rows)
            attend(
                lambda index: list_ref[which, index], count, store_ref, None, None,
                q_ref, k_ref, v_ref, s_ref, ref_ref, acc_ref, rows, scale,
            )
            finish(out_ref, ref_ref, acc_ref, rows, scale)

        @pl.when(count == 0)
        def _():
            out_ref[...] = jnp.zeros_like(out_ref)
            write_logs(out_ref, jnp.full((q_ref.shape[0] // rows, rows), LOW, jnp.float32))


def attention_scratch(heads, rows, head_dim, block_rows):
    keys = TILE * block_rows
    return [
        pltpu.VMEM((heads * rows, head_dim), jnp.bfloat16),
        pltpu.VMEM((2, keys, head_dim), jnp.bfloat16),
        pltpu.VMEM((2, keys, 2 * head_dim), jnp.bfloat16),
        pltpu.VMEM((rows * math.gcd(heads, STACK), keys), jnp.float32),
        pltpu.VMEM((heads * rows, head_dim), jnp.float32),
        pltpu.VMEM((heads * rows, 2 * head_dim), jnp.float32),
    ]


def attention_cost(rows, keys, head_dim, heads):
    return pl.CostEstimate(
        flops=4 * rows * keys * head_dim * heads,
        bytes_accessed=4 * 1024 * 1024,
        transcendentals=rows * keys * heads,
    )


def project_kernel(peers, heads, me_ref, turn_ref, span_live_ref, *refs):
    parts = refs[: 2 * peers - 1]
    weight_ref, away_ref, keep_ref, att_ref, sorted_ref = refs[2 * peers - 1 :]
    rows, features = att_ref.shape
    head_dim = features // heads
    me = me_ref[0]
    logs = []
    for index, part in enumerate(parts):
        pieces = part[rows:, :].astype(jnp.float32)[:heads]
        log = pieces[:, :rows] + pieces[:, rows : 2 * rows] + pieces[:, 2 * rows : 3 * rows]
        if index:
            away = (index + 1) // 2
            valid = me >= away if index % 2 else me + away < peers
            log = jnp.where(valid, log, LOW)
        logs.append(log)
    top = functools.reduce(jnp.maximum, logs)
    weights = [jnp.exp2(log - top) for log in logs]
    inverse = 1.0 / functools.reduce(jnp.add, weights)
    row = lax.broadcasted_iota(jnp.int32, (heads, rows), 1)
    inverse = jnp.where(row < span_live_ref[0], inverse, 0.0)
    weights = [(weight * inverse).T for weight in weights]
    for g in range(heads):
        at = slice(g * head_dim, (g + 1) * head_dim)
        total = jnp.zeros((rows, head_dim), jnp.float32)
        for part, weight in zip(parts, weights):
            total += part[:rows, at].astype(jnp.float32) * weight[:, g : g + 1]
        att_ref[:, at] = total.astype(jnp.bfloat16)

    chips = keep_ref.shape[0]
    block = keep_ref.shape[1]
    chip, core = turn_ref[0] // 2, lax.rem(turn_ref[0], 2)
    for side, wanted in enumerate((1 - core, core)):
        for k in range(chips):
            owner = 2 * lax.rem(chip + k, chips) + wanted
            at = (side * chips + k) * block
            sorted_ref[at : at + block, :] = att_ref[
                pl.ds(pl.multiple_of(owner * block, block), block), :
            ]
    width = 512
    for i in range(weight_ref.shape[1] // width):
        at = slice(i * width, (i + 1) * width)
        product = jnp.dot(
            sorted_ref[...], weight_ref[:, at], preferred_element_type=jnp.float32
        ).astype(jnp.bfloat16)
        for k in range(chips):
            away_ref[k, :, at] = product[k * block : (k + 1) * block]
            keep_ref[k, :, at] = product[(chips + k) * block : (chips + k + 1) * block]


def project(me, turn, span_live, parts, out_weight, peers, heads, members):
    features, outputs = out_weight.shape
    rows = parts[0].shape[0] - 16
    block_shape = jax.ShapeDtypeStruct((members // 2, rows // members, outputs), jnp.bfloat16)
    return pl.pallas_call(
        functools.partial(project_kernel, peers, heads),
        out_shape=(block_shape, block_shape),
        in_specs=[SMEM, SMEM, SMEM] + [VMEM] * (len(parts) + 1),
        out_specs=(VMEM, VMEM),
        scratch_shapes=[
            pltpu.VMEM((rows, features), jnp.bfloat16),
            pltpu.VMEM((rows, features), jnp.bfloat16),
        ],
        compiler_params=pltpu.CompilerParams(vmem_limit_bytes=VMEM_LIMIT),
        cost_estimate=pl.CostEstimate(
            flops=2 * rows * features * outputs,
            bytes_accessed=2 * (features + rows) * outputs,
            transcendentals=0,
        ),
        name="project",
    )(me, turn, span_live, *parts, out_weight)


def add_kernel(kept_ref, come_ref, *out_refs):
    for k, out_ref in enumerate(out_refs):
        out_ref[...] = (
            kept_ref[k + 1].astype(jnp.float32) + come_ref[k + 1].astype(jnp.float32)
        ).astype(jnp.bfloat16)


def total_kernel(kept_ref, come_ref, *refs):
    total = kept_ref[0].astype(jnp.float32) + come_ref[0].astype(jnp.float32)
    for ref in refs[:-1]:
        total += ref[...].astype(jnp.float32)
    refs[-1][...] = total.astype(jnp.bfloat16)


def scatter_sum(away, keep, members):
    chips, block, outputs = keep.shape
    shape = jax.ShapeDtypeStruct((block, outputs), jnp.bfloat16)
    params = pltpu.CompilerParams(vmem_limit_bytes=VMEM_LIMIT)
    come = lax.ppermute(away, "tp", [(i, i ^ 1) for i in range(members)])
    sums = pl.pallas_call(
        add_kernel,
        out_shape=[shape] * (chips - 1),
        in_specs=[VMEM, VMEM],
        out_specs=[VMEM] * (chips - 1),
        compiler_params=params,
        name="add_cores",
    )(keep, come)
    arrived = [
        lax.ppermute(each, "tp", [(i, (i + 2 * (k + 1)) % members) for i in range(members)])
        for k, each in enumerate(sums)
    ]
    return pl.pallas_call(
        total_kernel,
        out_shape=shape,
        in_specs=[VMEM] * (2 + len(arrived)),
        out_specs=VMEM,
        compiler_params=params,
        name="add_chips",
    )(keep, come, *arrived)


def pack_kernel(span_live_ref, owners_ref, span_ref, out_ref, counts_ref):
    peers = out_ref.shape[1]
    block_rows, head_dim = out_ref.shape[3:]
    out_ref[...] = jnp.zeros_like(out_ref)
    for k in range(peers):
        counts_ref[k] = 0
    row = lax.broadcasted_iota(jnp.int32, (block_rows, head_dim), 0)
    for b in range(span_ref.shape[1] // block_rows):
        owner = owners_ref[b]
        rank = counts_ref[owner]
        counts_ref[owner] = rank + 1
        keep = row + b * block_rows < span_live_ref[0]
        for side in range(2):
            block = span_ref[side, b * block_rows : (b + 1) * block_rows, :]
            out_ref[side, owner, rank] = jnp.where(keep, block, jnp.zeros_like(block))


def shards(
    queries,
    cache_store,
    span_cache,
    out_weight,
    prefix_blocks,
    span_lengths,
    hit_holders,
    hit_slots,
    store_owners,
):
    peers = lax.axis_size("inst")
    block_rows, head_dim = cache_store.shape[2:]
    rows, columns = queries.shape
    heads = columns // head_dim
    block_max = hit_slots.shape[1]
    cap = max(2, block_max * 5 // (4 * peers))
    new_count = rows // block_rows
    push_cap = max(2, 2 * new_count // peers)
    scale = math.log2(math.e) / math.sqrt(head_dim)
    me = lax.axis_index("inst").reshape(1)
    width = round_up(cap + 1, 128)
    part_shape = jax.ShapeDtypeStruct((rows + 16, columns), jnp.bfloat16)
    scratch = attention_scratch(heads, rows, head_dim, block_rows)
    params = pltpu.CompilerParams(vmem_limit_bytes=VMEM_LIMIT)

    def shift(value, by):
        pairs = [(i, i + by) for i in range(peers) if 0 <= i + by < peers]
        return lax.ppermute(value, "inst", pairs)

    lists, loaded = route(
        prefix_blocks, hit_holders.reshape(1, -1), hit_slots, queries, peers, width
    )
    from_left, from_right = shift(loaded, 1), shift(loaded, -1)
    own = pl.pallas_call(
        functools.partial(own_kernel, scale),
        out_shape=part_shape,
        in_specs=[SMEM, SMEM, SMEM, HBM, HBM, HBM],
        out_specs=VMEM,
        scratch_shapes=[
            pltpu.VMEM(queries.shape, jnp.bfloat16),
            pltpu.VMEM(cache_store.shape, jnp.bfloat16),
            pltpu.VMEM(span_cache.shape, jnp.bfloat16),
            pltpu.SemaphoreType.DMA((3,)),
            *scratch,
        ],
        compiler_params=params,
        cost_estimate=attention_cost(rows, 8 * rows, head_dim, heads),
        name="own_attention",
    )(me, span_lengths, lists, queries, cache_store, span_cache)

    parts, after = [own], own
    for away in range(1, peers):
        guests = (from_left, from_right)
        if away + 1 < peers:
            from_left, from_right, after = lax.optimization_barrier((*guests, after))
            from_left, from_right = shift(from_left, 1), shift(from_right, -1)
        part_a, part_b = pl.pallas_call(
            functools.partial(guest_kernel, scale, width, rows),
            out_shape=(part_shape, part_shape),
            in_specs=[SMEM, VMEM, VMEM, VMEM, pl.BlockSpec(memory_space=pl.ANY)],
            out_specs=(VMEM, VMEM),
            scratch_shapes=[
                pltpu.VMEM((2, width), jnp.int32),
                pltpu.SMEM((2, width), jnp.int32),
                pltpu.SemaphoreType.DMA,
                *scratch,
            ],
            compiler_params=params,
            cost_estimate=attention_cost(rows, 8 * rows, head_dim, heads),
            name="guest_attention",
        )(me, *guests, cache_store, after)
        after = part_a
        parts.append(shift(part_b, away))
        parts.append(shift(part_a, -away))

    members = lax.axis_size("tp")
    turn = lax.axis_index("tp").reshape(1)
    away, keep = project(
        me, turn, span_lengths, parts, out_weight, peers, heads, members
    )
    projected = scatter_sum(away, keep, members)

    outgoing = pl.pallas_call(
        pack_kernel,
        out_shape=jax.ShapeDtypeStruct(
            (2, peers, push_cap, block_rows, head_dim), jnp.bfloat16
        ),
        in_specs=[SMEM, SMEM, VMEM],
        out_specs=VMEM,
        scratch_shapes=[pltpu.SMEM((peers,), jnp.int32)],
        compiler_params=pltpu.CompilerParams(vmem_limit_bytes=VMEM_LIMIT),
        name="pack_blocks",
    )(span_lengths, store_owners.reshape(-1), span_cache)
    incoming = lax.all_to_all(outgoing, "inst", split_axis=1, concat_axis=1, tiled=True)
    pushed_blocks = incoming.reshape(2, peers * push_cap, block_rows, head_dim)
    return (projected, pushed_blocks)


def solution(mesh):
    return jax.shard_map(
        shards,
        mesh=mesh,
        in_specs=(
            P(("pods", "inst"), "tp"),
            P(None, ("pods", "inst"), None, "tp"),
            P(None, ("pods", "inst"), "tp"),
            P("tp", None),
            P(("pods", "inst")),
            P(("pods", "inst")),
            P(("pods", "inst"), None, None),
            P(("pods", "inst"), None),
            P(("pods", "inst"), None, None),
        ),
        out_specs=(P(("pods", "inst", "tp"), None), P(None, ("pods", "inst"), None, "tp")),
        check_vma=False,
    )
```

```python
import functools
import math

import jax
import jax.numpy as jnp
from jax import lax
from jax.experimental import pallas as pl
from jax.experimental.pallas import tpu as pltpu
from jax.sharding import PartitionSpec as P

LOW = -1e30
TOP = 2.0**100
TILE = 16
STACK = 4
VMEM_LIMIT = 20 * 1024 * 1024

SMEM = pl.BlockSpec(memory_space=pltpu.SMEM)
VMEM = pl.BlockSpec(memory_space=pltpu.VMEM)
HBM = pl.BlockSpec(memory_space=pltpu.HBM)


def round_up(number, step):
    return -(-number // step) * step


def route_kernel(
    live_ref, holders_in, slots_in, q_in, lists_ref, out_ref, holders_ref, slots_ref, all_ref, sems
):
    rows, columns = q_in.shape
    loading = [
        pltpu.make_async_copy(holders_in, holders_ref, sems.at[0]),
        pltpu.make_async_copy(slots_in, slots_ref, sems.at[1]),
    ]
    passing = pltpu.make_async_copy(q_in, all_ref.at[pl.ds(0, rows)], sems.at[2])
    for copy in loading:
        copy.start()
    passing.start()
    for copy in loading:
        copy.wait()
    peers, width = lists_ref.shape
    number = holders_ref.shape[1]
    padded = round_up(peers, 16)
    holder = lax.broadcasted_iota(jnp.int32, (padded, number), 0)
    entry = lax.broadcasted_iota(jnp.int32, (padded, number), 1)
    hot = (holders_ref[...] == holder) & (entry < live_ref[0])
    ones = jnp.where(hot, 1.0, 0.0)
    earlier = lax.broadcasted_iota(jnp.int32, (number, number), 0) < lax.broadcasted_iota(
        jnp.int32, (number, number), 1
    )
    ranks = jnp.dot(
        ones.astype(jnp.bfloat16),
        jnp.where(earlier, 1.0, 0.0).astype(jnp.bfloat16),
        preferred_element_type=jnp.float32,
    )
    rank = jnp.sum(ranks * ones, axis=0, keepdims=True)
    rank = jnp.broadcast_to(rank, (8, number)).T[:, :1].astype(jnp.int32)
    place = lax.broadcasted_iota(jnp.int32, (number, width), 1) == rank
    slots = jnp.where(hot, slots_ref[...], 0).astype(jnp.float32)
    lists = jnp.dot(
        slots.astype(jnp.bfloat16),
        jnp.where(place, 1.0, 0.0).astype(jnp.bfloat16),
        preferred_element_type=jnp.float32,
    )
    counts = jnp.sum(ones, axis=1, keepdims=True)
    last = lax.broadcasted_iota(jnp.int32, (padded, width), 1) == width - 1
    lists = jnp.where(last, counts, lists)[:peers]
    lists_ref[...] = lists.astype(jnp.int32)

    each = columns // width
    riders = all_ref.shape[0] - rows
    row = lax.broadcasted_iota(jnp.int32, (riders, columns), 0)
    tail = jnp.zeros((riders, columns), jnp.float32)
    for r in range(-(-peers // each)):
        line = [lists[h : h + 1] for h in range(r * each, min(peers, (r + 1) * each))]
        line += [jnp.zeros((1, width), jnp.float32)] * (each - len(line))
        tail = jnp.where(row == r, jnp.concatenate(line, axis=1), tail)
    all_ref[rows:, :] = tail.astype(jnp.bfloat16)
    passing.wait()
    leaving = pltpu.make_async_copy(all_ref, out_ref, sems.at[3])
    leaving.start()
    leaving.wait()


def route(live, holders, slots, queries, peers, width):
    rows, columns = queries.shape
    riders = round_up(-(-peers // (columns // width)), 16)
    return pl.pallas_call(
        route_kernel,
        out_shape=(
            jax.ShapeDtypeStruct((peers, width), jnp.int32),
            jax.ShapeDtypeStruct((rows + riders, columns), jnp.bfloat16),
        ),
        in_specs=[SMEM, HBM, HBM, HBM],
        out_specs=(VMEM, HBM),
        scratch_shapes=[
            pltpu.VMEM(holders.shape, jnp.int32),
            pltpu.VMEM(slots.shape, jnp.int32),
            pltpu.VMEM((rows + riders, columns), jnp.bfloat16),
            pltpu.SemaphoreType.DMA((4,)),
        ],
        compiler_params=pltpu.CompilerParams(vmem_limit_bytes=62 * 1024 * 1024),
        name="route",
    )(live, holders, slots, queries)


def score(q, keys):
    return lax.dot_general(q, keys, (((1,), (1,)), ((), ())), preferred_element_type=jnp.float32)


def twice(value):
    return jnp.concatenate([value, value], axis=1)


def attend(
    slot, count, store_ref, span_ref, span_live, q_ref, k_ref, v_ref, s_ref, ref_ref, acc_ref, rows,
    scale, stored=None,
):
    block_rows, head_dim = store_ref.shape[2:]
    heads = q_ref.shape[0] // rows
    stack = rows * math.gcd(heads, STACK)
    stacks = q_ref.shape[0] // stack
    tiles = (count + TILE - 1) // TILE

    def fetch(tile, into):
        for j in range(TILE):
            index = tile * TILE + j
            here = slot(jnp.maximum(jnp.minimum(index, count - 1), 0))
            at = slice(j * block_rows, (j + 1) * block_rows)
            k_ref[into, at, :] = store_ref[0, here]
            block = store_ref[1, here]
            v_ref[into, at, :head_dim] = jnp.where(index < count, block, jnp.zeros_like(block))
            v_ref[into, at, head_dim:] = jnp.where(
                index < count, jnp.ones_like(block), jnp.zeros_like(block)
            )

    def start():
        if span_ref is None:
            acc_ref[...] = jnp.zeros_like(acc_ref)
            return
        keys = span_ref.shape[1]
        key = lax.broadcasted_iota(jnp.int32, (rows, keys), 1)
        row = lax.broadcasted_iota(jnp.int32, (rows, keys), 0)
        mask = (key <= row) & (key < span_live)
        values = jnp.concatenate(
            [span_ref[1], jnp.ones((keys, head_dim), jnp.bfloat16)], axis=1
        )
        s = score(q_ref[:rows, :], span_ref[0])
        for g in range(heads):
            at = slice(g * rows, (g + 1) * rows)
            if g + 1 < heads:
                following = score(q_ref[(g + 1) * rows : (g + 2) * rows, :], span_ref[0])
            s = jnp.where(mask, s, LOW)
            top = jnp.max(s, axis=1, keepdims=True)
            ref_ref[at, :] = jnp.broadcast_to(top, (rows, head_dim))
            p = jnp.exp2((s - top) * scale).astype(jnp.bfloat16)
            acc_ref[at, :] = jnp.dot(p, values, preferred_element_type=jnp.float32)
            s = following

    start()
    if stored is not None:
        stored()

    @pl.when(count > 0)
    def _():
        fetch(0, 0)
        if span_ref is None:
            few = score(q_ref[...], k_ref[0, : 8 * block_rows, :])
            ref_ref[...] = jnp.broadcast_to(
                jnp.max(few, axis=1, keepdims=True), ref_ref.shape
            )
        s_ref[...] = score(q_ref[:stack, :], k_ref[0])

        def step(tile, carry):
            now = lax.rem(tile, 2)
            later = 1 - now
            keys, values = k_ref[now], v_ref[now]
            s = s_ref[...]
            fetch(tile + 1, later)
            for c in range(stacks):
                at = slice(c * stack, (c + 1) * stack)
                if c + 1 < stacks:
                    following = score(q_ref[(c + 1) * stack : (c + 2) * stack, :], keys)
                else:
                    s_ref[...] = score(q_ref[:stack, :], k_ref[later])
                p = jnp.exp2((s - twice(ref_ref[at, :])) * scale).astype(jnp.bfloat16)
                acc_ref[at, :] += jnp.dot(p, values, preferred_element_type=jnp.float32)
                s = following
            return carry

        lax.fori_loop(0, tiles, step, 0)
        beyond = jnp.max(jnp.where(acc_ref[:, head_dim:] < TOP, 0.0, 1.0))

        @pl.when(beyond > 0.0)
        def _():
            start()
            if span_ref is None:
                ref_ref[...] = jnp.full_like(ref_ref, LOW)

            def careful(tile, carry):
                fetch(tile, 0)

                def head(g, inner):
                    at = pl.ds(pl.multiple_of(g * rows, rows), rows)
                    s = score(q_ref[at, :], k_ref[0])
                    old = ref_ref[at, :]
                    new = jnp.maximum(old, jnp.max(s, axis=1, keepdims=True))
                    p = jnp.exp2((s - twice(new)) * scale).astype(jnp.bfloat16)
                    update = jnp.dot(p, v_ref[0], preferred_element_type=jnp.float32)
                    acc_ref[at, :] = (
                        acc_ref[at, :] * twice(jnp.exp2((old - new) * scale)) + update
                    )
                    ref_ref[at, :] = new
                    return inner

                return lax.fori_loop(0, heads, head, carry)

            lax.fori_loop(0, tiles, careful, 0)


def stack_heads(queries_ref, q_ref, rows):
    head_dim = q_ref.shape[1]
    for g in range(q_ref.shape[0] // rows):
        q_ref[g * rows : (g + 1) * rows, :] = queries_ref[
            :rows, g * head_dim : (g + 1) * head_dim
        ]


def write_logs(out_ref, logs):
    heads, rows = logs.shape
    first = logs.astype(jnp.bfloat16).astype(jnp.float32)
    rest = logs - first
    second = rest.astype(jnp.bfloat16).astype(jnp.float32)
    third = rest - second
    spare = jnp.zeros((heads, out_ref.shape[1] - 3 * rows), jnp.float32)
    line = jnp.concatenate([first, second, third, spare], axis=1)
    padding = jnp.zeros((16 - heads, out_ref.shape[1]), jnp.float32)
    out_ref[rows:, :] = jnp.concatenate([line, padding], axis=0).astype(jnp.bfloat16)


def finish(out_ref, ref_ref, acc_ref, rows, scale):
    head_dim = ref_ref.shape[1]
    heads = ref_ref.shape[0] // rows
    lane = lax.broadcasted_iota(jnp.int32, (rows, head_dim), 1)
    logs = jnp.zeros((rows, head_dim), jnp.float32)
    for g in range(heads):
        at = slice(g * rows, (g + 1) * rows)
        total = acc_ref[at, head_dim:]
        out_ref[:rows, g * head_dim : (g + 1) * head_dim] = (
            acc_ref[at, :head_dim] / total
        ).astype(jnp.bfloat16)
        logs = jnp.where(lane == g, ref_ref[at, :] * scale + jnp.log2(total), logs)
    write_logs(out_ref, logs.T[:heads])


def own_kernel(
    scale, me_ref, span_live_ref, lists_ref, queries_in, store_in, span_in, out_ref,
    queries_ref, store_ref, span_ref, sems, q_ref, k_ref, v_ref, s_ref, ref_ref, acc_ref,
):
    me = me_ref[0]
    rows = queries_ref.shape[0]
    copies = [
        pltpu.make_async_copy(source, target, sems.at[i])
        for i, (source, target) in enumerate(
            ((queries_in, queries_ref), (span_in, span_ref), (store_in, store_ref))
        )
    ]
    for copy in copies:
        copy.start()
    copies[0].wait()
    stack_heads(queries_ref, q_ref, rows)
    copies[1].wait()
    attend(
        lambda index: lists_ref[me, index], lists_ref[me, lists_ref.shape[1] - 1], store_ref,
        span_ref, span_live_ref[0], q_ref, k_ref, v_ref, s_ref, ref_ref, acc_ref, rows, scale,
        copies[2].wait,
    )
    finish(out_ref, ref_ref, acc_ref, rows, scale)


def guest_kernel(
    scale, width, rows, me_ref, a_ref, b_ref, store_ref, after_ref, out_a_ref, out_b_ref,
    wide_ref, list_ref, sem_ref, q_ref, k_ref, v_ref, s_ref, ref_ref, acc_ref,
):
    each = a_ref.shape[1] // width
    me = me_ref[0]
    lane = pl.multiple_of(lax.rem(me, each) * width, 128)
    for which, loaded_ref in enumerate((a_ref, b_ref)):
        riders = loaded_ref[rows:, pl.ds(lane, width)].astype(jnp.float32)
        row = lax.broadcasted_iota(jnp.int32, riders.shape, 0)
        mine = jnp.sum(jnp.where(row == me // each, riders, 0.0), axis=0, keepdims=True)
        wide_ref[which : which + 1, :] = mine.astype(jnp.int32)
    copy = pltpu.make_async_copy(wide_ref, list_ref, sem_ref)
    copy.start()
    stack_heads(a_ref, q_ref, rows)
    copy.wait()
    for which, (loaded_ref, out_ref) in enumerate(((a_ref, out_a_ref), (b_ref, out_b_ref))):
        count = list_ref[which, width - 1]

        @pl.when(count > 0)
        def _():
            if which:
                stack_heads(loaded_ref, q_ref, rows)
            attend(
                lambda index: list_ref[which, index], count, store_ref, None, None,
                q_ref, k_ref, v_ref, s_ref, ref_ref, acc_ref, rows, scale,
            )
            finish(out_ref, ref_ref, acc_ref, rows, scale)

        @pl.when(count == 0)
        def _():
            out_ref[...] = jnp.zeros_like(out_ref)
            write_logs(out_ref, jnp.full((q_ref.shape[0] // rows, rows), LOW, jnp.float32))


def attention_scratch(heads, rows, head_dim, block_rows):
    keys = TILE * block_rows
    return [
        pltpu.VMEM((heads * rows, head_dim), jnp.bfloat16),
        pltpu.VMEM((2, keys, head_dim), jnp.bfloat16),
        pltpu.VMEM((2, keys, 2 * head_dim), jnp.bfloat16),
        pltpu.VMEM((rows * math.gcd(heads, STACK), keys), jnp.float32),
        pltpu.VMEM((heads * rows, head_dim), jnp.float32),
        pltpu.VMEM((heads * rows, 2 * head_dim), jnp.float32),
    ]


def attention_cost(rows, keys, head_dim, heads):
    return pl.CostEstimate(
        flops=4 * rows * keys * head_dim * heads,
        bytes_accessed=4 * 1024 * 1024,
        transcendentals=rows * keys * heads,
    )


def project_kernel(peers, heads, me_ref, turn_ref, span_live_ref, *refs):
    parts = refs[: 2 * peers - 1]
    weight_ref, away_ref, keep_ref, att_ref, sorted_ref = refs[2 * peers - 1 :]
    rows, features = att_ref.shape
    head_dim = features // heads
    me = me_ref[0]
    logs = []
    for index, part in enumerate(parts):
        pieces = part[rows:, :].astype(jnp.float32)[:heads]
        log = pieces[:, :rows] + pieces[:, rows : 2 * rows] + pieces[:, 2 * rows : 3 * rows]
        if index:
            away = (index + 1) // 2
            valid = me >= away if index % 2 else me + away < peers
            log = jnp.where(valid, log, LOW)
        logs.append(log)
    top = functools.reduce(jnp.maximum, logs)
    weights = [jnp.exp2(log - top) for log in logs]
    inverse = 1.0 / functools.reduce(jnp.add, weights)
    row = lax.broadcasted_iota(jnp.int32, (heads, rows), 1)
    inverse = jnp.where(row < span_live_ref[0], inverse, 0.0)
    weights = [(weight * inverse).T for weight in weights]
    for g in range(heads):
        at = slice(g * head_dim, (g + 1) * head_dim)
        total = jnp.zeros((rows, head_dim), jnp.float32)
        for part, weight in zip(parts, weights):
            total += part[:rows, at].astype(jnp.float32) * weight[:, g : g + 1]
        att_ref[:, at] = total.astype(jnp.bfloat16)

    chips = keep_ref.shape[0]
    block = keep_ref.shape[1]
    chip, core = turn_ref[0] // 2, lax.rem(turn_ref[0], 2)
    for side, wanted in enumerate((1 - core, core)):
        for k in range(chips):
            owner = 2 * lax.rem(chip + k, chips) + wanted
            at = (side * chips + k) * block
            sorted_ref[at : at + block, :] = att_ref[
                pl.ds(pl.multiple_of(owner * block, block), block), :
            ]
    width = 512
    for i in range(weight_ref.shape[1] // width):
        at = slice(i * width, (i + 1) * width)
        product = jnp.dot(
            sorted_ref[...], weight_ref[:, at], preferred_element_type=jnp.float32
        ).astype(jnp.bfloat16)
        for k in range(chips):
            away_ref[k, :, at] = product[k * block : (k + 1) * block]
            keep_ref[k, :, at] = product[(chips + k) * block : (chips + k + 1) * block]


def project(me, turn, span_live, parts, out_weight, peers, heads, members):
    features, outputs = out_weight.shape
    rows = parts[0].shape[0] - 16
    block_shape = jax.ShapeDtypeStruct((members // 2, rows // members, outputs), jnp.bfloat16)
    return pl.pallas_call(
        functools.partial(project_kernel, peers, heads),
        out_shape=(block_shape, block_shape),
        in_specs=[SMEM, SMEM, SMEM] + [VMEM] * (len(parts) + 1),
        out_specs=(VMEM, VMEM),
        scratch_shapes=[
            pltpu.VMEM((rows, features), jnp.bfloat16),
            pltpu.VMEM((rows, features), jnp.bfloat16),
        ],
        compiler_params=pltpu.CompilerParams(vmem_limit_bytes=VMEM_LIMIT + len(parts) * 1024 * 1024),
        cost_estimate=pl.CostEstimate(
            flops=2 * rows * features * outputs,
            bytes_accessed=2 * (features + rows) * outputs,
            transcendentals=0,
        ),
        name="project",
    )(me, turn, span_live, *parts, out_weight)


def add_kernel(kept_ref, come_ref, *out_refs):
    for k, out_ref in enumerate(out_refs):
        out_ref[...] = (
            kept_ref[k + 1].astype(jnp.float32) + come_ref[k + 1].astype(jnp.float32)
        ).astype(jnp.bfloat16)


def total_kernel(kept_ref, come_ref, *refs):
    total = kept_ref[0].astype(jnp.float32) + come_ref[0].astype(jnp.float32)
    for ref in refs[:-1]:
        total += ref[...].astype(jnp.float32)
    refs[-1][...] = total.astype(jnp.bfloat16)


def scatter_sum(away, keep, members):
    chips, block, outputs = keep.shape
    shape = jax.ShapeDtypeStruct((block, outputs), jnp.bfloat16)
    params = pltpu.CompilerParams(vmem_limit_bytes=VMEM_LIMIT)
    come = lax.ppermute(away, "tp", [(i, i ^ 1) for i in range(members)])
    sums = pl.pallas_call(
        add_kernel,
        out_shape=[shape] * (chips - 1),
        in_specs=[VMEM, VMEM],
        out_specs=[VMEM] * (chips - 1),
        compiler_params=params,
        name="add_cores",
    )(keep, come)
    arrived = [
        lax.ppermute(each, "tp", [(i, (i + 2 * (k + 1)) % members) for i in range(members)])
        for k, each in enumerate(sums)
    ]
    return pl.pallas_call(
        total_kernel,
        out_shape=shape,
        in_specs=[VMEM] * (2 + len(arrived)),
        out_specs=VMEM,
        compiler_params=params,
        name="add_chips",
    )(keep, come, *arrived)


def pack_kernel(span_live_ref, owners_ref, span_ref, out_ref, counts_ref):
    peers = out_ref.shape[1]
    block_rows, head_dim = out_ref.shape[3:]
    out_ref[...] = jnp.zeros_like(out_ref)
    for k in range(peers):
        counts_ref[k] = 0
    row = lax.broadcasted_iota(jnp.int32, (block_rows, head_dim), 0)
    for b in range(span_ref.shape[1] // block_rows):
        owner = owners_ref[b]
        rank = counts_ref[owner]
        counts_ref[owner] = rank + 1
        keep = row + b * block_rows < span_live_ref[0]
        for side in range(2):
            block = span_ref[side, b * block_rows : (b + 1) * block_rows, :]
            out_ref[side, owner, rank] = jnp.where(keep, block, jnp.zeros_like(block))


def shards(
    queries,
    cache_store,
    span_cache,
    out_weight,
    prefix_blocks,
    span_lengths,
    hit_holders,
    hit_slots,
    store_owners,
):
    peers = lax.axis_size("inst")
    block_rows, head_dim = cache_store.shape[2:]
    rows, columns = queries.shape
    heads = columns // head_dim
    block_max = hit_slots.shape[1]
    cap = max(2, block_max * 5 // (4 * peers))
    new_count = rows // block_rows
    push_cap = max(2, 2 * new_count // peers)
    scale = math.log2(math.e) / math.sqrt(head_dim)
    me = lax.axis_index("inst").reshape(1)
    width = round_up(cap + 1, 128)
    part_shape = jax.ShapeDtypeStruct((rows + 16, columns), jnp.bfloat16)
    scratch = attention_scratch(heads, rows, head_dim, block_rows)
    params = pltpu.CompilerParams(vmem_limit_bytes=VMEM_LIMIT)

    def shift(value, by):
        pairs = [(i, i + by) for i in range(peers) if 0 <= i + by < peers]
        return lax.ppermute(value, "inst", pairs)

    lists, loaded = route(
        prefix_blocks, hit_holders.reshape(1, -1), hit_slots, queries, peers, width
    )
    from_left = [shift(loaded, away) for away in range(1, peers)]
    from_right = [shift(loaded, -away) for away in range(1, peers)]

    own = pl.pallas_call(
        functools.partial(own_kernel, scale),
        out_shape=part_shape,
        in_specs=[SMEM, SMEM, SMEM, HBM, HBM, HBM],
        out_specs=VMEM,
        scratch_shapes=[
            pltpu.VMEM(queries.shape, jnp.bfloat16),
            pltpu.VMEM(cache_store.shape, jnp.bfloat16),
            pltpu.VMEM(span_cache.shape, jnp.bfloat16),
            pltpu.SemaphoreType.DMA((3,)),
            *scratch,
        ],
        compiler_params=params,
        cost_estimate=attention_cost(rows, 8 * rows, head_dim, heads),
        name="own_attention",
    )(me, span_lengths, lists, queries, cache_store, span_cache)
    parts, after = [own], own
    for away in range(1, peers):
        guests = from_left[away - 1], from_right[away - 1]
        if away > 2:
            *parts[-4:-2], after = lax.optimization_barrier((*parts[-4:-2], after))
        part_a, part_b = pl.pallas_call(
            functools.partial(guest_kernel, scale, width, rows),
            out_shape=(part_shape, part_shape),
            in_specs=[SMEM, VMEM, VMEM, VMEM, pl.BlockSpec(memory_space=pl.ANY)],
            out_specs=(VMEM, VMEM),
            scratch_shapes=[
                pltpu.VMEM((2, width), jnp.int32),
                pltpu.SMEM((2, width), jnp.int32),
                pltpu.SemaphoreType.DMA,
                *scratch,
            ],
            compiler_params=params,
            cost_estimate=attention_cost(rows, 8 * rows, head_dim, heads),
            name="guest_attention",
        )(me, *guests, cache_store, after)
        after = part_a
        parts.append(shift(part_b, away))
        parts.append(shift(part_a, -away))

    members = lax.axis_size("tp")
    turn = lax.axis_index("tp").reshape(1)
    away, keep = project(
        me, turn, span_lengths, parts, out_weight, peers, heads, members
    )
    projected = scatter_sum(away, keep, members)

    outgoing = pl.pallas_call(
        pack_kernel,
        out_shape=jax.ShapeDtypeStruct(
            (2, peers, push_cap, block_rows, head_dim), jnp.bfloat16
        ),
        in_specs=[SMEM, SMEM, VMEM],
        out_specs=VMEM,
        scratch_shapes=[pltpu.SMEM((peers,), jnp.int32)],
        compiler_params=pltpu.CompilerParams(vmem_limit_bytes=VMEM_LIMIT),
        name="pack_blocks",
    )(span_lengths, store_owners.reshape(-1), span_cache)
    incoming = lax.all_to_all(outgoing, "inst", split_axis=1, concat_axis=1, tiled=True)
    pushed_blocks = incoming.reshape(2, peers * push_cap, block_rows, head_dim)
    return (projected, pushed_blocks)


def solution(mesh):
    return jax.shard_map(
        shards,
        mesh=mesh,
        in_specs=(
            P(("pods", "inst"), "tp"),
            P(None, ("pods", "inst"), None, "tp"),
            P(None, ("pods", "inst"), "tp"),
            P("tp", None),
            P(("pods", "inst")),
            P(("pods", "inst")),
            P(("pods", "inst"), None, None),
            P(("pods", "inst"), None),
            P(("pods", "inst"), None, None),
        ),
        out_specs=(P(("pods", "inst", "tp"), None), P(None, ("pods", "inst"), None, "tp")),
        check_vma=False,
    )
```

```python
import functools
import math

import jax
import jax.numpy as jnp
from jax import lax
from jax.experimental import pallas as pl
from jax.experimental.pallas import tpu as pltpu
from jax.sharding import PartitionSpec as P

LOW = -1e30
TOP = 2.0**100
TILE = 16
STACK = 512
HALVES = 2
VMEM_LIMIT = 20 * 1024 * 1024

SMEM = pl.BlockSpec(memory_space=pltpu.SMEM)
VMEM = pl.BlockSpec(memory_space=pltpu.VMEM)
HBM = pl.BlockSpec(memory_space=pltpu.HBM)


def round_up(number, step):
    return -(-number // step) * step


def route_kernel(
    live_ref, holders_in, slots_in, q_in, lists_ref, *refs
):
    out_refs, (holders_ref, slots_ref, all_ref, sems) = refs[:HALVES], refs[HALVES:]
    rows = q_in.shape[0]
    columns = all_ref.shape[2]
    loading = [
        pltpu.make_async_copy(holders_in, holders_ref, sems.at[0]),
        pltpu.make_async_copy(slots_in, slots_ref, sems.at[1]),
    ]
    passing = [
        pltpu.make_async_copy(
            q_in.at[:, pl.ds(h * columns, columns)],
            all_ref.at[h, pl.ds(0, rows)],
            sems.at[2 + h],
        )
        for h in range(HALVES)
    ]
    for copy in loading + passing:
        copy.start()
    for copy in loading:
        copy.wait()
    peers, width = lists_ref.shape
    number = holders_ref.shape[1]
    padded = round_up(peers, 16)
    holder = lax.broadcasted_iota(jnp.int32, (padded, number), 0)
    entry = lax.broadcasted_iota(jnp.int32, (padded, number), 1)
    hot = (holders_ref[...] == holder) & (entry < live_ref[0])
    ones = jnp.where(hot, 1.0, 0.0)
    earlier = lax.broadcasted_iota(jnp.int32, (number, number), 0) < lax.broadcasted_iota(
        jnp.int32, (number, number), 1
    )
    ranks = jnp.dot(
        ones.astype(jnp.bfloat16),
        jnp.where(earlier, 1.0, 0.0).astype(jnp.bfloat16),
        preferred_element_type=jnp.float32,
    )
    rank = jnp.sum(ranks * ones, axis=0, keepdims=True)
    rank = jnp.broadcast_to(rank, (8, number)).T[:, :1].astype(jnp.int32)
    place = lax.broadcasted_iota(jnp.int32, (number, width), 1) == rank
    slots = jnp.where(hot, slots_ref[...], 0).astype(jnp.float32)
    lists = jnp.dot(
        slots.astype(jnp.bfloat16),
        jnp.where(place, 1.0, 0.0).astype(jnp.bfloat16),
        preferred_element_type=jnp.float32,
    )
    counts = jnp.sum(ones, axis=1, keepdims=True)
    last = lax.broadcasted_iota(jnp.int32, (padded, width), 1) == width - 1
    lists = jnp.where(last, counts, lists)[:peers]
    lists_ref[...] = lists.astype(jnp.int32)

    each = columns // width
    riders = all_ref.shape[1] - rows
    row = lax.broadcasted_iota(jnp.int32, (riders, columns), 0)
    tail = jnp.zeros((riders, columns), jnp.float32)
    for r in range(-(-peers // each)):
        line = [lists[h : h + 1] for h in range(r * each, min(peers, (r + 1) * each))]
        line += [jnp.zeros((1, width), jnp.float32)] * (each - len(line))
        tail = jnp.where(row == r, jnp.concatenate(line, axis=1), tail)
    leaving = [
        pltpu.make_async_copy(all_ref.at[h], out_refs[h], sems.at[2 + HALVES + h])
        for h in range(HALVES)
    ]
    for h in range(HALVES):
        all_ref[h, rows:, :] = tail.astype(jnp.bfloat16)
        passing[h].wait()
        leaving[h].start()
    for copy in leaving:
        copy.wait()


def route(live, holders, slots, queries, peers, width):
    rows, columns = queries.shape[0], queries.shape[1] // HALVES
    riders = round_up(-(-peers // (columns // width)), 16)
    return pl.pallas_call(
        route_kernel,
        out_shape=(
            jax.ShapeDtypeStruct((peers, width), jnp.int32),
            *[jax.ShapeDtypeStruct((rows + riders, columns), jnp.bfloat16)] * HALVES,
        ),
        in_specs=[SMEM, HBM, HBM, HBM],
        out_specs=(VMEM, *[HBM] * HALVES),
        scratch_shapes=[
            pltpu.VMEM(holders.shape, jnp.int32),
            pltpu.VMEM(slots.shape, jnp.int32),
            pltpu.VMEM((HALVES, rows + riders, columns), jnp.bfloat16),
            pltpu.SemaphoreType.DMA((2 + 2 * HALVES,)),
        ],
        compiler_params=pltpu.CompilerParams(vmem_limit_bytes=62 * 1024 * 1024),
        name="route",
    )(live, holders, slots, queries)


def score(q, keys):
    return lax.dot_general(q, keys, (((1,), (1,)), ((), ())), preferred_element_type=jnp.float32)


def twice(value):
    return jnp.concatenate([value, value], axis=1)


def attend(
    slot, count, store_ref, span_ref, span_live, q_ref, k_ref, v_ref, s_ref, ref_ref, acc_ref, rows,
    scale, stored=None,
):
    block_rows, head_dim = store_ref.shape[2:]
    heads = q_ref.shape[0] // rows
    stack = s_ref.shape[0]
    stacks = q_ref.shape[0] // stack
    tiles = (count + TILE - 1) // TILE

    def fetch(tile, into):
        for j in range(TILE):
            index = tile * TILE + j
            here = slot(jnp.maximum(jnp.minimum(index, count - 1), 0))
            at = slice(j * block_rows, (j + 1) * block_rows)
            k_ref[into, at, :] = store_ref[0, here]
            block = store_ref[1, here]
            v_ref[into, at, :head_dim] = jnp.where(index < count, block, jnp.zeros_like(block))
            v_ref[into, at, head_dim:] = jnp.where(
                index < count, jnp.ones_like(block), jnp.zeros_like(block)
            )

    def start():
        if span_ref is None:
            acc_ref[...] = jnp.zeros_like(acc_ref)
            return
        keys = span_ref.shape[1]
        key = lax.broadcasted_iota(jnp.int32, (rows, keys), 1)
        row = lax.broadcasted_iota(jnp.int32, (rows, keys), 0)
        mask = (key <= row) & (key < span_live)
        values = jnp.concatenate(
            [span_ref[1], jnp.ones((keys, head_dim), jnp.bfloat16)], axis=1
        )
        s = score(q_ref[:rows, :], span_ref[0])
        for g in range(heads):
            at = slice(g * rows, (g + 1) * rows)
            if g + 1 < heads:
                following = score(q_ref[(g + 1) * rows : (g + 2) * rows, :], span_ref[0])
            s = jnp.where(mask, s, LOW)
            top = jnp.max(s, axis=1, keepdims=True)
            ref_ref[at, :] = jnp.broadcast_to(top, (rows, head_dim))
            p = jnp.exp2((s - top) * scale).astype(jnp.bfloat16)
            acc_ref[at, :] = jnp.dot(p, values, preferred_element_type=jnp.float32)
            s = following

    start()
    if stored is not None:
        stored()

    @pl.when(count > 0)
    def _():
        fetch(0, 0)
        if span_ref is None:
            few = score(q_ref[...], k_ref[0, : 8 * block_rows, :])
            ref_ref[...] = jnp.broadcast_to(
                jnp.max(few, axis=1, keepdims=True), ref_ref.shape
            )
        s_ref[...] = score(q_ref[:stack, :], k_ref[0])

        def step(tile, carry):
            now = lax.rem(tile, 2)
            later = 1 - now
            keys, values = k_ref[now], v_ref[now]
            s = s_ref[...]
            fetch(tile + 1, later)
            for c in range(stacks):
                at = slice(c * stack, (c + 1) * stack)
                if c + 1 < stacks:
                    following = score(q_ref[(c + 1) * stack : (c + 2) * stack, :], keys)
                else:
                    s_ref[...] = score(q_ref[:stack, :], k_ref[later])
                p = jnp.exp2((s - twice(ref_ref[at, :])) * scale).astype(jnp.bfloat16)
                acc_ref[at, :] += jnp.dot(p, values, preferred_element_type=jnp.float32)
                s = following
            return carry

        lax.fori_loop(0, tiles, step, 0)
        beyond = jnp.max(jnp.where(acc_ref[:, head_dim:] < TOP, 0.0, 1.0))

        @pl.when(beyond > 0.0)
        def _():
            start()
            if span_ref is None:
                ref_ref[...] = jnp.full_like(ref_ref, LOW)

            def careful(tile, carry):
                fetch(tile, 0)

                def head(g, inner):
                    at = pl.ds(pl.multiple_of(g * rows, rows), rows)
                    s = score(q_ref[at, :], k_ref[0])
                    old = ref_ref[at, :]
                    new = jnp.maximum(old, jnp.max(s, axis=1, keepdims=True))
                    p = jnp.exp2((s - twice(new)) * scale).astype(jnp.bfloat16)
                    update = jnp.dot(p, v_ref[0], preferred_element_type=jnp.float32)
                    acc_ref[at, :] = (
                        acc_ref[at, :] * twice(jnp.exp2((old - new) * scale)) + update
                    )
                    ref_ref[at, :] = new
                    return inner

                return lax.fori_loop(0, heads, head, carry)

            lax.fori_loop(0, tiles, careful, 0)


def stack_heads(queries_ref, q_ref, rows):
    head_dim = q_ref.shape[1]
    for g in range(q_ref.shape[0] // rows):
        q_ref[g * rows : (g + 1) * rows, :] = queries_ref[
            :rows, g * head_dim : (g + 1) * head_dim
        ]


def write_logs(out_ref, logs):
    heads, rows = logs.shape
    first = logs.astype(jnp.bfloat16).astype(jnp.float32)
    rest = logs - first
    second = rest.astype(jnp.bfloat16).astype(jnp.float32)
    third = rest - second
    spare = jnp.zeros((16 - 3 * heads, rows), jnp.float32)
    lines = jnp.concatenate([first, second, third, spare], axis=0)
    if out_ref.shape[1] > rows:
        lines = jnp.concatenate(
            [lines, jnp.zeros((16, out_ref.shape[1] - rows), jnp.float32)], axis=1
        )
    out_ref[rows:, :] = lines.astype(jnp.bfloat16)


def read_logs(part_ref, heads, rows):
    lines = part_ref[rows:, :].astype(jnp.float32)[:, :rows]
    return lines[:heads] + lines[heads : 2 * heads] + lines[2 * heads : 3 * heads]


def finish(out_refs, ref_ref, acc_ref, rows, scale):
    head_dim = ref_ref.shape[1]
    heads = ref_ref.shape[0] // rows // len(out_refs)
    lane = lax.broadcasted_iota(jnp.int32, (rows, head_dim), 1)
    for h, out_ref in enumerate(out_refs):
        logs = jnp.zeros((rows, head_dim), jnp.float32)
        for g in range(heads):
            at = slice((h * heads + g) * rows, (h * heads + g + 1) * rows)
            total = acc_ref[at, head_dim:]
            out_ref[:rows, g * head_dim : (g + 1) * head_dim] = (
                acc_ref[at, :head_dim] / total
            ).astype(jnp.bfloat16)
            logs = jnp.where(lane == g, ref_ref[at, :] * scale + jnp.log2(total), logs)
        write_logs(out_ref, logs.T[:heads])


def own_kernel(
    scale, me_ref, span_live_ref, lists_ref, queries_in, store_in, span_in, after_ref, *refs
):
    out_refs = refs[:HALVES]
    queries_ref, store_ref, span_ref, sems, q_ref, k_ref, v_ref, s_ref, ref_ref, acc_ref = refs[
        HALVES:
    ]
    me = me_ref[0]
    rows = queries_ref.shape[0]
    copies = [
        pltpu.make_async_copy(source, target, sems.at[i])
        for i, (source, target) in enumerate(
            ((queries_in, queries_ref), (span_in, span_ref), (store_in, store_ref))
        )
    ]
    for copy in copies:
        copy.start()
    copies[0].wait()
    stack_heads(queries_ref, q_ref, rows)
    copies[1].wait()
    attend(
        lambda index: lists_ref[me, index], lists_ref[me, lists_ref.shape[1] - 1], store_ref,
        span_ref, span_live_ref[0], q_ref, k_ref, v_ref, s_ref, ref_ref, acc_ref, rows, scale,
        copies[2].wait,
    )
    finish(out_refs, ref_ref, acc_ref, rows, scale)


def guest_kernel(scale, width, rows, number, me_ref, *refs):
    loaded_refs, store_ref = refs[:number], refs[number]
    out_refs = refs[number + 2 : 2 * number + 2]
    wide_ref, list_ref, sem_ref, q_ref, k_ref, v_ref, s_ref, ref_ref, acc_ref = refs[
        2 * number + 2 :
    ]
    each = loaded_refs[0].shape[1] // width
    me = me_ref[0]
    lane = pl.multiple_of(lax.rem(me, each) * width, 128)
    for which, loaded_ref in enumerate(loaded_refs):
        riders = loaded_ref[rows:, pl.ds(lane, width)].astype(jnp.float32)
        row = lax.broadcasted_iota(jnp.int32, riders.shape, 0)
        mine = jnp.sum(jnp.where(row == me // each, riders, 0.0), axis=0, keepdims=True)
        wide_ref[which : which + 1, :] = mine.astype(jnp.int32)
    copy = pltpu.make_async_copy(wide_ref, list_ref, sem_ref)
    copy.start()
    stack_heads(loaded_refs[0], q_ref, rows)
    copy.wait()
    for which, (loaded_ref, out_ref) in enumerate(zip(loaded_refs, out_refs)):
        count = list_ref[which, width - 1]

        @pl.when(count > 0)
        def _():
            if which:
                stack_heads(loaded_ref, q_ref, rows)
            attend(
                lambda index: list_ref[which, index], count, store_ref, None, None,
                q_ref, k_ref, v_ref, s_ref, ref_ref, acc_ref, rows, scale,
            )
            finish([out_ref], ref_ref, acc_ref, rows, scale)

        @pl.when(count == 0)
        def _():
            out_ref[...] = jnp.zeros_like(out_ref)
            write_logs(out_ref, jnp.full((q_ref.shape[0] // rows, rows), LOW, jnp.float32))


def attention_scratch(heads, rows, head_dim, block_rows):
    keys = TILE * block_rows
    return [
        pltpu.VMEM((heads * rows, head_dim), jnp.bfloat16),
        pltpu.VMEM((2, keys, head_dim), jnp.bfloat16),
        pltpu.VMEM((2, keys, 2 * head_dim), jnp.bfloat16),
        pltpu.VMEM((math.gcd(heads * rows, STACK), keys), jnp.float32),
        pltpu.VMEM((heads * rows, head_dim), jnp.float32),
        pltpu.VMEM((heads * rows, 2 * head_dim), jnp.float32),
    ]


def attention_cost(rows, keys, head_dim, heads):
    return pl.CostEstimate(
        flops=4 * rows * keys * head_dim * heads,
        bytes_accessed=4 * 1024 * 1024,
        transcendentals=rows * keys * heads,
    )


def merged(parts, heads, rows):
    logs = [read_logs(part, heads, rows) for part in parts]
    top = functools.reduce(jnp.maximum, logs)
    weights = [jnp.exp2(log - top) for log in logs]
    total = functools.reduce(jnp.add, weights)
    return [weight / total for weight in weights], top + jnp.log2(total)


def weighted(parts, weights, g, head_dim, rows):
    total = jnp.zeros((rows, head_dim), jnp.float32)
    for part, weight in zip(parts, weights):
        part_rows = part[:rows, g * head_dim : (g + 1) * head_dim]
        total += part_rows.astype(jnp.float32) * weight[:, g : g + 1]
    return total.astype(jnp.bfloat16)


def merge_kernel(heads, number, *refs):
    parts, out_ref = refs[:number], refs[number + 1]
    rows = out_ref.shape[0] - 16
    head_dim = out_ref.shape[1] // heads
    weights, logs = merged(parts, heads, rows)
    weights = [weight.T for weight in weights]
    for g in range(heads):
        out_ref[:rows, g * head_dim : (g + 1) * head_dim] = weighted(
            parts, weights, g, head_dim, rows
        )
    write_logs(out_ref, logs)


def project_kernel(heads, number, turn_ref, span_live_ref, *refs):
    parts = refs[: HALVES * number]
    weight_ref, away_ref, keep_ref, att_ref, sorted_ref, held_ref, sems = refs[HALVES * number :]
    rows, features = att_ref.shape
    chunks, _, width = held_ref.shape
    head_dim = features // heads
    copies = [
        pltpu.make_async_copy(weight_ref.at[:, pl.ds(i * width, width)], held_ref.at[i], sems.at[i])
        for i in range(chunks)
    ]
    for copy in copies:
        copy.start()

    some = heads // HALVES
    row = lax.broadcasted_iota(jnp.int32, (some, rows), 1)
    for h in range(HALVES):
        here = parts[h * number : (h + 1) * number]
        weights, _ = merged(here, some, rows)
        weights = [jnp.where(row < span_live_ref[0], weight, 0.0).T for weight in weights]
        for g in range(some):
            at = (h * some + g) * head_dim
            att_ref[:, at : at + head_dim] = weighted(here, weights, g, head_dim, rows)

    chips = keep_ref.shape[0]
    block = keep_ref.shape[1]
    chip, core = turn_ref[0] // 2, lax.rem(turn_ref[0], 2)
    for side, wanted in enumerate((1 - core, core)):
        for k in range(chips):
            owner = 2 * lax.rem(chip + k, chips) + wanted
            at = (side * chips + k) * block
            sorted_ref[at : at + block, :] = att_ref[
                pl.ds(pl.multiple_of(owner * block, block), block), :
            ]
    for i in range(chunks):
        copies[i].wait()
        at = slice(i * width, (i + 1) * width)
        product = jnp.dot(
            sorted_ref[...], held_ref[i], preferred_element_type=jnp.float32
        ).astype(jnp.bfloat16)
        for k in range(chips):
            away_ref[k, :, at] = product[k * block : (k + 1) * block]
            keep_ref[k, :, at] = product[(chips + k) * block : (chips + k + 1) * block]


def project(turn, span_live, parts, out_weight, heads, members):
    features, outputs = out_weight.shape
    rows = parts[0].shape[0] - 16
    width = 512
    chunks = outputs // width
    block_shape = jax.ShapeDtypeStruct((members // 2, rows // members, outputs), jnp.bfloat16)
    return pl.pallas_call(
        functools.partial(project_kernel, heads, len(parts) // HALVES),
        out_shape=(block_shape, block_shape),
        in_specs=[SMEM, SMEM] + [VMEM] * len(parts) + [HBM],
        out_specs=(VMEM, VMEM),
        scratch_shapes=[
            pltpu.VMEM((rows, features), jnp.bfloat16),
            pltpu.VMEM((rows, features), jnp.bfloat16),
            pltpu.VMEM((chunks, features, width), jnp.bfloat16),
            pltpu.SemaphoreType.DMA((chunks,)),
        ],
        compiler_params=pltpu.CompilerParams(vmem_limit_bytes=VMEM_LIMIT + 8 * 1024 * 1024),
        cost_estimate=pl.CostEstimate(
            flops=2 * rows * features * outputs,
            bytes_accessed=2 * (features + rows) * outputs,
            transcendentals=0,
        ),
        name="project",
    )(turn, span_live, *parts, out_weight)


def add_kernel(kept_ref, come_ref, *out_refs):
    for k, out_ref in enumerate(out_refs):
        out_ref[...] = (
            kept_ref[k + 1].astype(jnp.float32) + come_ref[k + 1].astype(jnp.float32)
        ).astype(jnp.bfloat16)


def total_kernel(kept_ref, come_ref, *refs):
    total = kept_ref[0].astype(jnp.float32) + come_ref[0].astype(jnp.float32)
    for ref in refs[:-1]:
        total += ref[...].astype(jnp.float32)
    refs[-1][...] = total.astype(jnp.bfloat16)


def scatter_sum(away, keep, members):
    chips, block, outputs = keep.shape
    shape = jax.ShapeDtypeStruct((block, outputs), jnp.bfloat16)
    params = pltpu.CompilerParams(vmem_limit_bytes=VMEM_LIMIT)
    come = lax.ppermute(away, "tp", [(i, i ^ 1) for i in range(members)])
    sums = pl.pallas_call(
        add_kernel,
        out_shape=[shape] * (chips - 1),
        in_specs=[VMEM, VMEM],
        out_specs=[VMEM] * (chips - 1),
        compiler_params=params,
        name="add_cores",
    )(keep, come)
    arrived = [
        lax.ppermute(each, "tp", [(i, (i + 2 * (k + 1)) % members) for i in range(members)])
        for k, each in enumerate(sums)
    ]
    return pl.pallas_call(
        total_kernel,
        out_shape=shape,
        in_specs=[VMEM] * (2 + len(arrived)),
        out_specs=VMEM,
        compiler_params=params,
        name="add_chips",
    )(keep, come, *arrived)


def pack_kernel(span_live_ref, owners_ref, span_ref, out_ref, counts_ref):
    peers = out_ref.shape[1]
    block_rows, head_dim = out_ref.shape[3:]
    out_ref[...] = jnp.zeros_like(out_ref)
    for k in range(peers):
        counts_ref[k] = 0
    row = lax.broadcasted_iota(jnp.int32, (block_rows, head_dim), 0)
    for b in range(span_ref.shape[1] // block_rows):
        owner = owners_ref[b]
        rank = counts_ref[owner]
        counts_ref[owner] = rank + 1
        keep = row + b * block_rows < span_live_ref[0]
        for side in range(2):
            block = span_ref[side, b * block_rows : (b + 1) * block_rows, :]
            out_ref[side, owner, rank] = jnp.where(keep, block, jnp.zeros_like(block))


def shards(
    queries,
    cache_store,
    span_cache,
    out_weight,
    prefix_blocks,
    span_lengths,
    hit_holders,
    hit_slots,
    store_owners,
):
    peers = lax.axis_size("inst")
    block_rows, head_dim = cache_store.shape[2:]
    rows, columns = queries.shape
    heads = columns // head_dim
    block_max = hit_slots.shape[1]
    cap = max(2, block_max * 5 // (4 * peers))
    new_count = rows // block_rows
    push_cap = max(2, 2 * new_count // peers)
    scale = math.log2(math.e) / math.sqrt(head_dim)
    me = lax.axis_index("inst").reshape(1)
    width = round_up(cap + 1, 128)
    some = heads // HALVES
    part_shape = jax.ShapeDtypeStruct((rows + 16, columns // HALVES), jnp.bfloat16)
    params = pltpu.CompilerParams(vmem_limit_bytes=VMEM_LIMIT)
    anywhere = pl.BlockSpec(memory_space=pl.ANY)

    def exchange(value, bit):
        return lax.ppermute(value, "inst", [(i, i ^ bit) for i in range(peers)])

    order = sorted(range(1, peers), key=lambda k: -(k & -k))

    def spread(loaded):
        held = {0: loaded}
        for k in order:
            held[k] = exchange(held[k & (k - 1)], k & -k)
        return held

    def guests(held, group, after):
        return pl.pallas_call(
            functools.partial(guest_kernel, scale, width, rows, len(group)),
            out_shape=[part_shape] * len(group),
            in_specs=[SMEM] + [VMEM] * (len(group) + 1) + [anywhere],
            out_specs=[VMEM] * len(group),
            scratch_shapes=[
                pltpu.VMEM((len(group), width), jnp.int32),
                pltpu.SMEM((len(group), width), jnp.int32),
                pltpu.SemaphoreType.DMA,
                *attention_scratch(some, rows, head_dim, block_rows),
            ],
            compiler_params=params,
            cost_estimate=attention_cost(rows, 6 * rows * len(group), head_dim, some),
            name="guest_attention",
        )(me, *[held[k] for k in group], cache_store, after)

    def gather_back(parts, after):
        parts = dict(parts)
        for k in reversed(order):
            arrived = [exchange(parts[c], c & -c) for c in order if c & (c - 1) == k]
            if arrived:
                parts[k] = after = pl.pallas_call(
                    functools.partial(merge_kernel, some, len(arrived) + 1),
                    out_shape=part_shape,
                    in_specs=[VMEM] * (len(arrived) + 1) + [anywhere],
                    out_specs=VMEM,
                    compiler_params=params,
                    name="merge",
                )(parts[k], *arrived, after)
        parts[1], after = lax.optimization_barrier((parts[1], after))
        return [exchange(parts[k], k) for k in order if k & (k - 1) == 0], after

    lists, *loaded = route(
        prefix_blocks, hit_holders.reshape(1, -1), hit_slots, queries, peers, width
    )
    groups = [order[i : i + 2] for i in range(0, peers - 1, 2)]
    after, before, arrived = loaded[0], None, []
    for h in range(HALVES):
        held = spread(loaded[h])
        if h + 1 < HALVES:
            loaded[h + 1], held[1] = lax.optimization_barrier((loaded[h + 1], held[1]))
        parts = {}
        for index, group in enumerate(groups):
            results = guests(held, group, after)
            after = results[0]
            parts.update(zip(group, results))
            if index == 0 and before is not None:
                back, after = gather_back(before, after)
                arrived.append(back)
        before = parts
    back, after = gather_back(before, after)
    *arrived[0], after = lax.optimization_barrier((*arrived[0], after))
    arrived.append(back)

    own = pl.pallas_call(
        functools.partial(own_kernel, scale),
        out_shape=[part_shape] * HALVES,
        in_specs=[SMEM, SMEM, SMEM, HBM, HBM, HBM, anywhere],
        out_specs=[VMEM] * HALVES,
        scratch_shapes=[
            pltpu.VMEM(queries.shape, jnp.bfloat16),
            pltpu.VMEM(cache_store.shape, jnp.bfloat16),
            pltpu.VMEM(span_cache.shape, jnp.bfloat16),
            pltpu.SemaphoreType.DMA((3,)),
            *attention_scratch(heads, rows, head_dim, block_rows),
        ],
        compiler_params=params,
        cost_estimate=attention_cost(rows, 8 * rows, head_dim, heads),
        name="own_attention",
    )(me, span_lengths, lists, queries, cache_store, span_cache, after)

    members = lax.axis_size("tp")
    turn = lax.axis_index("tp").reshape(1)
    parts = [part for h in range(HALVES) for part in (own[h], *arrived[h])]
    away, keep = project(turn, span_lengths, parts, out_weight, heads, members)
    projected = scatter_sum(away, keep, members)

    outgoing = pl.pallas_call(
        pack_kernel,
        out_shape=jax.ShapeDtypeStruct(
            (2, peers, push_cap, block_rows, head_dim), jnp.bfloat16
        ),
        in_specs=[SMEM, SMEM, VMEM],
        out_specs=VMEM,
        scratch_shapes=[pltpu.SMEM((peers,), jnp.int32)],
        compiler_params=pltpu.CompilerParams(vmem_limit_bytes=VMEM_LIMIT),
        name="pack_blocks",
    )(span_lengths, store_owners.reshape(-1), span_cache)
    incoming = lax.all_to_all(outgoing, "inst", split_axis=1, concat_axis=1, tiled=True)
    pushed_blocks = incoming.reshape(2, peers * push_cap, block_rows, head_dim)
    return (projected, pushed_blocks)


def solution(mesh):
    return jax.shard_map(
        shards,
        mesh=mesh,
        in_specs=(
            P(("pods", "inst"), "tp"),
            P(None, ("pods", "inst"), None, "tp"),
            P(None, ("pods", "inst"), "tp"),
            P("tp", None),
            P(("pods", "inst")),
            P(("pods", "inst")),
            P(("pods", "inst"), None, None),
            P(("pods", "inst"), None),
            P(("pods", "inst"), None, None),
        ),
        out_specs=(P(("pods", "inst", "tp"), None), P(None, ("pods", "inst"), None, "tp")),
        check_vma=False,
    )
```

```python
import functools
import math

import jax
import jax.numpy as jnp
from jax import lax
from jax.experimental import pallas as pl
from jax.experimental.pallas import tpu as pltpu
from jax.sharding import PartitionSpec as P

LOW = -1e30
TOP = 2.0**100
TILE = 16
STACK = 512
HALVES = 2
VMEM_LIMIT = 20 * 1024 * 1024

SMEM = pl.BlockSpec(memory_space=pltpu.SMEM)
VMEM = pl.BlockSpec(memory_space=pltpu.VMEM)
HBM = pl.BlockSpec(memory_space=pltpu.HBM)


def round_up(number, step):
    return -(-number // step) * step


def route_kernel(
    live_ref, holders_in, slots_in, q_in, lists_ref, *refs
):
    out_refs, (holders_ref, slots_ref, all_ref, sems) = refs[:HALVES], refs[HALVES:]
    rows = q_in.shape[0]
    columns = all_ref.shape[2]
    loading = [
        pltpu.make_async_copy(holders_in, holders_ref, sems.at[0]),
        pltpu.make_async_copy(slots_in, slots_ref, sems.at[1]),
    ]
    passing = [
        pltpu.make_async_copy(
            q_in.at[:, pl.ds(h * columns, columns)],
            all_ref.at[h, pl.ds(0, rows)],
            sems.at[2 + h],
        )
        for h in range(HALVES)
    ]
    for copy in loading + passing:
        copy.start()
    for copy in loading:
        copy.wait()
    peers, width = lists_ref.shape
    number = holders_ref.shape[1]
    padded = round_up(peers, 16)
    holder = lax.broadcasted_iota(jnp.int32, (padded, number), 0)
    entry = lax.broadcasted_iota(jnp.int32, (padded, number), 1)
    hot = (holders_ref[...] == holder) & (entry < live_ref[0])
    ones = jnp.where(hot, 1.0, 0.0)
    earlier = lax.broadcasted_iota(jnp.int32, (number, number), 0) < lax.broadcasted_iota(
        jnp.int32, (number, number), 1
    )
    ranks = jnp.dot(
        ones.astype(jnp.bfloat16),
        jnp.where(earlier, 1.0, 0.0).astype(jnp.bfloat16),
        preferred_element_type=jnp.float32,
    )
    rank = jnp.sum(ranks * ones, axis=0, keepdims=True)
    rank = jnp.broadcast_to(rank, (8, number)).T[:, :1].astype(jnp.int32)
    place = lax.broadcasted_iota(jnp.int32, (number, width), 1) == rank
    slots = jnp.where(hot, slots_ref[...], 0).astype(jnp.float32)
    lists = jnp.dot(
        slots.astype(jnp.bfloat16),
        jnp.where(place, 1.0, 0.0).astype(jnp.bfloat16),
        preferred_element_type=jnp.float32,
    )
    counts = jnp.sum(ones, axis=1, keepdims=True)
    last = lax.broadcasted_iota(jnp.int32, (padded, width), 1) == width - 1
    lists = jnp.where(last, counts, lists)[:peers]
    lists_ref[...] = lists.astype(jnp.int32)

    each = columns // width
    riders = all_ref.shape[1] - rows
    row = lax.broadcasted_iota(jnp.int32, (riders, columns), 0)
    tail = jnp.zeros((riders, columns), jnp.float32)
    for r in range(-(-peers // each)):
        line = [lists[h : h + 1] for h in range(r * each, min(peers, (r + 1) * each))]
        line += [jnp.zeros((1, width), jnp.float32)] * (each - len(line))
        tail = jnp.where(row == r, jnp.concatenate(line, axis=1), tail)
    leaving = [
        pltpu.make_async_copy(all_ref.at[h], out_refs[h], sems.at[2 + HALVES + h])
        for h in range(HALVES)
    ]
    for h in range(HALVES):
        all_ref[h, rows:, :] = tail.astype(jnp.bfloat16)
        passing[h].wait()
        leaving[h].start()
    for copy in leaving:
        copy.wait()


def route(live, holders, slots, queries, peers, width):
    rows, columns = queries.shape[0], queries.shape[1] // HALVES
    riders = round_up(-(-peers // (columns // width)), 16)
    return pl.pallas_call(
        route_kernel,
        out_shape=(
            jax.ShapeDtypeStruct((peers, width), jnp.int32),
            *[jax.ShapeDtypeStruct((rows + riders, columns), jnp.bfloat16)] * HALVES,
        ),
        in_specs=[SMEM, HBM, HBM, HBM],
        out_specs=(VMEM, *[HBM] * HALVES),
        scratch_shapes=[
            pltpu.VMEM(holders.shape, jnp.int32),
            pltpu.VMEM(slots.shape, jnp.int32),
            pltpu.VMEM((HALVES, rows + riders, columns), jnp.bfloat16),
            pltpu.SemaphoreType.DMA((2 + 2 * HALVES,)),
        ],
        compiler_params=pltpu.CompilerParams(vmem_limit_bytes=62 * 1024 * 1024),
        name="route",
    )(live, holders, slots, queries)


def score(q, keys):
    return lax.dot_general(q, keys, (((1,), (1,)), ((), ())), preferred_element_type=jnp.float32)


def twice(value):
    return jnp.concatenate([value, value], axis=1)


def attend(
    slot, count, store_ref, span_ref, span_live, q_ref, k_ref, v_ref, s_ref, ref_ref, acc_ref, rows,
    scale, stored=None,
):
    block_rows, head_dim = store_ref.shape[2:]
    heads = q_ref.shape[0] // rows
    stack = s_ref.shape[0]
    stacks = q_ref.shape[0] // stack
    tiles = (count + TILE - 1) // TILE

    def fetch(tile, into):
        for j in range(TILE):
            index = tile * TILE + j
            here = slot(jnp.maximum(jnp.minimum(index, count - 1), 0))
            at = slice(j * block_rows, (j + 1) * block_rows)
            k_ref[into, at, :] = store_ref[0, here]
            block = store_ref[1, here]
            v_ref[into, at, :head_dim] = jnp.where(index < count, block, jnp.zeros_like(block))
            v_ref[into, at, head_dim:] = jnp.where(
                index < count, jnp.ones_like(block), jnp.zeros_like(block)
            )

    def start():
        if span_ref is None:
            acc_ref[...] = jnp.zeros_like(acc_ref)
            return
        keys = span_ref.shape[1]
        key = lax.broadcasted_iota(jnp.int32, (rows, keys), 1)
        row = lax.broadcasted_iota(jnp.int32, (rows, keys), 0)
        mask = (key <= row) & (key < span_live)
        values = jnp.concatenate(
            [span_ref[1], jnp.ones((keys, head_dim), jnp.bfloat16)], axis=1
        )
        s = score(q_ref[:rows, :], span_ref[0])
        for g in range(heads):
            at = slice(g * rows, (g + 1) * rows)
            if g + 1 < heads:
                following = score(q_ref[(g + 1) * rows : (g + 2) * rows, :], span_ref[0])
            s = jnp.where(mask, s, LOW)
            top = jnp.max(s, axis=1, keepdims=True)
            ref_ref[at, :] = jnp.broadcast_to(top, (rows, head_dim))
            p = jnp.exp2((s - top) * scale).astype(jnp.bfloat16)
            acc_ref[at, :] = jnp.dot(p, values, preferred_element_type=jnp.float32)
            s = following

    start()
    if stored is not None:
        stored()

    @pl.when(count > 0)
    def _():
        fetch(0, 0)
        if span_ref is None:
            few = score(q_ref[...], k_ref[0, : 8 * block_rows, :])
            ref_ref[...] = jnp.broadcast_to(
                jnp.max(few, axis=1, keepdims=True), ref_ref.shape
            )
        s_ref[...] = score(q_ref[:stack, :], k_ref[0])

        def step(tile, carry):
            now = lax.rem(tile, 2)
            later = 1 - now
            keys, values = k_ref[now], v_ref[now]
            s = s_ref[...]
            fetch(tile + 1, later)
            for c in range(stacks):
                at = slice(c * stack, (c + 1) * stack)
                if c + 1 < stacks:
                    following = score(q_ref[(c + 1) * stack : (c + 2) * stack, :], keys)
                else:
                    s_ref[...] = score(q_ref[:stack, :], k_ref[later])
                p = jnp.exp2((s - twice(ref_ref[at, :])) * scale).astype(jnp.bfloat16)
                acc_ref[at, :] += jnp.dot(p, values, preferred_element_type=jnp.float32)
                s = following
            return carry

        lax.fori_loop(0, tiles, step, 0)
        beyond = jnp.max(jnp.where(acc_ref[:, head_dim:] < TOP, 0.0, 1.0))

        @pl.when(beyond > 0.0)
        def _():
            start()
            if span_ref is None:
                ref_ref[...] = jnp.full_like(ref_ref, LOW)

            def careful(tile, carry):
                fetch(tile, 0)

                def head(g, inner):
                    at = pl.ds(pl.multiple_of(g * rows, rows), rows)
                    s = score(q_ref[at, :], k_ref[0])
                    old = ref_ref[at, :]
                    new = jnp.maximum(old, jnp.max(s, axis=1, keepdims=True))
                    p = jnp.exp2((s - twice(new)) * scale).astype(jnp.bfloat16)
                    update = jnp.dot(p, v_ref[0], preferred_element_type=jnp.float32)
                    acc_ref[at, :] = (
                        acc_ref[at, :] * twice(jnp.exp2((old - new) * scale)) + update
                    )
                    ref_ref[at, :] = new
                    return inner

                return lax.fori_loop(0, heads, head, carry)

            lax.fori_loop(0, tiles, careful, 0)


def stack_heads(queries_ref, q_ref, rows):
    head_dim = q_ref.shape[1]
    for g in range(q_ref.shape[0] // rows):
        q_ref[g * rows : (g + 1) * rows, :] = queries_ref[
            :rows, g * head_dim : (g + 1) * head_dim
        ]


def write_logs(out_ref, logs):
    heads, rows = logs.shape
    first = logs.astype(jnp.bfloat16).astype(jnp.float32)
    rest = logs - first
    second = rest.astype(jnp.bfloat16).astype(jnp.float32)
    third = rest - second
    spare = jnp.zeros((16 - 3 * heads, rows), jnp.float32)
    lines = jnp.concatenate([first, second, third, spare], axis=0)
    if out_ref.shape[1] > rows:
        lines = jnp.concatenate(
            [lines, jnp.zeros((16, out_ref.shape[1] - rows), jnp.float32)], axis=1
        )
    out_ref[rows:, :] = lines.astype(jnp.bfloat16)


def read_logs(part_ref, heads, rows):
    lines = part_ref[rows:, :].astype(jnp.float32)[:, :rows]
    return lines[:heads] + lines[heads : 2 * heads] + lines[2 * heads : 3 * heads]


def finish(out_refs, ref_ref, acc_ref, rows, scale):
    head_dim = ref_ref.shape[1]
    heads = ref_ref.shape[0] // rows // len(out_refs)
    lane = lax.broadcasted_iota(jnp.int32, (rows, head_dim), 1)
    for h, out_ref in enumerate(out_refs):
        logs = jnp.zeros((rows, head_dim), jnp.float32)
        for g in range(heads):
            at = slice((h * heads + g) * rows, (h * heads + g + 1) * rows)
            total = acc_ref[at, head_dim:]
            out_ref[:rows, g * head_dim : (g + 1) * head_dim] = (
                acc_ref[at, :head_dim] / total
            ).astype(jnp.bfloat16)
            logs = jnp.where(lane == g, ref_ref[at, :] * scale + jnp.log2(total), logs)
        write_logs(out_ref, logs.T[:heads])


def own_kernel(
    scale, me_ref, span_live_ref, lists_ref, queries_in, store_in, span_in, *refs
):
    out_refs = refs[:HALVES]
    queries_ref, store_ref, span_ref, sems, q_ref, k_ref, v_ref, s_ref, ref_ref, acc_ref = refs[
        HALVES:
    ]
    me = me_ref[0]
    rows = queries_ref.shape[0]
    copies = [
        pltpu.make_async_copy(source, target, sems.at[i])
        for i, (source, target) in enumerate(
            ((queries_in, queries_ref), (span_in, span_ref), (store_in, store_ref))
        )
    ]
    for copy in copies:
        copy.start()
    copies[0].wait()
    stack_heads(queries_ref, q_ref, rows)
    copies[1].wait()
    attend(
        lambda index: lists_ref[me, index], lists_ref[me, lists_ref.shape[1] - 1], store_ref,
        span_ref, span_live_ref[0], q_ref, k_ref, v_ref, s_ref, ref_ref, acc_ref, rows, scale,
        copies[2].wait,
    )
    finish(out_refs, ref_ref, acc_ref, rows, scale)


def guest_kernel(scale, width, rows, number, me_ref, *refs):
    loaded_refs, store_ref = refs[:number], refs[number]
    out_refs = refs[number + 2 : 2 * number + 2]
    wide_ref, list_ref, sem_ref, q_ref, k_ref, v_ref, s_ref, ref_ref, acc_ref = refs[
        2 * number + 2 :
    ]
    each = loaded_refs[0].shape[1] // width
    me = me_ref[0]
    lane = pl.multiple_of(lax.rem(me, each) * width, 128)
    for which, loaded_ref in enumerate(loaded_refs):
        riders = loaded_ref[rows:, pl.ds(lane, width)].astype(jnp.float32)
        row = lax.broadcasted_iota(jnp.int32, riders.shape, 0)
        mine = jnp.sum(jnp.where(row == me // each, riders, 0.0), axis=0, keepdims=True)
        wide_ref[which : which + 1, :] = mine.astype(jnp.int32)
    copy = pltpu.make_async_copy(wide_ref, list_ref, sem_ref)
    copy.start()
    stack_heads(loaded_refs[0], q_ref, rows)
    copy.wait()
    for which, (loaded_ref, out_ref) in enumerate(zip(loaded_refs, out_refs)):
        count = list_ref[which, width - 1]

        @pl.when(count > 0)
        def _():
            if which:
                stack_heads(loaded_ref, q_ref, rows)
            attend(
                lambda index: list_ref[which, index], count, store_ref, None, None,
                q_ref, k_ref, v_ref, s_ref, ref_ref, acc_ref, rows, scale,
            )
            finish([out_ref], ref_ref, acc_ref, rows, scale)

        @pl.when(count == 0)
        def _():
            out_ref[...] = jnp.zeros_like(out_ref)
            write_logs(out_ref, jnp.full((q_ref.shape[0] // rows, rows), LOW, jnp.float32))


def attention_scratch(heads, rows, head_dim, block_rows):
    keys = TILE * block_rows
    return [
        pltpu.VMEM((heads * rows, head_dim), jnp.bfloat16),
        pltpu.VMEM((2, keys, head_dim), jnp.bfloat16),
        pltpu.VMEM((2, keys, 2 * head_dim), jnp.bfloat16),
        pltpu.VMEM((math.gcd(heads * rows, STACK), keys), jnp.float32),
        pltpu.VMEM((heads * rows, head_dim), jnp.float32),
        pltpu.VMEM((heads * rows, 2 * head_dim), jnp.float32),
    ]


def attention_cost(rows, keys, head_dim, heads):
    return pl.CostEstimate(
        flops=4 * rows * keys * head_dim * heads,
        bytes_accessed=4 * 1024 * 1024,
        transcendentals=rows * keys * heads,
    )


def merged(parts, heads, rows):
    logs = [read_logs(part, heads, rows) for part in parts]
    top = functools.reduce(jnp.maximum, logs)
    weights = [jnp.exp2(log - top) for log in logs]
    total = functools.reduce(jnp.add, weights)
    return [weight / total for weight in weights], top + jnp.log2(total)


def weighted(parts, weights, g, head_dim, rows):
    total = jnp.zeros((rows, head_dim), jnp.float32)
    for part, weight in zip(parts, weights):
        part_rows = part[:rows, g * head_dim : (g + 1) * head_dim]
        total += part_rows.astype(jnp.float32) * weight[:, g : g + 1]
    return total.astype(jnp.bfloat16)


def merge_kernel(heads, number, *refs):
    parts, out_ref = refs[:number], refs[number + 1]
    rows = out_ref.shape[0] - 16
    head_dim = out_ref.shape[1] // heads
    weights, logs = merged(parts, heads, rows)
    weights = [weight.T for weight in weights]
    for g in range(heads):
        out_ref[:rows, g * head_dim : (g + 1) * head_dim] = weighted(
            parts, weights, g, head_dim, rows
        )
    write_logs(out_ref, logs)


def project_kernel(heads, number, turn_ref, span_live_ref, *refs):
    parts = refs[: HALVES * number]
    weight_ref, away_ref, keep_ref, att_ref, sorted_ref, held_ref, sems = refs[HALVES * number :]
    rows, features = att_ref.shape
    chunks, _, width = held_ref.shape
    head_dim = features // heads
    copies = [
        pltpu.make_async_copy(weight_ref.at[:, pl.ds(i * width, width)], held_ref.at[i], sems.at[i])
        for i in range(chunks)
    ]
    for copy in copies:
        copy.start()

    some = heads // HALVES
    row = lax.broadcasted_iota(jnp.int32, (some, rows), 1)
    for h in range(HALVES):
        here = parts[h * number : (h + 1) * number]
        weights, _ = merged(here, some, rows)
        weights = [jnp.where(row < span_live_ref[0], weight, 0.0).T for weight in weights]
        for g in range(some):
            at = (h * some + g) * head_dim
            att_ref[:, at : at + head_dim] = weighted(here, weights, g, head_dim, rows)

    chips = keep_ref.shape[0]
    block = keep_ref.shape[1]
    chip, core = turn_ref[0] // 2, lax.rem(turn_ref[0], 2)
    for side, wanted in enumerate((1 - core, core)):
        for k in range(chips):
            owner = 2 * lax.rem(chip + k, chips) + wanted
            at = (side * chips + k) * block
            sorted_ref[at : at + block, :] = att_ref[
                pl.ds(pl.multiple_of(owner * block, block), block), :
            ]
    for i in range(chunks):
        copies[i].wait()
        at = slice(i * width, (i + 1) * width)
        product = jnp.dot(
            sorted_ref[...], held_ref[i], preferred_element_type=jnp.float32
        ).astype(jnp.bfloat16)
        for k in range(chips):
            away_ref[k, :, at] = product[k * block : (k + 1) * block]
            keep_ref[k, :, at] = product[(chips + k) * block : (chips + k + 1) * block]


def project(turn, span_live, parts, out_weight, heads, members):
    features, outputs = out_weight.shape
    rows = parts[0].shape[0] - 16
    width = 512
    chunks = outputs // width
    block_shape = jax.ShapeDtypeStruct((members // 2, rows // members, outputs), jnp.bfloat16)
    return pl.pallas_call(
        functools.partial(project_kernel, heads, len(parts) // HALVES),
        out_shape=(block_shape, block_shape),
        in_specs=[SMEM, SMEM] + [VMEM] * len(parts) + [HBM],
        out_specs=(VMEM, VMEM),
        scratch_shapes=[
            pltpu.VMEM((rows, features), jnp.bfloat16),
            pltpu.VMEM((rows, features), jnp.bfloat16),
            pltpu.VMEM((chunks, features, width), jnp.bfloat16),
            pltpu.SemaphoreType.DMA((chunks,)),
        ],
        compiler_params=pltpu.CompilerParams(vmem_limit_bytes=48 * 1024 * 1024),
        cost_estimate=pl.CostEstimate(
            flops=2 * rows * features * outputs,
            bytes_accessed=2 * (features + rows) * outputs,
            transcendentals=0,
        ),
        name="project",
    )(turn, span_live, *parts, out_weight)


def add_kernel(kept_ref, come_ref, *out_refs):
    for k, out_ref in enumerate(out_refs):
        out_ref[...] = (
            kept_ref[k + 1].astype(jnp.float32) + come_ref[k + 1].astype(jnp.float32)
        ).astype(jnp.bfloat16)


def total_kernel(kept_ref, come_ref, *refs):
    total = kept_ref[0].astype(jnp.float32) + come_ref[0].astype(jnp.float32)
    for ref in refs[:-1]:
        total += ref[...].astype(jnp.float32)
    refs[-1][...] = total.astype(jnp.bfloat16)


def scatter_sum(away, keep, members):
    chips, block, outputs = keep.shape
    shape = jax.ShapeDtypeStruct((block, outputs), jnp.bfloat16)
    params = pltpu.CompilerParams(vmem_limit_bytes=VMEM_LIMIT)
    come = lax.ppermute(away, "tp", [(i, i ^ 1) for i in range(members)])
    sums = pl.pallas_call(
        add_kernel,
        out_shape=[shape] * (chips - 1),
        in_specs=[VMEM, VMEM],
        out_specs=[VMEM] * (chips - 1),
        compiler_params=params,
        name="add_cores",
    )(keep, come)
    arrived = [
        lax.ppermute(each, "tp", [(i, (i + 2 * (k + 1)) % members) for i in range(members)])
        for k, each in enumerate(sums)
    ]
    return pl.pallas_call(
        total_kernel,
        out_shape=shape,
        in_specs=[VMEM] * (2 + len(arrived)),
        out_specs=VMEM,
        compiler_params=params,
        name="add_chips",
    )(keep, come, *arrived)


def pack_kernel(me_ref, span_live_ref, owners_ref, span_ref, *refs):
    out_refs, (out_ref, counts_ref) = refs[:-2], refs[-2:]
    peers = out_ref.shape[0]
    block_rows, head_dim = out_ref.shape[3:]
    out_ref[...] = jnp.zeros_like(out_ref)
    for k in range(peers):
        counts_ref[k] = 0
    row = lax.broadcasted_iota(jnp.int32, (block_rows, head_dim), 0)
    for b in range(span_ref.shape[1] // block_rows):
        owner = owners_ref[b]
        rank = counts_ref[owner]
        counts_ref[owner] = rank + 1
        keep = row + b * block_rows < span_live_ref[0]
        for side in range(2):
            block = span_ref[side, b * block_rows : (b + 1) * block_rows, :]
            out_ref[owner, side, rank] = jnp.where(keep, block, jnp.zeros_like(block))
    for k, each_ref in enumerate(out_refs):
        each_ref[...] = out_ref[me_ref[0] ^ k]


def unpack_kernel(me_ref, *refs):
    for k, each_ref in enumerate(refs[:-1]):
        refs[-1][:, me_ref[0] ^ k] = each_ref[...]


def shards(
    queries,
    cache_store,
    span_cache,
    out_weight,
    prefix_blocks,
    span_lengths,
    hit_holders,
    hit_slots,
    store_owners,
):
    peers = lax.axis_size("inst")
    block_rows, head_dim = cache_store.shape[2:]
    rows, columns = queries.shape
    heads = columns // head_dim
    block_max = hit_slots.shape[1]
    cap = max(2, block_max * 5 // (4 * peers))
    new_count = rows // block_rows
    push_cap = max(2, 2 * new_count // peers)
    scale = math.log2(math.e) / math.sqrt(head_dim)
    me = lax.axis_index("inst").reshape(1)
    width = round_up(cap + 1, 128)
    some = heads // HALVES
    part_shape = jax.ShapeDtypeStruct((rows + 16, columns // HALVES), jnp.bfloat16)
    params = pltpu.CompilerParams(vmem_limit_bytes=VMEM_LIMIT)
    anywhere = pl.BlockSpec(memory_space=pl.ANY)

    def exchange(value, bit):
        return lax.ppermute(value, "inst", [(i, i ^ bit) for i in range(peers)])

    order = sorted(range(1, peers), key=lambda k: -(k & -k))

    def spread(loaded, after):
        held = {0: loaded}
        for k in order:
            source = held[k & (k - 1)]
            if k & (k - 1):
                source, after = lax.optimization_barrier((source, after))
            held[k] = exchange(source, k & -k)
        return held

    def guests(held, group, after):
        return pl.pallas_call(
            functools.partial(guest_kernel, scale, width, rows, len(group)),
            out_shape=[part_shape] * len(group),
            in_specs=[SMEM] + [VMEM] * (len(group) + 1) + [anywhere],
            out_specs=[VMEM] * len(group),
            scratch_shapes=[
                pltpu.VMEM((len(group), width), jnp.int32),
                pltpu.SMEM((len(group), width), jnp.int32),
                pltpu.SemaphoreType.DMA,
                *attention_scratch(some, rows, head_dim, block_rows),
            ],
            compiler_params=params,
            cost_estimate=attention_cost(rows, 6 * rows * len(group), head_dim, some),
            name="guest_attention",
        )(me, *[held[k] for k in group], cache_store, after)

    def gather_back(parts, after):
        parts = dict(parts)
        for k in reversed(order):
            arrived = [exchange(parts[c], c & -c) for c in order if c & (c - 1) == k]
            if arrived:
                parts[k] = after = pl.pallas_call(
                    functools.partial(merge_kernel, some, len(arrived) + 1),
                    out_shape=part_shape,
                    in_specs=[VMEM] * (len(arrived) + 1) + [anywhere],
                    out_specs=VMEM,
                    compiler_params=params,
                    name="merge",
                )(parts[k], *arrived, after)
        parts[1], after = lax.optimization_barrier((parts[1], after))
        return [exchange(parts[k], k) for k in order if k & (k - 1) == 0], after

    lists, *loaded = route(
        prefix_blocks, hit_holders.reshape(1, -1), hit_slots, queries, peers, width
    )
    own = pl.pallas_call(
        functools.partial(own_kernel, scale),
        out_shape=[part_shape] * HALVES,
        in_specs=[SMEM, SMEM, SMEM, HBM, HBM, HBM],
        out_specs=[VMEM] * HALVES,
        scratch_shapes=[
            pltpu.VMEM(queries.shape, jnp.bfloat16),
            pltpu.VMEM(cache_store.shape, jnp.bfloat16),
            pltpu.VMEM(span_cache.shape, jnp.bfloat16),
            pltpu.SemaphoreType.DMA((3,)),
            *attention_scratch(heads, rows, head_dim, block_rows),
        ],
        compiler_params=params,
        cost_estimate=attention_cost(rows, 8 * rows, head_dim, heads),
        name="own_attention",
    )(me, span_lengths, lists, queries, cache_store, span_cache)

    after, before, arrived = own[0], None, []
    for h in range(HALVES):
        held = spread(loaded[h], after)
        if h + 1 < HALVES:
            loaded[h + 1], after = lax.optimization_barrier((loaded[h + 1], after))
            groups = [order[i : i + 2] for i in range(0, peers - 1, 2)]
        else:
            groups = [[k] for k in order if k > 1] + [[1]]
        parts = {}
        for index, group in enumerate(groups):
            results = guests(held, group, after)
            after = results[0]
            parts.update(zip(group, results))
            if index == 0 and before is not None:
                back, after = gather_back(before, after)
                arrived.append(back)
        before = parts
    back, after = gather_back(before, after)
    arrived.append(back)

    members = lax.axis_size("tp")
    turn = lax.axis_index("tp").reshape(1)
    parts = [part for h in range(HALVES) for part in (own[h], *arrived[h])]
    away, keep = project(turn, span_lengths, parts, out_weight, heads, members)
    projected = scatter_sum(away, keep, members)

    push_shape = jax.ShapeDtypeStruct((2, push_cap, block_rows, head_dim), jnp.bfloat16)
    outgoing = pl.pallas_call(
        pack_kernel,
        out_shape=[push_shape] * peers,
        in_specs=[SMEM, SMEM, SMEM, VMEM],
        out_specs=[VMEM] * peers,
        scratch_shapes=[
            pltpu.VMEM((peers, *push_shape.shape), jnp.bfloat16),
            pltpu.SMEM((peers,), jnp.int32),
        ],
        compiler_params=params,
        name="pack_blocks",
    )(me, span_lengths, store_owners.reshape(-1), span_cache)
    incoming = [outgoing[0], *[exchange(outgoing[k], k) for k in range(1, peers)]]
    pushed_blocks = pl.pallas_call(
        unpack_kernel,
        out_shape=jax.ShapeDtypeStruct(
            (2, peers, push_cap, block_rows, head_dim), jnp.bfloat16
        ),
        in_specs=[SMEM] + [VMEM] * peers,
        out_specs=VMEM,
        compiler_params=params,
        name="unpack_blocks",
    )(me, *incoming).reshape(2, peers * push_cap, block_rows, head_dim)
    return (projected, pushed_blocks)


def solution(mesh):
    return jax.shard_map(
        shards,
        mesh=mesh,
        in_specs=(
            P(("pods", "inst"), "tp"),
            P(None, ("pods", "inst"), None, "tp"),
            P(None, ("pods", "inst"), "tp"),
            P("tp", None),
            P(("pods", "inst")),
            P(("pods", "inst")),
            P(("pods", "inst"), None, None),
            P(("pods", "inst"), None),
            P(("pods", "inst"), None, None),
        ),
        out_specs=(P(("pods", "inst", "tp"), None), P(None, ("pods", "inst"), None, "tp")),
        check_vma=False,
    )
```

```python
import functools
import math

import jax
import jax.numpy as jnp
from jax import lax
from jax.experimental import pallas as pl
from jax.experimental.pallas import tpu as pltpu
from jax.sharding import PartitionSpec as P

LOW = -1e30
TOP = 2.0**100
TILE = 16
STACK = 512
HALVES = 2
TAIL = 8
VMEM_LIMIT = 20 * 1024 * 1024

SMEM = pl.BlockSpec(memory_space=pltpu.SMEM)
VMEM = pl.BlockSpec(memory_space=pltpu.VMEM)
HBM = pl.BlockSpec(memory_space=pltpu.HBM)


def round_up(number, step):
    return -(-number // step) * step


def original_row(row, h, members, own_rows):
    each = own_rows // HALVES
    member = sum((row >= m * each).astype(jnp.int32) for m in range(1, members))
    return row + member * (own_rows - each) + h * each


def route_kernel(
    members, live_ref, holders_in, slots_in, q_in, lists_ref, *refs
):
    out_refs, (holders_ref, slots_ref, sems) = refs[:HALVES], refs[HALVES:]
    columns = q_in.shape[1]
    rows = q_in.shape[0] // HALVES
    each = rows // members
    loading = [
        pltpu.make_async_copy(holders_in, holders_ref, sems.at[0]),
        pltpu.make_async_copy(slots_in, slots_ref, sems.at[1]),
    ]
    passing = [
        pltpu.make_async_copy(
            q_in.at[pl.ds((m * HALVES + h) * each, each)],
            out_refs[h].at[pl.ds(m * each, each)],
            sems.at[2 + h * members + m],
        )
        for h in range(HALVES)
        for m in range(members)
    ]
    for copy in loading + passing:
        copy.start()
    for copy in loading:
        copy.wait()
    peers, width = lists_ref.shape
    number = holders_ref.shape[1]
    padded = round_up(peers, 16)
    holder = lax.broadcasted_iota(jnp.int32, (padded, number), 0)
    entry = lax.broadcasted_iota(jnp.int32, (padded, number), 1)
    hot = (holders_ref[...] == holder) & (entry < live_ref[0])
    ones = jnp.where(hot, 1.0, 0.0)
    earlier = lax.broadcasted_iota(jnp.int32, (number, number), 0) < lax.broadcasted_iota(
        jnp.int32, (number, number), 1
    )
    ranks = jnp.dot(
        ones.astype(jnp.bfloat16),
        jnp.where(earlier, 1.0, 0.0).astype(jnp.bfloat16),
        preferred_element_type=jnp.float32,
    )
    rank = jnp.sum(ranks * ones, axis=0, keepdims=True)
    rank = jnp.broadcast_to(rank, (8, number)).T[:, :1].astype(jnp.int32)
    place = lax.broadcasted_iota(jnp.int32, (number, width), 1) == rank
    slots = jnp.where(hot, slots_ref[...], 0).astype(jnp.float32)
    lists = jnp.dot(
        slots.astype(jnp.bfloat16),
        jnp.where(place, 1.0, 0.0).astype(jnp.bfloat16),
        preferred_element_type=jnp.float32,
    )
    counts = jnp.sum(ones, axis=1, keepdims=True)
    last = lax.broadcasted_iota(jnp.int32, (padded, width), 1) == width - 1
    lists = jnp.where(last, counts, lists)[:peers]
    lists_ref[...] = lists.astype(jnp.int32)

    lines = columns // width
    row = lax.broadcasted_iota(jnp.int32, (TAIL, columns), 0)
    tail = jnp.zeros((TAIL, columns), jnp.float32)
    for r in range(-(-peers // lines)):
        line = [lists[h : h + 1] for h in range(r * lines, min(peers, (r + 1) * lines))]
        line += [jnp.zeros((1, width), jnp.float32)] * (lines - len(line))
        tail = jnp.where(row == r, jnp.concatenate(line, axis=1), tail)
    for out_ref in out_refs:
        out_ref[rows:, :] = tail.astype(jnp.bfloat16)
    for copy in passing:
        copy.wait()


def route(live, holders, slots, queries, peers, width, members):
    rows, columns = queries.shape[0] // HALVES, queries.shape[1]
    return pl.pallas_call(
        functools.partial(route_kernel, members),
        out_shape=(
            jax.ShapeDtypeStruct((peers, width), jnp.int32),
            *[jax.ShapeDtypeStruct((rows + TAIL, columns), jnp.bfloat16)] * HALVES,
        ),
        in_specs=[SMEM, HBM, HBM, HBM],
        out_specs=[VMEM] * (1 + HALVES),
        scratch_shapes=[
            pltpu.VMEM(holders.shape, jnp.int32),
            pltpu.VMEM(slots.shape, jnp.int32),
            pltpu.SemaphoreType.DMA((2 + HALVES * members,)),
        ],
        compiler_params=pltpu.CompilerParams(vmem_limit_bytes=62 * 1024 * 1024),
        name="route",
    )(live, holders, slots, queries)


def score(q, keys):
    return lax.dot_general(q, keys, (((1,), (1,)), ((), ())), preferred_element_type=jnp.float32)


def twice(value):
    return jnp.concatenate([value, value], axis=1)


def attend(
    slot, count, store_ref, span_ref, masks, q_ref, k_ref, v_ref, s_ref, ref_ref, acc_ref, rows,
    scale, stored=None,
):
    block_rows, head_dim = store_ref.shape[2:]
    heads = q_ref.shape[0] // rows
    stack = s_ref.shape[0]
    stacks = q_ref.shape[0] // stack
    tiles = (count + TILE - 1) // TILE

    def fetch(tile, into):
        for j in range(TILE):
            index = tile * TILE + j
            here = slot(jnp.maximum(jnp.minimum(index, count - 1), 0))
            at = slice(j * block_rows, (j + 1) * block_rows)
            k_ref[into, at, :] = store_ref[0, here]
            block = store_ref[1, here]
            v_ref[into, at, :head_dim] = jnp.where(index < count, block, jnp.zeros_like(block))
            v_ref[into, at, head_dim:] = jnp.where(
                index < count, jnp.ones_like(block), jnp.zeros_like(block)
            )

    def start():
        if span_ref is None:
            acc_ref[...] = jnp.zeros_like(acc_ref)
            return
        keys = span_ref.shape[1]
        values = jnp.concatenate(
            [span_ref[1], jnp.ones((keys, head_dim), jnp.bfloat16)], axis=1
        )
        s = score(q_ref[:rows, :], span_ref[0])
        for g in range(heads):
            at = slice(g * rows, (g + 1) * rows)
            if g + 1 < heads:
                following = score(q_ref[(g + 1) * rows : (g + 2) * rows, :], span_ref[0])
            s = jnp.where(masks[g * HALVES // heads], s, LOW)
            top = jnp.max(s, axis=1, keepdims=True)
            ref_ref[at, :] = jnp.broadcast_to(top, (rows, head_dim))
            p = jnp.exp2((s - top) * scale).astype(jnp.bfloat16)
            acc_ref[at, :] = jnp.dot(p, values, preferred_element_type=jnp.float32)
            s = following

    start()
    if stored is not None:
        stored()

    @pl.when(count > 0)
    def _():
        fetch(0, 0)
        if span_ref is None:
            few = score(q_ref[...], k_ref[0, : 8 * block_rows, :])
            ref_ref[...] = jnp.broadcast_to(
                jnp.max(few, axis=1, keepdims=True), ref_ref.shape
            )
        s_ref[...] = score(q_ref[:stack, :], k_ref[0])

        def step(tile, carry):
            now = lax.rem(tile, 2)
            later = 1 - now
            keys, values = k_ref[now], v_ref[now]
            s = s_ref[...]
            fetch(tile + 1, later)
            for c in range(stacks):
                at = slice(c * stack, (c + 1) * stack)
                if c + 1 < stacks:
                    following = score(q_ref[(c + 1) * stack : (c + 2) * stack, :], keys)
                else:
                    s_ref[...] = score(q_ref[:stack, :], k_ref[later])
                p = jnp.exp2((s - twice(ref_ref[at, :])) * scale).astype(jnp.bfloat16)
                acc_ref[at, :] += jnp.dot(p, values, preferred_element_type=jnp.float32)
                s = following
            return carry

        lax.fori_loop(0, tiles, step, 0)
        beyond = jnp.max(jnp.where(acc_ref[:, head_dim:] < TOP, 0.0, 1.0))

        @pl.when(beyond > 0.0)
        def _():
            start()
            if span_ref is None:
                ref_ref[...] = jnp.full_like(ref_ref, LOW)

            def careful(tile, carry):
                fetch(tile, 0)

                def head(g, inner):
                    at = pl.ds(pl.multiple_of(g * rows, rows), rows)
                    s = score(q_ref[at, :], k_ref[0])
                    old = ref_ref[at, :]
                    new = jnp.maximum(old, jnp.max(s, axis=1, keepdims=True))
                    p = jnp.exp2((s - twice(new)) * scale).astype(jnp.bfloat16)
                    update = jnp.dot(p, v_ref[0], preferred_element_type=jnp.float32)
                    acc_ref[at, :] = (
                        acc_ref[at, :] * twice(jnp.exp2((old - new) * scale)) + update
                    )
                    ref_ref[at, :] = new
                    return inner

                return lax.fori_loop(0, heads, head, carry)

            lax.fori_loop(0, tiles, careful, 0)


def stack_heads(queries_ref, q_ref, rows, first=0):
    head_dim = q_ref.shape[1]
    for g in range(queries_ref.shape[1] // head_dim):
        q_ref[(first + g) * rows : (first + g + 1) * rows, :] = queries_ref[
            :rows, g * head_dim : (g + 1) * head_dim
        ]


def write_logs(out_ref, logs):
    heads, rows = logs.shape
    first = logs.astype(jnp.bfloat16).astype(jnp.float32)
    rest = logs - first
    second = rest.astype(jnp.bfloat16).astype(jnp.float32)
    third = rest - second
    spare = jnp.zeros((heads, out_ref.shape[1] - 3 * rows), jnp.float32)
    lines = jnp.concatenate([first, second, third, spare], axis=1)
    if heads < TAIL:
        more = jnp.zeros((TAIL - heads, out_ref.shape[1]), jnp.float32)
        lines = jnp.concatenate([lines, more], axis=0)
    out_ref[rows:, :] = lines.astype(jnp.bfloat16)


def read_logs(part_ref, heads, rows):
    lines = part_ref[rows:, :].astype(jnp.float32)[:heads]
    return lines[:, :rows] + lines[:, rows : 2 * rows] + lines[:, 2 * rows : 3 * rows]


def finish(out_refs, ref_ref, acc_ref, rows, scale):
    head_dim = ref_ref.shape[1]
    heads = ref_ref.shape[0] // rows // len(out_refs)
    lane = lax.broadcasted_iota(jnp.int32, (rows, head_dim), 1)
    for h, out_ref in enumerate(out_refs):
        logs = jnp.zeros((rows, head_dim), jnp.float32)
        for g in range(heads):
            at = slice((h * heads + g) * rows, (h * heads + g + 1) * rows)
            total = acc_ref[at, head_dim:]
            out_ref[:rows, g * head_dim : (g + 1) * head_dim] = (
                acc_ref[at, :head_dim] / total
            ).astype(jnp.bfloat16)
            logs = jnp.where(lane == g, ref_ref[at, :] * scale + jnp.log2(total), logs)
        write_logs(out_ref, logs.T[:heads])


def own_kernel(
    scale, members, me_ref, span_live_ref, lists_ref, queries_in, store_in, span_in, *refs
):
    out_refs = refs[:HALVES]
    queries_ref, store_ref, span_ref, sems, q_ref, k_ref, v_ref, s_ref, ref_ref, acc_ref = refs[
        HALVES:
    ]
    me = me_ref[0]
    rows = queries_ref.shape[1]
    each = rows // members
    copies = [
        pltpu.make_async_copy(span_in, span_ref, sems.at[0]),
        pltpu.make_async_copy(store_in, store_ref, sems.at[1]),
    ] + [
        pltpu.make_async_copy(
            queries_in.at[pl.ds((m * HALVES + h) * each, each)],
            queries_ref.at[h, pl.ds(m * each, each)],
            sems.at[2 + h * members + m],
        )
        for h in range(HALVES)
        for m in range(members)
    ]
    for copy in copies:
        copy.start()
    keys = span_ref.shape[1]
    key = lax.broadcasted_iota(jnp.int32, (rows, keys), 1)
    row = lax.broadcasted_iota(jnp.int32, (rows, keys), 0)
    masks = [
        (key <= original_row(row, h, members, each * HALVES)) & (key < span_live_ref[0])
        for h in range(HALVES)
    ]
    for copy in copies[2:]:
        copy.wait()
    for h in range(HALVES):
        stack_heads(queries_ref.at[h], q_ref, rows, h * queries_ref.shape[2] // q_ref.shape[1])
    copies[0].wait()
    attend(
        lambda index: lists_ref[me, index], lists_ref[me, lists_ref.shape[1] - 1], store_ref,
        span_ref, masks, q_ref, k_ref, v_ref, s_ref, ref_ref, acc_ref, rows, scale,
        copies[1].wait,
    )
    finish(out_refs, ref_ref, acc_ref, rows, scale)


def guest_kernel(scale, width, rows, number, me_ref, *refs):
    loaded_refs, store_ref = refs[:number], refs[number]
    out_refs = refs[number + 2 : 2 * number + 2]
    wide_ref, list_ref, sem_ref, q_ref, k_ref, v_ref, s_ref, ref_ref, acc_ref = refs[
        2 * number + 2 :
    ]
    each = loaded_refs[0].shape[1] // width
    me = me_ref[0]
    lane = pl.multiple_of(lax.rem(me, each) * width, 128)
    for which, loaded_ref in enumerate(loaded_refs):
        riders = loaded_ref[rows:, pl.ds(lane, width)].astype(jnp.float32)
        row = lax.broadcasted_iota(jnp.int32, riders.shape, 0)
        mine = jnp.sum(jnp.where(row == me // each, riders, 0.0), axis=0, keepdims=True)
        wide_ref[which : which + 1, :] = mine.astype(jnp.int32)
    copy = pltpu.make_async_copy(wide_ref, list_ref, sem_ref)
    copy.start()
    stack_heads(loaded_refs[0], q_ref, rows)
    copy.wait()
    for which, (loaded_ref, out_ref) in enumerate(zip(loaded_refs, out_refs)):
        count = list_ref[which, width - 1]

        @pl.when(count > 0)
        def _():
            if which:
                stack_heads(loaded_ref, q_ref, rows)
            attend(
                lambda index: list_ref[which, index], count, store_ref, None, None,
                q_ref, k_ref, v_ref, s_ref, ref_ref, acc_ref, rows, scale,
            )
            finish([out_ref], ref_ref, acc_ref, rows, scale)

        @pl.when(count == 0)
        def _():
            out_ref[...] = jnp.zeros_like(out_ref)
            write_logs(out_ref, jnp.full((q_ref.shape[0] // rows, rows), LOW, jnp.float32))


def attention_scratch(heads, rows, head_dim, block_rows):
    keys = TILE * block_rows
    return [
        pltpu.VMEM((heads * rows, head_dim), jnp.bfloat16),
        pltpu.VMEM((2, keys, head_dim), jnp.bfloat16),
        pltpu.VMEM((2, keys, 2 * head_dim), jnp.bfloat16),
        pltpu.VMEM((math.gcd(heads * rows, STACK), keys), jnp.float32),
        pltpu.VMEM((heads * rows, head_dim), jnp.float32),
        pltpu.VMEM((heads * rows, 2 * head_dim), jnp.float32),
    ]


def attention_cost(rows, keys, head_dim, heads):
    return pl.CostEstimate(
        flops=4 * rows * keys * head_dim * heads,
        bytes_accessed=64 * 1024,
        transcendentals=rows * keys * heads,
    )


def merged(parts, heads, rows):
    logs = [read_logs(part, heads, rows) for part in parts]
    top = functools.reduce(jnp.maximum, logs)
    weights = [jnp.exp2(log - top) for log in logs]
    total = functools.reduce(jnp.add, weights)
    return [weight / total for weight in weights], top + jnp.log2(total)


def weighted(parts, weights, g, head_dim, rows):
    total = jnp.zeros((rows, head_dim), jnp.float32)
    for part, weight in zip(parts, weights):
        part_rows = part[:rows, g * head_dim : (g + 1) * head_dim]
        total += part_rows.astype(jnp.float32) * weight[:, g : g + 1]
    return total.astype(jnp.bfloat16)


def merge_kernel(heads, number, *refs):
    parts, out_ref = refs[:number], refs[number + 1]
    rows = out_ref.shape[0] - TAIL
    head_dim = out_ref.shape[1] // heads
    weights, logs = merged(parts, heads, rows)
    weights = [weight.T for weight in weights]
    for g in range(heads):
        out_ref[:rows, g * head_dim : (g + 1) * head_dim] = weighted(
            parts, weights, g, head_dim, rows
        )
    write_logs(out_ref, logs)


def project_kernel(heads, number, h, members, cuts, turn_ref, span_live_ref, *refs):
    parts = refs[:number]
    weight_ref, after_ref, near_ref, *away_refs = refs[number : number + 3 + cuts]
    keep_ref, att_ref, sorted_ref, held_ref, sems = refs[number + 3 + cuts :]
    rows, features = att_ref.shape
    chunks, _, width = held_ref.shape
    head_dim = features // heads
    copies = [
        pltpu.make_async_copy(weight_ref.at[:, pl.ds(i * width, width)], held_ref.at[i], sems.at[i])
        for i in range(chunks)
    ]
    for copy in copies:
        copy.start()

    row = lax.broadcasted_iota(jnp.int32, (heads, rows), 1)
    live = original_row(row, h, members, rows * HALVES // members) < span_live_ref[0]
    weights, _ = merged(parts, heads, rows)
    weights = [jnp.where(live, weight, 0.0).T for weight in weights]
    for g in range(heads):
        att_ref[:, g * head_dim : (g + 1) * head_dim] = weighted(
            parts, weights, g, head_dim, rows
        )

    chips = keep_ref.shape[0]
    block = keep_ref.shape[1]
    chip, core = turn_ref[0] // 2, lax.rem(turn_ref[0], 2)
    for side, wanted in enumerate((1 - core, core)):
        for k in range(chips):
            owner = 2 * lax.rem(chip + k, chips) + wanted
            at = (side * chips + k) * block
            sorted_ref[at : at + block, :] = att_ref[
                pl.ds(pl.multiple_of(owner * block, block), block), :
            ]
    for i in range(chunks):
        copies[i].wait()
        at = slice(i * width, (i + 1) * width)
        product = jnp.dot(
            sorted_ref[...], held_ref[i], preferred_element_type=jnp.float32
        ).astype(jnp.bfloat16)
        for k in range(chips):
            leaving = product[k * block : (k + 1) * block]
            if k:
                cut = i * cuts // chunks
                first = i * width - cut * away_refs[cut].shape[2]
                away_refs[cut][k - 1, :, first : first + width] = leaving
            else:
                near_ref[:, at] = leaving
            keep_ref[k, :, at] = product[(chips + k) * block : (chips + k + 1) * block]


def project(turn, span_live, parts, out_weight, after, heads, h, members, cuts):
    features, outputs = out_weight.shape
    rows = parts[0].shape[0] - TAIL
    width = 512
    chunks = outputs // width
    chips, block = members // 2, rows // members
    return pl.pallas_call(
        functools.partial(project_kernel, heads, len(parts), h, members, cuts),
        out_shape=[
            jax.ShapeDtypeStruct(shape, jnp.bfloat16)
            for shape in (
                (block, outputs),
                *[(chips - 1, block, outputs // cuts)] * cuts,
                (chips, block, outputs),
            )
        ],
        in_specs=[SMEM, SMEM] + [VMEM] * len(parts) + [HBM, pl.BlockSpec(memory_space=pl.ANY)],
        out_specs=[VMEM] * (2 + cuts),
        scratch_shapes=[
            pltpu.VMEM((rows, features), jnp.bfloat16),
            pltpu.VMEM((rows, features), jnp.bfloat16),
            pltpu.VMEM((chunks, features, width), jnp.bfloat16),
            pltpu.SemaphoreType.DMA((chunks,)),
        ],
        compiler_params=pltpu.CompilerParams(vmem_limit_bytes=48 * 1024 * 1024),
        cost_estimate=pl.CostEstimate(
            flops=2 * rows * features * outputs,
            bytes_accessed=2 * (features + rows) * outputs,
            transcendentals=0,
        ),
        name="project",
    )(turn, span_live, *parts, out_weight, after)


def add_kernel(cuts, kept_ref, *refs):
    come_refs, out_refs = refs[:cuts], refs[cuts:]
    width = kept_ref.shape[2] // cuts
    for k in range(kept_ref.shape[0] - 1):
        for cut, come_ref in enumerate(come_refs):
            kept = kept_ref[k + 1, :, cut * width : (cut + 1) * width].astype(jnp.float32)
            out_refs[k * cuts + cut][...] = (kept + come_ref[k].astype(jnp.float32)).astype(
                jnp.bfloat16
            )


def total_kernel(counts, *refs):
    out_ref = refs[-1]
    block, width = out_ref.shape[0] // HALVES, out_ref.shape[1]
    first = 0
    for h, (others, cuts) in enumerate(counts):
        kept_ref, near_ref = refs[first : first + 2]
        arrived = refs[first + 2 : first + 2 + others]
        first += 2 + others
        for cut in range(cuts):
            at = slice(cut * width // cuts, (cut + 1) * width // cuts)
            total = kept_ref[0, :, at].astype(jnp.float32) + near_ref[:, at].astype(jnp.float32)
            for ref in arrived[cut::cuts]:
                total += ref[...].astype(jnp.float32)
            out_ref[h * block : (h + 1) * block, at] = total.astype(jnp.bfloat16)


def add_cores(near, aways, keep, members):
    chips, block, outputs = keep.shape
    cuts = len(aways)
    shape = jax.ShapeDtypeStruct((block, outputs // cuts), jnp.bfloat16)
    pairs = [(i, i ^ 1) for i in range(members)]
    come = [lax.ppermute(away, "tp", pairs) for away in aways]
    near = lax.ppermute(near, "tp", pairs)
    sums = pl.pallas_call(
        functools.partial(add_kernel, cuts),
        out_shape=[shape] * ((chips - 1) * cuts),
        in_specs=[VMEM] * (1 + cuts),
        out_specs=[VMEM] * ((chips - 1) * cuts),
        compiler_params=pltpu.CompilerParams(vmem_limit_bytes=VMEM_LIMIT),
        name="add_cores",
    )(keep, *come)
    return near, sums


def add_chips(sums, cuts, members):
    return [
        lax.ppermute(
            each, "tp", [(i, (i + 2 * (n // cuts + 1)) % members) for i in range(members)]
        )
        for n, each in enumerate(sums)
    ]


def total_sums(terms, counts, block, outputs):
    return pl.pallas_call(
        functools.partial(total_kernel, counts),
        out_shape=jax.ShapeDtypeStruct((HALVES * block, outputs), jnp.bfloat16),
        in_specs=[VMEM] * len(terms),
        out_specs=VMEM,
        compiler_params=pltpu.CompilerParams(vmem_limit_bytes=VMEM_LIMIT),
        name="total",
    )(*terms)


def pack_kernel(me_ref, span_live_ref, owners_ref, span_ref, *refs):
    out_refs, (out_ref, counts_ref) = refs[:-2], refs[-2:]
    peers = out_ref.shape[0]
    block_rows, head_dim = out_ref.shape[3:]
    out_ref[...] = jnp.zeros_like(out_ref)
    for k in range(peers):
        counts_ref[k] = 0
    row = lax.broadcasted_iota(jnp.int32, (block_rows, head_dim), 0)
    for b in range(span_ref.shape[1] // block_rows):
        owner = owners_ref[b]
        rank = counts_ref[owner]
        counts_ref[owner] = rank + 1
        keep = row + b * block_rows < span_live_ref[0]
        for side in range(2):
            block = span_ref[side, b * block_rows : (b + 1) * block_rows, :]
            out_ref[owner, side, rank] = jnp.where(keep, block, jnp.zeros_like(block))
    for k, each_ref in enumerate(out_refs):
        each_ref[...] = out_ref[me_ref[0] ^ k]


def unpack_kernel(me_ref, *refs):
    for k, each_ref in enumerate(refs[:-1]):
        refs[-1][:, me_ref[0] ^ k] = each_ref[...]


def shards(
    queries,
    cache_store,
    span_cache,
    out_weight,
    prefix_blocks,
    span_lengths,
    hit_holders,
    hit_slots,
    store_owners,
):
    peers = lax.axis_size("inst")
    block_rows, head_dim = cache_store.shape[2:]
    rows, columns = queries.shape
    heads = columns // head_dim
    block_max = hit_slots.shape[1]
    cap = max(2, block_max * 5 // (4 * peers))
    new_count = rows // block_rows
    push_cap = max(2, 2 * new_count // peers)
    scale = math.log2(math.e) / math.sqrt(head_dim)
    me = lax.axis_index("inst").reshape(1)
    width = round_up(cap + 1, 128)
    members = lax.axis_size("tp")
    some = rows // HALVES
    part_shape = jax.ShapeDtypeStruct((some + TAIL, columns), jnp.bfloat16)
    params = pltpu.CompilerParams(vmem_limit_bytes=VMEM_LIMIT)
    anywhere = pl.BlockSpec(memory_space=pl.ANY)

    def exchange(value, bit):
        return lax.ppermute(value, "inst", [(i, i ^ bit) for i in range(peers)])

    order = sorted(range(1, peers), key=lambda k: -(k & -k))

    def spread(loaded, after):
        held = {0: loaded}
        for k in order:
            source = held[k & (k - 1)]
            if k & (k - 1):
                source, after = lax.optimization_barrier((source, after))
            held[k] = exchange(source, k & -k)
        return held, after

    def guests(held, group, after):
        return pl.pallas_call(
            functools.partial(guest_kernel, scale, width, some, len(group)),
            out_shape=[part_shape] * len(group),
            in_specs=[SMEM] + [VMEM] * (len(group) + 1) + [anywhere],
            out_specs=[VMEM] * len(group),
            scratch_shapes=[
                pltpu.VMEM((len(group), width), jnp.int32),
                pltpu.SMEM((len(group), width), jnp.int32),
                pltpu.SemaphoreType.DMA,
                *attention_scratch(heads, some, head_dim, block_rows),
            ],
            compiler_params=params,
            cost_estimate=attention_cost(some, rows // 2, head_dim, heads),
            name="guest_attention",
        )(me, *[held[k] for k in group], cache_store, after)

    def gather_back(parts, after):
        parts = dict(parts)
        for k in reversed(order):
            arrived = [exchange(parts[c], c & -c) for c in order if c & (c - 1) == k]
            if arrived:
                parts[k] = after = pl.pallas_call(
                    functools.partial(merge_kernel, heads, len(arrived) + 1),
                    out_shape=part_shape,
                    in_specs=[VMEM] * (len(arrived) + 1) + [anywhere],
                    out_specs=VMEM,
                    compiler_params=params,
                    name="merge",
                )(parts[k], *arrived, after)
        parts[1], after = lax.optimization_barrier((parts[1], after))
        return [exchange(parts[k], k) for k in order if k & (k - 1) == 0], after

    lists, *loaded = route(
        prefix_blocks, hit_holders.reshape(1, -1), hit_slots, queries, peers, width, members
    )
    own = pl.pallas_call(
        functools.partial(own_kernel, scale, members),
        out_shape=[part_shape] * HALVES,
        in_specs=[SMEM, SMEM, SMEM, HBM, HBM, HBM],
        out_specs=[VMEM] * HALVES,
        scratch_shapes=[
            pltpu.VMEM((HALVES, some, columns), jnp.bfloat16),
            pltpu.VMEM(cache_store.shape, jnp.bfloat16),
            pltpu.VMEM(span_cache.shape, jnp.bfloat16),
            pltpu.SemaphoreType.DMA((2 + HALVES * members,)),
            *attention_scratch(heads, rows, head_dim, block_rows),
        ],
        compiler_params=params,
        cost_estimate=attention_cost(rows, 8 * rows, head_dim, heads),
        name="own_attention",
    )(me, span_lengths, lists, queries, cache_store, span_cache)

    own = list(own)
    before, arrived = None, []
    held, after = spread(loaded[0], own[0])
    for h in range(HALVES):
        if h + 1 < HALVES:
            loaded[h + 1], after = lax.optimization_barrier((loaded[h + 1], after))
            groups = [order[i : i + 2] for i in range(0, peers - 1, 2)]
        else:
            groups = [[k] for k in reversed(order) if k > 1] + [[1]]
        parts, following = {}, None
        for index, group in enumerate(groups):
            results = guests(held, group, after)
            after = results[0]
            parts.update(zip(group, results))
            if index == 0 and h + 1 < HALVES:
                following, after = spread(loaded[h + 1], after)
            if index == 0 and before is not None:
                back, after = gather_back(before, after)
                arrived.append(back)
        before, held = parts, following
    back, after = gather_back(before, after)
    arrived.append(back)

    push_shape = jax.ShapeDtypeStruct((2, push_cap, block_rows, head_dim), jnp.bfloat16)
    outgoing = pl.pallas_call(
        pack_kernel,
        out_shape=[push_shape] * peers,
        in_specs=[SMEM, SMEM, SMEM, VMEM],
        out_specs=[VMEM] * peers,
        scratch_shapes=[
            pltpu.VMEM((peers, *push_shape.shape), jnp.bfloat16),
            pltpu.SMEM((peers,), jnp.int32),
        ],
        compiler_params=params,
        name="pack_blocks",
    )(me, span_lengths, store_owners.reshape(-1), span_cache)
    turn = lax.axis_index("tp").reshape(1)
    terms, counts = [], []
    for h in range(HALVES):
        if h == 0:
            own[h], *outgoing = lax.optimization_barrier((own[h], *outgoing))
        parts = [own[h], *arrived[h]]
        cuts = 2 if h + 1 < HALVES else 1
        near, *aways, keep = project(
            turn, span_lengths, parts, out_weight, after, heads, h, members, cuts
        )
        near, sums = add_cores(near, aways, keep, members)
        crossed = add_chips(sums, cuts, members)
        if h + 1 < HALVES:
            own[h + 1], *crossed = lax.optimization_barrier((own[h + 1], *crossed))
        terms += [keep, near, *crossed]
        counts.append((len(crossed), cuts))
    keep, *outgoing = lax.optimization_barrier((keep, *outgoing))
    projected = total_sums(terms, counts, some // members, out_weight.shape[1])

    incoming = [outgoing[0], *[exchange(outgoing[k], k) for k in range(1, peers)]]
    pushed_blocks = pl.pallas_call(
        unpack_kernel,
        out_shape=jax.ShapeDtypeStruct(
            (2, peers, push_cap, block_rows, head_dim), jnp.bfloat16
        ),
        in_specs=[SMEM] + [VMEM] * peers,
        out_specs=VMEM,
        compiler_params=params,
        name="unpack_blocks",
    )(me, *incoming).reshape(2, peers * push_cap, block_rows, head_dim)
    return (projected, pushed_blocks)


def solution(mesh):
    return jax.shard_map(
        shards,
        mesh=mesh,
        in_specs=(
            P(("pods", "inst"), "tp"),
            P(None, ("pods", "inst"), None, "tp"),
            P(None, ("pods", "inst"), "tp"),
            P("tp", None),
            P(("pods", "inst")),
            P(("pods", "inst")),
            P(("pods", "inst"), None, None),
            P(("pods", "inst"), None),
            P(("pods", "inst"), None, None),
        ),
        out_specs=(P(("pods", "inst", "tp"), None), P(None, ("pods", "inst"), None, "tp")),
        check_vma=False,
    )
```

```python
import functools
import math

import jax
import jax.numpy as jnp
from jax import lax
from jax.experimental import pallas as pl
from jax.experimental.pallas import tpu as pltpu
from jax.sharding import PartitionSpec as P

LOW = -1e30
TOP = 2.0**100
TILE = 16
STACK = 512
HALVES = 2
TAIL = 8
VMEM_LIMIT = 20 * 1024 * 1024

SMEM = pl.BlockSpec(memory_space=pltpu.SMEM)
VMEM = pl.BlockSpec(memory_space=pltpu.VMEM)
HBM = pl.BlockSpec(memory_space=pltpu.HBM)


def round_up(number, step):
    return -(-number // step) * step


def original_row(row, h, members, own_rows):
    each = own_rows // HALVES
    member = sum((row >= m * each).astype(jnp.int32) for m in range(1, members))
    return row + member * (own_rows - each) + h * each


def route_kernel(
    members, live_ref, holders_in, slots_in, q_in, lists_ref, *refs
):
    out_refs, (holders_ref, slots_ref, sems) = refs[:HALVES], refs[HALVES:]
    columns = q_in.shape[1]
    rows = q_in.shape[0] // HALVES
    each = rows // members
    loading = [
        pltpu.make_async_copy(holders_in, holders_ref, sems.at[0]),
        pltpu.make_async_copy(slots_in, slots_ref, sems.at[1]),
    ]
    passing = [
        pltpu.make_async_copy(
            q_in.at[pl.ds((m * HALVES + h) * each, each)],
            out_refs[h].at[pl.ds(m * each, each)],
            sems.at[2 + h * members + m],
        )
        for h in range(HALVES)
        for m in range(members)
    ]
    for copy in loading + passing:
        copy.start()
    for copy in loading:
        copy.wait()
    peers, width = lists_ref.shape
    number = holders_ref.shape[1]
    padded = round_up(peers, 16)
    holder = lax.broadcasted_iota(jnp.int32, (padded, number), 0)
    entry = lax.broadcasted_iota(jnp.int32, (padded, number), 1)
    hot = (holders_ref[...] == holder) & (entry < live_ref[0])
    ones = jnp.where(hot, 1.0, 0.0)
    earlier = lax.broadcasted_iota(jnp.int32, (number, number), 0) < lax.broadcasted_iota(
        jnp.int32, (number, number), 1
    )
    ranks = jnp.dot(
        ones.astype(jnp.bfloat16),
        jnp.where(earlier, 1.0, 0.0).astype(jnp.bfloat16),
        preferred_element_type=jnp.float32,
    )
    rank = jnp.sum(ranks * ones, axis=0, keepdims=True)
    rank = jnp.broadcast_to(rank, (8, number)).T[:, :1].astype(jnp.int32)
    place = lax.broadcasted_iota(jnp.int32, (number, width), 1) == rank
    slots = jnp.where(hot, slots_ref[...], 0).astype(jnp.float32)
    lists = jnp.dot(
        slots.astype(jnp.bfloat16),
        jnp.where(place, 1.0, 0.0).astype(jnp.bfloat16),
        preferred_element_type=jnp.float32,
    )
    counts = jnp.sum(ones, axis=1, keepdims=True)
    last = lax.broadcasted_iota(jnp.int32, (padded, width), 1) == width - 1
    lists = jnp.where(last, counts, lists)[:peers]
    lists_ref[...] = lists.astype(jnp.int32)

    lines = columns // width
    row = lax.broadcasted_iota(jnp.int32, (TAIL, columns), 0)
    tail = jnp.zeros((TAIL, columns), jnp.float32)
    for r in range(-(-peers // lines)):
        line = [lists[h : h + 1] for h in range(r * lines, min(peers, (r + 1) * lines))]
        line += [jnp.zeros((1, width), jnp.float32)] * (lines - len(line))
        tail = jnp.where(row == r, jnp.concatenate(line, axis=1), tail)
    for out_ref in out_refs:
        out_ref[rows:, :] = tail.astype(jnp.bfloat16)
    for copy in passing:
        copy.wait()


def route(live, holders, slots, queries, peers, width, members):
    rows, columns = queries.shape[0] // HALVES, queries.shape[1]
    return pl.pallas_call(
        functools.partial(route_kernel, members),
        out_shape=(
            jax.ShapeDtypeStruct((peers, width), jnp.int32),
            *[jax.ShapeDtypeStruct((rows + TAIL, columns), jnp.bfloat16)] * HALVES,
        ),
        in_specs=[SMEM, HBM, HBM, HBM],
        out_specs=[VMEM] * (1 + HALVES),
        scratch_shapes=[
            pltpu.VMEM(holders.shape, jnp.int32),
            pltpu.VMEM(slots.shape, jnp.int32),
            pltpu.SemaphoreType.DMA((2 + HALVES * members,)),
        ],
        compiler_params=pltpu.CompilerParams(vmem_limit_bytes=62 * 1024 * 1024),
        name="route",
    )(live, holders, slots, queries)


def score(q, keys):
    return lax.dot_general(q, keys, (((1,), (1,)), ((), ())), preferred_element_type=jnp.float32)


def twice(value):
    return jnp.concatenate([value, value], axis=1)


def attend(
    slot, count, store_ref, span_ref, masks, q_ref, k_ref, v_ref, s_ref, ref_ref, acc_ref, rows,
    scale, stored=None,
):
    block_rows, head_dim = store_ref.shape[2:]
    heads = q_ref.shape[0] // rows
    stack = s_ref.shape[0]
    stacks = q_ref.shape[0] // stack
    tiles = (count + TILE - 1) // TILE

    def fetch(tile, into):
        for j in range(TILE):
            index = tile * TILE + j
            here = slot(jnp.maximum(jnp.minimum(index, count - 1), 0))
            at = slice(j * block_rows, (j + 1) * block_rows)
            k_ref[into, at, :] = store_ref[0, here]
            block = store_ref[1, here]
            v_ref[into, at, :head_dim] = jnp.where(index < count, block, jnp.zeros_like(block))
            v_ref[into, at, head_dim:] = jnp.where(
                index < count, jnp.ones_like(block), jnp.zeros_like(block)
            )

    def start():
        if span_ref is None:
            acc_ref[...] = jnp.zeros_like(acc_ref)
            return
        keys = span_ref.shape[1]
        values = jnp.concatenate(
            [span_ref[1], jnp.ones((keys, head_dim), jnp.bfloat16)], axis=1
        )
        s = score(q_ref[:rows, :], span_ref[0])
        for g in range(heads):
            at = slice(g * rows, (g + 1) * rows)
            if g + 1 < heads:
                following = score(q_ref[(g + 1) * rows : (g + 2) * rows, :], span_ref[0])
            s = jnp.where(masks[g * HALVES // heads], s, LOW)
            top = jnp.max(s, axis=1, keepdims=True)
            ref_ref[at, :] = jnp.broadcast_to(top, (rows, head_dim))
            p = jnp.exp2((s - top) * scale).astype(jnp.bfloat16)
            acc_ref[at, :] = jnp.dot(p, values, preferred_element_type=jnp.float32)
            s = following

    start()
    if stored is not None:
        stored()

    @pl.when(count > 0)
    def _():
        fetch(0, 0)
        if span_ref is None:
            few = score(q_ref[...], k_ref[0, : 8 * block_rows, :])
            ref_ref[...] = jnp.broadcast_to(
                jnp.max(few, axis=1, keepdims=True), ref_ref.shape
            )
        s_ref[...] = score(q_ref[:stack, :], k_ref[0])

        def step(tile, carry):
            now = lax.rem(tile, 2)
            later = 1 - now
            keys, values = k_ref[now], v_ref[now]
            s = s_ref[...]
            fetch(tile + 1, later)
            for c in range(stacks):
                at = slice(c * stack, (c + 1) * stack)
                if c + 1 < stacks:
                    following = score(q_ref[(c + 1) * stack : (c + 2) * stack, :], keys)
                else:
                    s_ref[...] = score(q_ref[:stack, :], k_ref[later])
                p = jnp.exp2((s - twice(ref_ref[at, :])) * scale).astype(jnp.bfloat16)
                acc_ref[at, :] += jnp.dot(p, values, preferred_element_type=jnp.float32)
                s = following
            return carry

        lax.fori_loop(0, tiles, step, 0)
        beyond = jnp.max(jnp.where(acc_ref[:, head_dim:] < TOP, 0.0, 1.0))

        @pl.when(beyond > 0.0)
        def _():
            start()
            if span_ref is None:
                ref_ref[...] = jnp.full_like(ref_ref, LOW)

            def careful(tile, carry):
                fetch(tile, 0)

                def head(g, inner):
                    at = pl.ds(pl.multiple_of(g * rows, rows), rows)
                    s = score(q_ref[at, :], k_ref[0])
                    old = ref_ref[at, :]
                    new = jnp.maximum(old, jnp.max(s, axis=1, keepdims=True))
                    p = jnp.exp2((s - twice(new)) * scale).astype(jnp.bfloat16)
                    update = jnp.dot(p, v_ref[0], preferred_element_type=jnp.float32)
                    acc_ref[at, :] = (
                        acc_ref[at, :] * twice(jnp.exp2((old - new) * scale)) + update
                    )
                    ref_ref[at, :] = new
                    return inner

                return lax.fori_loop(0, heads, head, carry)

            lax.fori_loop(0, tiles, careful, 0)


def stack_heads(queries_ref, q_ref, rows, first=0):
    head_dim = q_ref.shape[1]
    for g in range(queries_ref.shape[1] // head_dim):
        q_ref[(first + g) * rows : (first + g + 1) * rows, :] = queries_ref[
            :rows, g * head_dim : (g + 1) * head_dim
        ]


def write_logs(out_ref, logs):
    heads, rows = logs.shape
    first = logs.astype(jnp.bfloat16).astype(jnp.float32)
    rest = logs - first
    second = rest.astype(jnp.bfloat16).astype(jnp.float32)
    third = rest - second
    spare = jnp.zeros((heads, out_ref.shape[1] - 3 * rows), jnp.float32)
    lines = jnp.concatenate([first, second, third, spare], axis=1)
    if heads < TAIL:
        more = jnp.zeros((TAIL - heads, out_ref.shape[1]), jnp.float32)
        lines = jnp.concatenate([lines, more], axis=0)
    out_ref[rows:, :] = lines.astype(jnp.bfloat16)


def read_logs(part_ref, heads, rows):
    lines = part_ref[rows:, :].astype(jnp.float32)[:heads]
    return lines[:, :rows] + lines[:, rows : 2 * rows] + lines[:, 2 * rows : 3 * rows]


def finish(out_refs, ref_ref, acc_ref, rows, scale):
    head_dim = ref_ref.shape[1]
    heads = ref_ref.shape[0] // rows // len(out_refs)
    lane = lax.broadcasted_iota(jnp.int32, (rows, head_dim), 1)
    for h, out_ref in enumerate(out_refs):
        logs = jnp.zeros((rows, head_dim), jnp.float32)
        for g in range(heads):
            at = slice((h * heads + g) * rows, (h * heads + g + 1) * rows)
            total = acc_ref[at, head_dim:]
            out_ref[:rows, g * head_dim : (g + 1) * head_dim] = (
                acc_ref[at, :head_dim] / total
            ).astype(jnp.bfloat16)
            logs = jnp.where(lane == g, ref_ref[at, :] * scale + jnp.log2(total), logs)
        write_logs(out_ref, logs.T[:heads])


def own_kernel(
    scale, members, me_ref, span_live_ref, lists_ref, queries_in, store_in, span_in, *refs
):
    out_refs = refs[:HALVES]
    queries_ref, store_ref, span_ref, sems, q_ref, k_ref, v_ref, s_ref, ref_ref, acc_ref = refs[
        HALVES:
    ]
    me = me_ref[0]
    rows = queries_ref.shape[1]
    each = rows // members
    copies = [
        pltpu.make_async_copy(span_in, span_ref, sems.at[0]),
        pltpu.make_async_copy(store_in, store_ref, sems.at[1]),
    ] + [
        pltpu.make_async_copy(
            queries_in.at[pl.ds((m * HALVES + h) * each, each)],
            queries_ref.at[h, pl.ds(m * each, each)],
            sems.at[2 + h * members + m],
        )
        for h in range(HALVES)
        for m in range(members)
    ]
    for copy in copies:
        copy.start()
    keys = span_ref.shape[1]
    key = lax.broadcasted_iota(jnp.int32, (rows, keys), 1)
    row = lax.broadcasted_iota(jnp.int32, (rows, keys), 0)
    masks = [
        (key <= original_row(row, h, members, each * HALVES)) & (key < span_live_ref[0])
        for h in range(HALVES)
    ]
    for copy in copies[2:]:
        copy.wait()
    for h in range(HALVES):
        stack_heads(queries_ref.at[h], q_ref, rows, h * queries_ref.shape[2] // q_ref.shape[1])
    copies[0].wait()
    attend(
        lambda index: lists_ref[me, index], lists_ref[me, lists_ref.shape[1] - 1], store_ref,
        span_ref, masks, q_ref, k_ref, v_ref, s_ref, ref_ref, acc_ref, rows, scale,
        copies[1].wait,
    )
    finish(out_refs, ref_ref, acc_ref, rows, scale)


def guest_kernel(scale, width, rows, number, me_ref, *refs):
    loaded_refs, store_ref = refs[:number], refs[number]
    out_refs = refs[number + 2 : 2 * number + 2]
    wide_ref, list_ref, sem_ref, q_ref, k_ref, v_ref, s_ref, ref_ref, acc_ref = refs[
        2 * number + 2 :
    ]
    each = loaded_refs[0].shape[1] // width
    me = me_ref[0]
    lane = pl.multiple_of(lax.rem(me, each) * width, 128)
    for which, loaded_ref in enumerate(loaded_refs):
        riders = loaded_ref[rows:, pl.ds(lane, width)].astype(jnp.float32)
        row = lax.broadcasted_iota(jnp.int32, riders.shape, 0)
        mine = jnp.sum(jnp.where(row == me // each, riders, 0.0), axis=0, keepdims=True)
        wide_ref[which : which + 1, :] = mine.astype(jnp.int32)
    copy = pltpu.make_async_copy(wide_ref, list_ref, sem_ref)
    copy.start()
    stack_heads(loaded_refs[0], q_ref, rows)
    copy.wait()
    for which, (loaded_ref, out_ref) in enumerate(zip(loaded_refs, out_refs)):
        count = list_ref[which, width - 1]

        @pl.when(count > 0)
        def _():
            if which:
                stack_heads(loaded_ref, q_ref, rows)
            attend(
                lambda index: list_ref[which, index], count, store_ref, None, None,
                q_ref, k_ref, v_ref, s_ref, ref_ref, acc_ref, rows, scale,
            )
            finish([out_ref], ref_ref, acc_ref, rows, scale)

        @pl.when(count == 0)
        def _():
            out_ref[...] = jnp.zeros_like(out_ref)
            write_logs(out_ref, jnp.full((q_ref.shape[0] // rows, rows), LOW, jnp.float32))


def attention_scratch(heads, rows, head_dim, block_rows):
    keys = TILE * block_rows
    return [
        pltpu.VMEM((heads * rows, head_dim), jnp.bfloat16),
        pltpu.VMEM((2, keys, head_dim), jnp.bfloat16),
        pltpu.VMEM((2, keys, 2 * head_dim), jnp.bfloat16),
        pltpu.VMEM((math.gcd(heads * rows, STACK), keys), jnp.float32),
        pltpu.VMEM((heads * rows, head_dim), jnp.float32),
        pltpu.VMEM((heads * rows, 2 * head_dim), jnp.float32),
    ]


def attention_cost(rows, keys, head_dim, heads):
    return pl.CostEstimate(
        flops=4 * rows * keys * head_dim * heads,
        bytes_accessed=64 * 1024,
        transcendentals=rows * keys * heads,
    )


def merged(parts, heads, rows):
    logs = [read_logs(part, heads, rows) for part in parts]
    top = functools.reduce(jnp.maximum, logs)
    weights = [jnp.exp2(log - top) for log in logs]
    total = functools.reduce(jnp.add, weights)
    return [weight / total for weight in weights], top + jnp.log2(total)


def weighted(parts, weights, g, head_dim, rows):
    total = jnp.zeros((rows, head_dim), jnp.float32)
    for part, weight in zip(parts, weights):
        part_rows = part[:rows, g * head_dim : (g + 1) * head_dim]
        total += part_rows.astype(jnp.float32) * weight[:, g : g + 1]
    return total.astype(jnp.bfloat16)


def merge_kernel(heads, number, *refs):
    parts, out_ref = refs[:number], refs[number + 1]
    rows = out_ref.shape[0] - TAIL
    head_dim = out_ref.shape[1] // heads
    weights, logs = merged(parts, heads, rows)
    weights = [weight.T for weight in weights]
    for g in range(heads):
        out_ref[:rows, g * head_dim : (g + 1) * head_dim] = weighted(
            parts, weights, g, head_dim, rows
        )
    write_logs(out_ref, logs)


def project_kernel(heads, number, h, members, cuts, turn_ref, span_live_ref, *refs):
    parts = refs[:number]
    weight_ref, after_ref, near_ref, *away_refs = refs[number : number + 3 + cuts]
    keep_ref, att_ref, sorted_ref, held_ref, sems = refs[number + 3 + cuts :]
    rows, features = att_ref.shape
    chunks, _, width = held_ref.shape
    head_dim = features // heads
    copies = [
        pltpu.make_async_copy(weight_ref.at[:, pl.ds(i * width, width)], held_ref.at[i], sems.at[i])
        for i in range(chunks)
    ]
    for copy in copies:
        copy.start()

    row = lax.broadcasted_iota(jnp.int32, (heads, rows), 1)
    live = original_row(row, h, members, rows * HALVES // members) < span_live_ref[0]
    weights, _ = merged(parts, heads, rows)
    weights = [jnp.where(live, weight, 0.0).T for weight in weights]
    for g in range(heads):
        att_ref[:, g * head_dim : (g + 1) * head_dim] = weighted(
            parts, weights, g, head_dim, rows
        )

    chips = keep_ref.shape[0]
    block = keep_ref.shape[1]
    chip, core = turn_ref[0] // 2, lax.rem(turn_ref[0], 2)
    for side, wanted in enumerate((1 - core, core)):
        for k in range(chips):
            owner = 2 * lax.rem(chip + k, chips) + wanted
            at = (side * chips + k) * block
            sorted_ref[at : at + block, :] = att_ref[
                pl.ds(pl.multiple_of(owner * block, block), block), :
            ]
    for i in range(chunks):
        copies[i].wait()
        at = slice(i * width, (i + 1) * width)
        product = jnp.dot(
            sorted_ref[...], held_ref[i], preferred_element_type=jnp.float32
        ).astype(jnp.bfloat16)
        for k in range(chips):
            leaving = product[k * block : (k + 1) * block]
            if k:
                cut = i * cuts // chunks
                first = i * width - cut * away_refs[cut].shape[2]
                away_refs[cut][k - 1, :, first : first + width] = leaving
            else:
                near_ref[:, at] = leaving
            keep_ref[k, :, at] = product[(chips + k) * block : (chips + k + 1) * block]


def project(turn, span_live, parts, out_weight, after, heads, h, members, cuts):
    features, outputs = out_weight.shape
    rows = parts[0].shape[0] - TAIL
    width = 512
    chunks = outputs // width
    chips, block = members // 2, rows // members
    return pl.pallas_call(
        functools.partial(project_kernel, heads, len(parts), h, members, cuts),
        out_shape=[
            jax.ShapeDtypeStruct(shape, jnp.bfloat16)
            for shape in (
                (block, outputs),
                *[(chips - 1, block, outputs // cuts)] * cuts,
                (chips, block, outputs),
            )
        ],
        in_specs=[SMEM, SMEM] + [VMEM] * len(parts) + [HBM, pl.BlockSpec(memory_space=pl.ANY)],
        out_specs=[VMEM] * (2 + cuts),
        scratch_shapes=[
            pltpu.VMEM((rows, features), jnp.bfloat16),
            pltpu.VMEM((rows, features), jnp.bfloat16),
            pltpu.VMEM((chunks, features, width), jnp.bfloat16),
            pltpu.SemaphoreType.DMA((chunks,)),
        ],
        compiler_params=pltpu.CompilerParams(vmem_limit_bytes=48 * 1024 * 1024),
        cost_estimate=pl.CostEstimate(
            flops=2 * rows * features * outputs,
            bytes_accessed=2 * (features + rows) * outputs,
            transcendentals=0,
        ),
        name="project",
    )(turn, span_live, *parts, out_weight, after)


def add_kernel(cuts, kept_ref, *refs):
    come_refs, out_refs = refs[:cuts], refs[cuts:]
    width = kept_ref.shape[2] // cuts
    for k in range(kept_ref.shape[0] - 1):
        for cut, come_ref in enumerate(come_refs):
            kept = kept_ref[k + 1, :, cut * width : (cut + 1) * width].astype(jnp.float32)
            out_refs[k * cuts + cut][...] = (kept + come_ref[k].astype(jnp.float32)).astype(
                jnp.bfloat16
            )


def total_kernel(counts, *refs):
    out_ref = refs[-1]
    block, width = out_ref.shape[0] // HALVES, out_ref.shape[1]
    first = 0
    for h, (others, cuts) in enumerate(counts):
        kept_ref, near_ref = refs[first : first + 2]
        arrived = refs[first + 2 : first + 2 + others]
        first += 2 + others
        for cut in range(cuts):
            at = slice(cut * width // cuts, (cut + 1) * width // cuts)
            total = kept_ref[0, :, at].astype(jnp.float32) + near_ref[:, at].astype(jnp.float32)
            for ref in arrived[cut::cuts]:
                total += ref[...].astype(jnp.float32)
            out_ref[h * block : (h + 1) * block, at] = total.astype(jnp.bfloat16)


def add_cores(near, aways, keep, members):
    chips, block, outputs = keep.shape
    cuts = len(aways)
    shape = jax.ShapeDtypeStruct((block, outputs // cuts), jnp.bfloat16)
    pairs = [(i, i ^ 1) for i in range(members)]
    come = [lax.ppermute(away, "tp", pairs) for away in aways]
    near = lax.ppermute(near, "tp", pairs)
    sums = pl.pallas_call(
        functools.partial(add_kernel, cuts),
        out_shape=[shape] * ((chips - 1) * cuts),
        in_specs=[VMEM] * (1 + cuts),
        out_specs=[VMEM] * ((chips - 1) * cuts),
        compiler_params=pltpu.CompilerParams(vmem_limit_bytes=VMEM_LIMIT),
        name="add_cores",
    )(keep, *come)
    return near, sums


def add_chips(sums, cuts, members):
    return [
        lax.ppermute(
            each, "tp", [(i, (i + 2 * (n // cuts + 1)) % members) for i in range(members)]
        )
        for n, each in enumerate(sums)
    ]


def total_sums(terms, counts, block, outputs):
    return pl.pallas_call(
        functools.partial(total_kernel, counts),
        out_shape=jax.ShapeDtypeStruct((HALVES * block, outputs), jnp.bfloat16),
        in_specs=[VMEM] * len(terms),
        out_specs=VMEM,
        compiler_params=pltpu.CompilerParams(vmem_limit_bytes=VMEM_LIMIT),
        name="total",
    )(*terms)


def pack_kernel(me_ref, span_live_ref, owners_ref, span_ref, *refs):
    out_refs, (out_ref, counts_ref) = refs[:-2], refs[-2:]
    peers = out_ref.shape[0]
    block_rows, head_dim = out_ref.shape[3:]
    out_ref[...] = jnp.zeros_like(out_ref)
    for k in range(peers):
        counts_ref[k] = 0
    row = lax.broadcasted_iota(jnp.int32, (block_rows, head_dim), 0)
    for b in range(span_ref.shape[1] // block_rows):
        owner = owners_ref[b]
        rank = counts_ref[owner]
        counts_ref[owner] = rank + 1
        keep = row + b * block_rows < span_live_ref[0]
        for side in range(2):
            block = span_ref[side, b * block_rows : (b + 1) * block_rows, :]
            out_ref[owner, side, rank] = jnp.where(keep, block, jnp.zeros_like(block))
    for k, each_ref in enumerate(out_refs):
        each_ref[...] = out_ref[me_ref[0] ^ k]


def unpack_kernel(me_ref, *refs):
    for k, each_ref in enumerate(refs[:-1]):
        refs[-1][:, me_ref[0] ^ k] = each_ref[...]


def shards(
    queries,
    cache_store,
    span_cache,
    out_weight,
    prefix_blocks,
    span_lengths,
    hit_holders,
    hit_slots,
    store_owners,
):
    peers = lax.axis_size("inst")
    block_rows, head_dim = cache_store.shape[2:]
    rows, columns = queries.shape
    heads = columns // head_dim
    block_max = hit_slots.shape[1]
    cap = max(2, block_max * 5 // (4 * peers))
    new_count = rows // block_rows
    push_cap = max(2, 2 * new_count // peers)
    scale = math.log2(math.e) / math.sqrt(head_dim)
    me = lax.axis_index("inst").reshape(1)
    width = round_up(cap + 1, 128)
    members = lax.axis_size("tp")
    some = rows // HALVES
    part_shape = jax.ShapeDtypeStruct((some + TAIL, columns), jnp.bfloat16)
    params = pltpu.CompilerParams(vmem_limit_bytes=VMEM_LIMIT)
    anywhere = pl.BlockSpec(memory_space=pl.ANY)

    def exchange(value, bit):
        return lax.ppermute(value, "inst", [(i, i ^ bit) for i in range(peers)])

    order = sorted(range(1, peers), key=lambda k: -(k & -k))

    def spread(loaded, after, near=None):
        held = {0: loaded}
        for k in order:
            if k == 1 and near is not None:
                held[k] = near
                continue
            source = held[k & (k - 1)]
            if k & (k - 1):
                source, after = lax.optimization_barrier((source, after))
            held[k] = exchange(source, k & -k)
        return held, after

    def guests(held, group, after):
        return pl.pallas_call(
            functools.partial(guest_kernel, scale, width, some, len(group)),
            out_shape=[part_shape] * len(group),
            in_specs=[SMEM] + [VMEM] * (len(group) + 1) + [anywhere],
            out_specs=[VMEM] * len(group),
            scratch_shapes=[
                pltpu.VMEM((len(group), width), jnp.int32),
                pltpu.SMEM((len(group), width), jnp.int32),
                pltpu.SemaphoreType.DMA,
                *attention_scratch(heads, some, head_dim, block_rows),
            ],
            compiler_params=params,
            cost_estimate=attention_cost(some, rows // 2, head_dim, heads),
            name="guest_attention",
        )(me, *[held[k] for k in group], cache_store, after)

    def gather_back(parts, after):
        parts = dict(parts)
        for k in reversed(order):
            arrived = [exchange(parts[c], c & -c) for c in order if c & (c - 1) == k]
            if arrived:
                parts[k] = after = pl.pallas_call(
                    functools.partial(merge_kernel, heads, len(arrived) + 1),
                    out_shape=part_shape,
                    in_specs=[VMEM] * (len(arrived) + 1) + [anywhere],
                    out_specs=VMEM,
                    compiler_params=params,
                    name="merge",
                )(parts[k], *arrived, after)
        parts[1], after = lax.optimization_barrier((parts[1], after))
        return [exchange(parts[k], k) for k in order if k & (k - 1) == 0], after

    lists, *loaded = route(
        prefix_blocks, hit_holders.reshape(1, -1), hit_slots, queries, peers, width, members
    )
    own = pl.pallas_call(
        functools.partial(own_kernel, scale, members),
        out_shape=[part_shape] * HALVES,
        in_specs=[SMEM, SMEM, SMEM, HBM, HBM, HBM],
        out_specs=[VMEM] * HALVES,
        scratch_shapes=[
            pltpu.VMEM((HALVES, some, columns), jnp.bfloat16),
            pltpu.VMEM(cache_store.shape, jnp.bfloat16),
            pltpu.VMEM(span_cache.shape, jnp.bfloat16),
            pltpu.SemaphoreType.DMA((2 + HALVES * members,)),
            *attention_scratch(heads, rows, head_dim, block_rows),
        ],
        compiler_params=params,
        cost_estimate=attention_cost(rows, 8 * rows, head_dim, heads),
        name="own_attention",
    )(me, span_lengths, lists, queries, cache_store, span_cache)

    own = list(own)
    before, arrived = None, []
    held, after = spread(loaded[0], own[0])
    nears = [None] + [exchange(each, 1) for each in loaded[1:]]
    *loaded[1:], after = lax.optimization_barrier((*loaded[1:], after))
    after, *nears[1:] = lax.optimization_barrier((after, *nears[1:]))
    for h in range(HALVES):
        if h + 1 < HALVES:
            groups = [order[i : i + 2] for i in range(0, peers - 1, 2)]
        else:
            groups = [[k] for k in reversed(order) if k > 1] + [[1]]
        parts, following = {}, None
        for index, group in enumerate(groups):
            results = guests(held, group, after)
            after = results[0]
            parts.update(zip(group, results))
            if index == 0 and h + 1 < HALVES:
                following, after = spread(loaded[h + 1], after, nears[h + 1])
            if index == 0 and before is not None:
                back, after = gather_back(before, after)
                arrived.append(back)
        before, held = parts, following
    back, after = gather_back(before, after)
    arrived.append(back)

    push_shape = jax.ShapeDtypeStruct((2, push_cap, block_rows, head_dim), jnp.bfloat16)
    outgoing = pl.pallas_call(
        pack_kernel,
        out_shape=[push_shape] * peers,
        in_specs=[SMEM, SMEM, SMEM, VMEM],
        out_specs=[VMEM] * peers,
        scratch_shapes=[
            pltpu.VMEM((peers, *push_shape.shape), jnp.bfloat16),
            pltpu.SMEM((peers,), jnp.int32),
        ],
        compiler_params=params,
        name="pack_blocks",
    )(me, span_lengths, store_owners.reshape(-1), span_cache)
    turn = lax.axis_index("tp").reshape(1)
    terms, counts = [], []
    for h in range(HALVES):
        if h == 0:
            own[h], *outgoing = lax.optimization_barrier((own[h], *outgoing))
        parts = [own[h], *arrived[h]]
        cuts = 2 if h + 1 < HALVES else 1
        near, *aways, keep = project(
            turn, span_lengths, parts, out_weight, after, heads, h, members, cuts
        )
        near, sums = add_cores(near, aways, keep, members)
        if h + 1 == HALVES:
            near, *sums = lax.optimization_barrier((near, *sums))
        crossed = add_chips(sums, cuts, members)
        if h + 1 < HALVES:
            own[h + 1], near, crossed[0] = lax.optimization_barrier(
                (own[h + 1], near, crossed[0])
            )
        terms += [keep, near, *crossed]
        counts.append((len(crossed), cuts))
    keep, *outgoing = lax.optimization_barrier((keep, *outgoing))
    projected = total_sums(terms, counts, some // members, out_weight.shape[1])

    incoming = [outgoing[0], *[exchange(outgoing[k], k) for k in range(1, peers)]]
    pushed_blocks = pl.pallas_call(
        unpack_kernel,
        out_shape=jax.ShapeDtypeStruct(
            (2, peers, push_cap, block_rows, head_dim), jnp.bfloat16
        ),
        in_specs=[SMEM] + [VMEM] * peers,
        out_specs=VMEM,
        compiler_params=params,
        name="unpack_blocks",
    )(me, *incoming).reshape(2, peers * push_cap, block_rows, head_dim)
    return (projected, pushed_blocks)


def solution(mesh):
    return jax.shard_map(
        shards,
        mesh=mesh,
        in_specs=(
            P(("pods", "inst"), "tp"),
            P(None, ("pods", "inst"), None, "tp"),
            P(None, ("pods", "inst"), "tp"),
            P("tp", None),
            P(("pods", "inst")),
            P(("pods", "inst")),
            P(("pods", "inst"), None, None),
            P(("pods", "inst"), None),
            P(("pods", "inst"), None, None),
        ),
        out_specs=(P(("pods", "inst", "tp"), None), P(None, ("pods", "inst"), None, "tp")),
        check_vma=False,
    )
```

```python
import functools
import math

import jax
import jax.numpy as jnp
from jax import lax
from jax.experimental import pallas as pl
from jax.experimental.pallas import tpu as pltpu
from jax.sharding import PartitionSpec as P

LOW = -1e30
TOP = 2.0**100
TILE = 16
STACK = 512
HALVES = 2
TAIL = 8
VMEM_LIMIT = 20 * 1024 * 1024

SMEM = pl.BlockSpec(memory_space=pltpu.SMEM)
VMEM = pl.BlockSpec(memory_space=pltpu.VMEM)
HBM = pl.BlockSpec(memory_space=pltpu.HBM)


def round_up(number, step):
    return -(-number // step) * step


def original_row(row, h, members, own_rows):
    each = own_rows // HALVES
    member = sum((row >= m * each).astype(jnp.int32) for m in range(1, members))
    return row + member * (own_rows - each) + h * each


def route_kernel(
    members, live_ref, holders_in, slots_in, q_in, lists_ref, *refs
):
    out_refs, (holders_ref, slots_ref, sems) = refs[:HALVES], refs[HALVES:]
    columns = q_in.shape[1]
    rows = q_in.shape[0] // HALVES
    each = rows // members
    loading = [
        pltpu.make_async_copy(holders_in, holders_ref, sems.at[0]),
        pltpu.make_async_copy(slots_in, slots_ref, sems.at[1]),
    ]
    passing = [
        pltpu.make_async_copy(
            q_in.at[pl.ds((m * HALVES + h) * each, each)],
            out_refs[h].at[pl.ds(m * each, each)],
            sems.at[2 + h * members + m],
        )
        for h in range(HALVES)
        for m in range(members)
    ]
    for copy in loading + passing:
        copy.start()
    for copy in loading:
        copy.wait()
    peers, width = lists_ref.shape
    number = holders_ref.shape[1]
    padded = round_up(peers, 16)
    holder = lax.broadcasted_iota(jnp.int32, (padded, number), 0)
    entry = lax.broadcasted_iota(jnp.int32, (padded, number), 1)
    hot = (holders_ref[...] == holder) & (entry < live_ref[0])
    ones = jnp.where(hot, 1.0, 0.0)
    earlier = lax.broadcasted_iota(jnp.int32, (number, number), 0) < lax.broadcasted_iota(
        jnp.int32, (number, number), 1
    )
    ranks = jnp.dot(
        ones.astype(jnp.bfloat16),
        jnp.where(earlier, 1.0, 0.0).astype(jnp.bfloat16),
        preferred_element_type=jnp.float32,
    )
    rank = jnp.sum(ranks * ones, axis=0, keepdims=True)
    rank = jnp.broadcast_to(rank, (8, number)).T[:, :1].astype(jnp.int32)
    place = lax.broadcasted_iota(jnp.int32, (number, width), 1) == rank
    slots = jnp.where(hot, slots_ref[...], 0).astype(jnp.float32)
    lists = jnp.dot(
        slots.astype(jnp.bfloat16),
        jnp.where(place, 1.0, 0.0).astype(jnp.bfloat16),
        preferred_element_type=jnp.float32,
    )
    counts = jnp.sum(ones, axis=1, keepdims=True)
    last = lax.broadcasted_iota(jnp.int32, (padded, width), 1) == width - 1
    lists = jnp.where(last, counts, lists)[:peers]
    lists_ref[...] = lists.astype(jnp.int32)

    lines = columns // width
    row = lax.broadcasted_iota(jnp.int32, (TAIL, columns), 0)
    tail = jnp.zeros((TAIL, columns), jnp.float32)
    for r in range(-(-peers // lines)):
        line = [lists[h : h + 1] for h in range(r * lines, min(peers, (r + 1) * lines))]
        line += [jnp.zeros((1, width), jnp.float32)] * (lines - len(line))
        tail = jnp.where(row == r, jnp.concatenate(line, axis=1), tail)
    for out_ref in out_refs:
        out_ref[rows:, :] = tail.astype(jnp.bfloat16)
    for copy in passing:
        copy.wait()


def route(live, holders, slots, queries, peers, width, members):
    rows, columns = queries.shape[0] // HALVES, queries.shape[1]
    return pl.pallas_call(
        functools.partial(route_kernel, members),
        out_shape=(
            jax.ShapeDtypeStruct((peers, width), jnp.int32),
            *[jax.ShapeDtypeStruct((rows + TAIL, columns), jnp.bfloat16)] * HALVES,
        ),
        in_specs=[SMEM, HBM, HBM, HBM],
        out_specs=[VMEM] * (1 + HALVES),
        scratch_shapes=[
            pltpu.VMEM(holders.shape, jnp.int32),
            pltpu.VMEM(slots.shape, jnp.int32),
            pltpu.SemaphoreType.DMA((2 + HALVES * members,)),
        ],
        compiler_params=pltpu.CompilerParams(vmem_limit_bytes=62 * 1024 * 1024),
        name="route",
    )(live, holders, slots, queries)


def score(q, keys):
    return lax.dot_general(q, keys, (((1,), (1,)), ((), ())), preferred_element_type=jnp.float32)


def twice(value):
    return jnp.concatenate([value, value], axis=1)


def attend(
    slot, count, store_ref, span_ref, masks, q_ref, k_ref, v_ref, s_ref, ref_ref, acc_ref, rows,
    scale, stored=None,
):
    block_rows, head_dim = store_ref.shape[2:]
    heads = q_ref.shape[0] // rows
    stack = s_ref.shape[0]
    stacks = q_ref.shape[0] // stack
    tiles = (count + TILE - 1) // TILE

    def fetch(tile, into):
        for j in range(TILE):
            index = tile * TILE + j
            here = slot(jnp.minimum(index, count - 1))
            at = slice(j * block_rows, (j + 1) * block_rows)
            k_ref[into, at, :] = store_ref[0, here]
            block = store_ref[1, here]
            v_ref[into, at, :head_dim] = jnp.where(index < count, block, jnp.zeros_like(block))
            v_ref[into, at, head_dim:] = jnp.where(
                index < count, jnp.ones_like(block), jnp.zeros_like(block)
            )

    def one_key(key_row):
        row = key_row.astype(jnp.float32)[:1]
        return score(
            q_ref[...], jnp.broadcast_to(row, (head_dim, head_dim)).astype(jnp.bfloat16)
        )

    def start(exact):
        if span_ref is None:
            acc_ref[...] = jnp.zeros_like(acc_ref)
            if exact:
                ref_ref[...] = jnp.full_like(ref_ref, LOW)
            return
        keys = span_ref.shape[1]
        values = jnp.concatenate(
            [span_ref[1], jnp.ones((keys, head_dim), jnp.bfloat16)], axis=1
        )
        if not exact:
            ref_ref[...] = one_key(span_ref[0, :16, :])
        s = score(q_ref[:rows, :], span_ref[0])
        for g in range(heads):
            at = slice(g * rows, (g + 1) * rows)
            if g + 1 < heads:
                following = score(q_ref[(g + 1) * rows : (g + 2) * rows, :], span_ref[0])
            mask = masks[g * HALVES // heads]
            if exact:
                top = jnp.max(jnp.where(mask, s, LOW), axis=1, keepdims=True)
                ref_ref[at, :] = jnp.broadcast_to(top, (rows, head_dim))
            p = jnp.exp2((s - jnp.concatenate([ref_ref[at, :]] * (keys // head_dim), axis=1)) * scale)
            p = jnp.where(mask, p, 0.0).astype(jnp.bfloat16)
            acc_ref[at, :] = jnp.dot(p, values, preferred_element_type=jnp.float32)
            s = following

    start(False)
    if stored is not None:
        stored()

    @pl.when(count > 0)
    def _():
        fetch(0, 0)
        if span_ref is None:
            ref_ref[...] = one_key(k_ref[0, :16, :])
        s_ref[...] = score(q_ref[:stack, :], k_ref[0])

        def step(tile, carry):
            now = lax.rem(tile, 2)
            later = 1 - now
            keys, values = k_ref[now], v_ref[now]
            s = s_ref[...]
            fetch(tile + 1, later)
            for c in range(stacks):
                at = slice(c * stack, (c + 1) * stack)
                if c + 1 < stacks:
                    following = score(q_ref[(c + 1) * stack : (c + 2) * stack, :], keys)
                else:
                    s_ref[...] = score(q_ref[:stack, :], k_ref[later])
                p = jnp.exp2((s - twice(ref_ref[at, :])) * scale).astype(jnp.bfloat16)
                acc_ref[at, :] += jnp.dot(p, values, preferred_element_type=jnp.float32)
                s = following
            return carry

        lax.fori_loop(0, tiles, step, 0)
    beyond = jnp.max(jnp.where(acc_ref[:, head_dim:] < TOP, 0.0, 1.0))

    @pl.when(beyond > 0.0)
    def _():
        start(True)

        def careful(tile, carry):
            fetch(tile, 0)

            def head(g, inner):
                at = pl.ds(pl.multiple_of(g * rows, rows), rows)
                s = score(q_ref[at, :], k_ref[0])
                old = ref_ref[at, :]
                new = jnp.maximum(old, jnp.max(s, axis=1, keepdims=True))
                p = jnp.exp2((s - twice(new)) * scale).astype(jnp.bfloat16)
                update = jnp.dot(p, v_ref[0], preferred_element_type=jnp.float32)
                acc_ref[at, :] = acc_ref[at, :] * twice(jnp.exp2((old - new) * scale)) + update
                ref_ref[at, :] = new
                return inner

            return lax.fori_loop(0, heads, head, carry)

        lax.fori_loop(0, tiles, careful, 0)


def stack_heads(queries_ref, q_ref, rows, first=0):
    head_dim = q_ref.shape[1]
    for g in range(queries_ref.shape[1] // head_dim):
        q_ref[(first + g) * rows : (first + g + 1) * rows, :] = queries_ref[
            :rows, g * head_dim : (g + 1) * head_dim
        ]


def write_logs(out_ref, logs):
    heads, rows = logs.shape
    first = logs.astype(jnp.bfloat16).astype(jnp.float32)
    rest = logs - first
    second = rest.astype(jnp.bfloat16).astype(jnp.float32)
    third = rest - second
    spare = jnp.zeros((heads, out_ref.shape[1] - 3 * rows), jnp.float32)
    lines = jnp.concatenate([first, second, third, spare], axis=1)
    if heads < TAIL:
        more = jnp.zeros((TAIL - heads, out_ref.shape[1]), jnp.float32)
        lines = jnp.concatenate([lines, more], axis=0)
    out_ref[rows:, :] = lines.astype(jnp.bfloat16)


def read_logs(part_ref, heads, rows):
    lines = part_ref[rows:, :].astype(jnp.float32)[:heads]
    return lines[:, :rows] + lines[:, rows : 2 * rows] + lines[:, 2 * rows : 3 * rows]


def finish(out_refs, ref_ref, acc_ref, rows, scale):
    head_dim = ref_ref.shape[1]
    heads = ref_ref.shape[0] // rows // len(out_refs)
    lane = lax.broadcasted_iota(jnp.int32, (rows, head_dim), 1)
    for h, out_ref in enumerate(out_refs):
        totals = jnp.ones((rows, head_dim), jnp.float32)
        tops = jnp.zeros((rows, head_dim), jnp.float32)
        for g in range(heads):
            at = slice((h * heads + g) * rows, (h * heads + g + 1) * rows)
            total = acc_ref[at, head_dim:]
            inverse = pl.reciprocal(total, approx=True)
            inverse = inverse * (2.0 - total * inverse)
            out_ref[:rows, g * head_dim : (g + 1) * head_dim] = (
                acc_ref[at, :head_dim] * inverse
            ).astype(jnp.bfloat16)
            totals = jnp.where(lane == g, total, totals)
            tops = jnp.where(lane == g, ref_ref[at, :], tops)
        logs = tops * scale + jnp.log2(totals)
        write_logs(out_ref, logs.T[:heads])


def own_kernel(
    scale, members, me_ref, span_live_ref, lists_ref, queries_in, store_in, span_in, *refs
):
    out_refs = refs[:HALVES]
    queries_ref, store_ref, span_ref, sems, q_ref, k_ref, v_ref, s_ref, ref_ref, acc_ref = refs[
        HALVES:
    ]
    me = me_ref[0]
    rows = queries_ref.shape[1]
    each = rows // members
    copies = [
        pltpu.make_async_copy(span_in, span_ref, sems.at[0]),
        pltpu.make_async_copy(store_in, store_ref, sems.at[1]),
    ] + [
        pltpu.make_async_copy(
            queries_in.at[pl.ds((m * HALVES + h) * each, each)],
            queries_ref.at[h, pl.ds(m * each, each)],
            sems.at[2 + h * members + m],
        )
        for h in range(HALVES)
        for m in range(members)
    ]
    for copy in copies:
        copy.start()
    keys = span_ref.shape[1]
    key = lax.broadcasted_iota(jnp.int32, (rows, keys), 1)
    row = lax.broadcasted_iota(jnp.int32, (rows, keys), 0)
    masks = [
        (key <= original_row(row, h, members, each * HALVES)) & (key < span_live_ref[0])
        for h in range(HALVES)
    ]
    for copy in copies[2:]:
        copy.wait()
    for h in range(HALVES):
        stack_heads(queries_ref.at[h], q_ref, rows, h * queries_ref.shape[2] // q_ref.shape[1])
    copies[0].wait()
    attend(
        lambda index: lists_ref[me, index], lists_ref[me, lists_ref.shape[1] - 1], store_ref,
        span_ref, masks, q_ref, k_ref, v_ref, s_ref, ref_ref, acc_ref, rows, scale,
        copies[1].wait,
    )
    finish(out_refs, ref_ref, acc_ref, rows, scale)


def guest_kernel(scale, width, rows, number, me_ref, *refs):
    loaded_refs, store_ref = refs[:number], refs[number]
    out_refs = refs[number + 2 : 2 * number + 2]
    wide_ref, list_ref, sem_ref, q_ref, k_ref, v_ref, s_ref, ref_ref, acc_ref = refs[
        2 * number + 2 :
    ]
    each = loaded_refs[0].shape[1] // width
    me = me_ref[0]
    lane = pl.multiple_of(lax.rem(me, each) * width, 128)
    for which, loaded_ref in enumerate(loaded_refs):
        riders = loaded_ref[rows:, pl.ds(lane, width)].astype(jnp.float32)
        row = lax.broadcasted_iota(jnp.int32, riders.shape, 0)
        mine = jnp.sum(jnp.where(row == me // each, riders, 0.0), axis=0, keepdims=True)
        wide_ref[which : which + 1, :] = mine.astype(jnp.int32)
    copy = pltpu.make_async_copy(wide_ref, list_ref, sem_ref)
    copy.start()
    stack_heads(loaded_refs[0], q_ref, rows)
    copy.wait()
    for which, (loaded_ref, out_ref) in enumerate(zip(loaded_refs, out_refs)):
        count = list_ref[which, width - 1]

        @pl.when(count > 0)
        def _():
            if which:
                stack_heads(loaded_ref, q_ref, rows)
            attend(
                lambda index: list_ref[which, index], count, store_ref, None, None,
                q_ref, k_ref, v_ref, s_ref, ref_ref, acc_ref, rows, scale,
            )
            finish([out_ref], ref_ref, acc_ref, rows, scale)

        @pl.when(count == 0)
        def _():
            out_ref[...] = jnp.zeros_like(out_ref)
            write_logs(out_ref, jnp.full((q_ref.shape[0] // rows, rows), LOW, jnp.float32))


def attention_scratch(heads, rows, head_dim, block_rows):
    keys = TILE * block_rows
    return [
        pltpu.VMEM((heads * rows, head_dim), jnp.bfloat16),
        pltpu.VMEM((2, keys, head_dim), jnp.bfloat16),
        pltpu.VMEM((2, keys, 2 * head_dim), jnp.bfloat16),
        pltpu.VMEM((math.gcd(heads * rows, STACK), keys), jnp.float32),
        pltpu.VMEM((heads * rows, head_dim), jnp.float32),
        pltpu.VMEM((heads * rows, 2 * head_dim), jnp.float32),
    ]


def attention_cost(rows, keys, head_dim, heads):
    return pl.CostEstimate(
        flops=4 * rows * keys * head_dim * heads,
        bytes_accessed=64 * 1024,
        transcendentals=rows * keys * heads,
    )


def merged(parts, heads, rows):
    logs = [read_logs(part, heads, rows) for part in parts]
    top = functools.reduce(jnp.maximum, logs)
    weights = [jnp.exp2(log - top) for log in logs]
    total = functools.reduce(jnp.add, weights)
    return [weight / total for weight in weights], top + jnp.log2(total)


def weighted(parts, weights, g, head_dim, rows):
    total = jnp.zeros((rows, head_dim), jnp.float32)
    for part, weight in zip(parts, weights):
        part_rows = part[:rows, g * head_dim : (g + 1) * head_dim]
        total += part_rows.astype(jnp.float32) * weight[:, g : g + 1]
    return total.astype(jnp.bfloat16)


def merge_kernel(heads, number, *refs):
    parts, out_ref = refs[:number], refs[number + 1]
    rows = out_ref.shape[0] - TAIL
    head_dim = out_ref.shape[1] // heads
    weights, logs = merged(parts, heads, rows)
    weights = [weight.T for weight in weights]
    for g in range(heads):
        out_ref[:rows, g * head_dim : (g + 1) * head_dim] = weighted(
            parts, weights, g, head_dim, rows
        )
    write_logs(out_ref, logs)


def project_kernel(heads, number, h, members, cuts, turn_ref, span_live_ref, *refs):
    parts = refs[:number]
    weight_ref, after_ref, near_ref, *away_refs = refs[number : number + 3 + cuts]
    keep_ref, att_ref, sorted_ref, held_ref, sems = refs[number + 3 + cuts :]
    rows, features = att_ref.shape
    chunks, _, width = held_ref.shape
    head_dim = features // heads
    copies = [
        pltpu.make_async_copy(weight_ref.at[:, pl.ds(i * width, width)], held_ref.at[i], sems.at[i])
        for i in range(chunks)
    ]
    for copy in copies:
        copy.start()

    row = lax.broadcasted_iota(jnp.int32, (heads, rows), 1)
    live = original_row(row, h, members, rows * HALVES // members) < span_live_ref[0]
    weights, _ = merged(parts, heads, rows)
    weights = [jnp.where(live, weight, 0.0).T for weight in weights]
    for g in range(heads):
        att_ref[:, g * head_dim : (g + 1) * head_dim] = weighted(
            parts, weights, g, head_dim, rows
        )

    chips = keep_ref.shape[0]
    block = keep_ref.shape[1]
    chip, core = turn_ref[0] // 2, lax.rem(turn_ref[0], 2)
    for side, wanted in enumerate((1 - core, core)):
        for k in range(chips):
            owner = 2 * lax.rem(chip + k, chips) + wanted
            at = (side * chips + k) * block
            sorted_ref[at : at + block, :] = att_ref[
                pl.ds(pl.multiple_of(owner * block, block), block), :
            ]
    for i in range(chunks):
        copies[i].wait()
        at = slice(i * width, (i + 1) * width)
        product = jnp.dot(
            sorted_ref[...], held_ref[i], preferred_element_type=jnp.float32
        ).astype(jnp.bfloat16)
        for k in range(chips):
            leaving = product[k * block : (k + 1) * block]
            if k:
                cut = i * cuts // chunks
                first = i * width - cut * away_refs[cut].shape[2]
                away_refs[cut][k - 1, :, first : first + width] = leaving
            else:
                near_ref[:, at] = leaving
            keep_ref[k, :, at] = product[(chips + k) * block : (chips + k + 1) * block]


def project(turn, span_live, parts, out_weight, after, heads, h, members, cuts):
    features, outputs = out_weight.shape
    rows = parts[0].shape[0] - TAIL
    width = 512
    chunks = outputs // width
    chips, block = members // 2, rows // members
    return pl.pallas_call(
        functools.partial(project_kernel, heads, len(parts), h, members, cuts),
        out_shape=[
            jax.ShapeDtypeStruct(shape, jnp.bfloat16)
            for shape in (
                (block, outputs),
                *[(chips - 1, block, outputs // cuts)] * cuts,
                (chips, block, outputs),
            )
        ],
        in_specs=[SMEM, SMEM] + [VMEM] * len(parts) + [HBM, pl.BlockSpec(memory_space=pl.ANY)],
        out_specs=[VMEM] * (2 + cuts),
        scratch_shapes=[
            pltpu.VMEM((rows, features), jnp.bfloat16),
            pltpu.VMEM((rows, features), jnp.bfloat16),
            pltpu.VMEM((chunks, features, width), jnp.bfloat16),
            pltpu.SemaphoreType.DMA((chunks,)),
        ],
        compiler_params=pltpu.CompilerParams(vmem_limit_bytes=48 * 1024 * 1024),
        cost_estimate=pl.CostEstimate(
            flops=2 * rows * features * outputs,
            bytes_accessed=2 * (features + rows) * outputs,
            transcendentals=0,
        ),
        name="project",
    )(turn, span_live, *parts, out_weight, after)


def add_kernel(cuts, kept_ref, *refs):
    come_refs, out_refs = refs[:cuts], refs[cuts:]
    width = kept_ref.shape[2] // cuts
    for k in range(kept_ref.shape[0] - 1):
        for cut, come_ref in enumerate(come_refs):
            kept = kept_ref[k + 1, :, cut * width : (cut + 1) * width].astype(jnp.float32)
            out_refs[k * cuts + cut][...] = (kept + come_ref[k].astype(jnp.float32)).astype(
                jnp.bfloat16
            )


def total_kernel(counts, *refs):
    out_ref = refs[-1]
    block, width = out_ref.shape[0] // HALVES, out_ref.shape[1]
    first = 0
    for h, (others, cuts) in enumerate(counts):
        kept_ref, near_ref = refs[first : first + 2]
        arrived = refs[first + 2 : first + 2 + others]
        first += 2 + others
        for cut in range(cuts):
            at = slice(cut * width // cuts, (cut + 1) * width // cuts)
            total = kept_ref[0, :, at].astype(jnp.float32) + near_ref[:, at].astype(jnp.float32)
            for ref in arrived[cut::cuts]:
                total += ref[...].astype(jnp.float32)
            out_ref[h * block : (h + 1) * block, at] = total.astype(jnp.bfloat16)


def add_cores(near, aways, keep, members):
    chips, block, outputs = keep.shape
    cuts = len(aways)
    shape = jax.ShapeDtypeStruct((block, outputs // cuts), jnp.bfloat16)
    pairs = [(i, i ^ 1) for i in range(members)]
    come = [lax.ppermute(away, "tp", pairs) for away in aways]
    near = lax.ppermute(near, "tp", pairs)
    sums = pl.pallas_call(
        functools.partial(add_kernel, cuts),
        out_shape=[shape] * ((chips - 1) * cuts),
        in_specs=[VMEM] * (1 + cuts),
        out_specs=[VMEM] * ((chips - 1) * cuts),
        compiler_params=pltpu.CompilerParams(vmem_limit_bytes=VMEM_LIMIT),
        name="add_cores",
    )(keep, *come)
    return near, sums


def add_chips(sums, cuts, members):
    return [
        lax.ppermute(
            each, "tp", [(i, (i + 2 * (n // cuts + 1)) % members) for i in range(members)]
        )
        for n, each in enumerate(sums)
    ]


def total_sums(terms, counts, block, outputs):
    return pl.pallas_call(
        functools.partial(total_kernel, counts),
        out_shape=jax.ShapeDtypeStruct((HALVES * block, outputs), jnp.bfloat16),
        in_specs=[VMEM] * len(terms),
        out_specs=VMEM,
        compiler_params=pltpu.CompilerParams(vmem_limit_bytes=VMEM_LIMIT),
        name="total",
    )(*terms)


def pack_kernel(me_ref, span_live_ref, owners_ref, span_ref, *refs):
    out_refs, (out_ref, counts_ref) = refs[:-2], refs[-2:]
    peers = out_ref.shape[0]
    block_rows, head_dim = out_ref.shape[3:]
    out_ref[...] = jnp.zeros_like(out_ref)
    for k in range(peers):
        counts_ref[k] = 0
    row = lax.broadcasted_iota(jnp.int32, (block_rows, head_dim), 0)
    for b in range(span_ref.shape[1] // block_rows):
        owner = owners_ref[b]
        rank = counts_ref[owner]
        counts_ref[owner] = rank + 1
        keep = row + b * block_rows < span_live_ref[0]
        for side in range(2):
            block = span_ref[side, b * block_rows : (b + 1) * block_rows, :]
            out_ref[owner, side, rank] = jnp.where(keep, block, jnp.zeros_like(block))
    for k, each_ref in enumerate(out_refs):
        each_ref[...] = out_ref[me_ref[0] ^ k]


def unpack_kernel(me_ref, *refs):
    for k, each_ref in enumerate(refs[:-1]):
        refs[-1][:, me_ref[0] ^ k] = each_ref[...]


def shards(
    queries,
    cache_store,
    span_cache,
    out_weight,
    prefix_blocks,
    span_lengths,
    hit_holders,
    hit_slots,
    store_owners,
):
    peers = lax.axis_size("inst")
    block_rows, head_dim = cache_store.shape[2:]
    rows, columns = queries.shape
    heads = columns // head_dim
    block_max = hit_slots.shape[1]
    cap = max(2, block_max * 5 // (4 * peers))
    new_count = rows // block_rows
    push_cap = max(2, 2 * new_count // peers)
    scale = math.log2(math.e) / math.sqrt(head_dim)
    me = lax.axis_index("inst").reshape(1)
    width = round_up(cap + 1, 128)
    members = lax.axis_size("tp")
    some = rows // HALVES
    part_shape = jax.ShapeDtypeStruct((some + TAIL, columns), jnp.bfloat16)
    params = pltpu.CompilerParams(vmem_limit_bytes=VMEM_LIMIT)
    anywhere = pl.BlockSpec(memory_space=pl.ANY)

    def exchange(value, bit):
        return lax.ppermute(value, "inst", [(i, i ^ bit) for i in range(peers)])

    order = sorted(range(1, peers), key=lambda k: -(k & -k))

    def spread(loaded, after, near=None):
        held = {0: loaded}
        for k in order:
            if k == 1 and near is not None:
                held[k] = near
                continue
            source = held[k & (k - 1)]
            if k & (k - 1):
                source, after = lax.optimization_barrier((source, after))
            held[k] = exchange(source, k & -k)
        return held, after

    def guests(held, group, after):
        return pl.pallas_call(
            functools.partial(guest_kernel, scale, width, some, len(group)),
            out_shape=[part_shape] * len(group),
            in_specs=[SMEM] + [VMEM] * (len(group) + 1) + [anywhere],
            out_specs=[VMEM] * len(group),
            scratch_shapes=[
                pltpu.VMEM((len(group), width), jnp.int32),
                pltpu.SMEM((len(group), width), jnp.int32),
                pltpu.SemaphoreType.DMA,
                *attention_scratch(heads, some, head_dim, block_rows),
            ],
            compiler_params=params,
            cost_estimate=attention_cost(some, rows // 2, head_dim, heads),
            name="guest_attention",
        )(me, *[held[k] for k in group], cache_store, after)

    def gather_back(parts, after):
        parts = dict(parts)
        for k in reversed(order):
            arrived = [exchange(parts[c], c & -c) for c in order if c & (c - 1) == k]
            if arrived:
                parts[k] = after = pl.pallas_call(
                    functools.partial(merge_kernel, heads, len(arrived) + 1),
                    out_shape=part_shape,
                    in_specs=[VMEM] * (len(arrived) + 1) + [anywhere],
                    out_specs=VMEM,
                    compiler_params=params,
                    name="merge",
                )(parts[k], *arrived, after)
        parts[1], after = lax.optimization_barrier((parts[1], after))
        return [exchange(parts[k], k) for k in order if k & (k - 1) == 0], after

    lists, *loaded = route(
        prefix_blocks, hit_holders.reshape(1, -1), hit_slots, queries, peers, width, members
    )
    own = pl.pallas_call(
        functools.partial(own_kernel, scale, members),
        out_shape=[part_shape] * HALVES,
        in_specs=[SMEM, SMEM, SMEM, HBM, HBM, HBM],
        out_specs=[VMEM] * HALVES,
        scratch_shapes=[
            pltpu.VMEM((HALVES, some, columns), jnp.bfloat16),
            pltpu.VMEM(cache_store.shape, jnp.bfloat16),
            pltpu.VMEM(span_cache.shape, jnp.bfloat16),
            pltpu.SemaphoreType.DMA((2 + HALVES * members,)),
            *attention_scratch(heads, rows, head_dim, block_rows),
        ],
        compiler_params=params,
        cost_estimate=attention_cost(rows, 8 * rows, head_dim, heads),
        name="own_attention",
    )(me, span_lengths, lists, queries, cache_store, span_cache)

    own = list(own)
    before, arrived = None, []
    held, after = spread(loaded[0], own[0])
    nears = [None] + [exchange(each, 1) for each in loaded[1:]]
    *loaded[1:], after = lax.optimization_barrier((*loaded[1:], after))
    after, *nears[1:] = lax.optimization_barrier((after, *nears[1:]))
    for h in range(HALVES):
        if h + 1 < HALVES:
            groups = [order[i : i + 2] for i in range(0, peers - 1, 2)]
        else:
            groups = [[k] for k in reversed(order) if k > 1] + [[1]]
        parts, following = {}, None
        for index, group in enumerate(groups):
            results = guests(held, group, after)
            after = results[0]
            parts.update(zip(group, results))
            if index == 0 and h + 1 < HALVES:
                following, after = spread(loaded[h + 1], after, nears[h + 1])
            if index == 0 and before is not None:
                back, after = gather_back(before, after)
                arrived.append(back)
        before, held = parts, following
    back, after = gather_back(before, after)
    arrived.append(back)

    push_shape = jax.ShapeDtypeStruct((2, push_cap, block_rows, head_dim), jnp.bfloat16)
    outgoing = pl.pallas_call(
        pack_kernel,
        out_shape=[push_shape] * peers,
        in_specs=[SMEM, SMEM, SMEM, VMEM],
        out_specs=[VMEM] * peers,
        scratch_shapes=[
            pltpu.VMEM((peers, *push_shape.shape), jnp.bfloat16),
            pltpu.SMEM((peers,), jnp.int32),
        ],
        compiler_params=params,
        name="pack_blocks",
    )(me, span_lengths, store_owners.reshape(-1), span_cache)
    turn = lax.axis_index("tp").reshape(1)
    terms, counts = [], []
    for h in range(HALVES):
        if h == 0:
            own[h], *outgoing = lax.optimization_barrier((own[h], *outgoing))
        parts = [own[h], *arrived[h]]
        cuts = 1
        near, *aways, keep = project(
            turn, span_lengths, parts, out_weight, after, heads, h, members, cuts
        )
        near, sums = add_cores(near, aways, keep, members)
        if h + 1 == HALVES:
            near, *sums = lax.optimization_barrier((near, *sums))
        crossed = add_chips(sums, cuts, members)
        if h + 1 < HALVES:
            own[h + 1], near, after = lax.optimization_barrier((own[h + 1], near, sums[0]))
        terms += [keep, near, *crossed]
        counts.append((len(crossed), cuts))
    keep, *outgoing = lax.optimization_barrier((keep, *outgoing))
    projected = total_sums(terms, counts, some // members, out_weight.shape[1])

    incoming = [outgoing[0], *[exchange(outgoing[k], k) for k in range(1, peers)]]
    pushed_blocks = pl.pallas_call(
        unpack_kernel,
        out_shape=jax.ShapeDtypeStruct(
            (2, peers, push_cap, block_rows, head_dim), jnp.bfloat16
        ),
        in_specs=[SMEM] + [VMEM] * peers,
        out_specs=VMEM,
        compiler_params=params,
        name="unpack_blocks",
    )(me, *incoming).reshape(2, peers * push_cap, block_rows, head_dim)
    return (projected, pushed_blocks)


def solution(mesh):
    return jax.shard_map(
        shards,
        mesh=mesh,
        in_specs=(
            P(("pods", "inst"), "tp"),
            P(None, ("pods", "inst"), None, "tp"),
            P(None, ("pods", "inst"), "tp"),
            P("tp", None),
            P(("pods", "inst")),
            P(("pods", "inst")),
            P(("pods", "inst"), None, None),
            P(("pods", "inst"), None),
            P(("pods", "inst"), None, None),
        ),
        out_specs=(P(("pods", "inst", "tp"), None), P(None, ("pods", "inst"), None, "tp")),
        check_vma=False,
    )
```

```python
import functools
import math

import jax
import jax.numpy as jnp
from jax import lax
from jax.experimental import pallas as pl
from jax.experimental.pallas import tpu as pltpu
from jax.sharding import PartitionSpec as P

LOW = -1e30
TOP = 2.0**100
TILE = 16
STACK = 512
HALVES = 2
TAIL = 8
VMEM_LIMIT = 20 * 1024 * 1024

SMEM = pl.BlockSpec(memory_space=pltpu.SMEM)
VMEM = pl.BlockSpec(memory_space=pltpu.VMEM)
HBM = pl.BlockSpec(memory_space=pltpu.HBM)


def round_up(number, step):
    return -(-number // step) * step


def original_row(row, h, members, own_rows):
    each = own_rows // HALVES
    member = sum((row >= m * each).astype(jnp.int32) for m in range(1, members))
    return row + member * (own_rows - each) + h * each


def route_kernel(
    members, live_ref, holders_in, slots_in, q_in, lists_ref, *refs
):
    out_refs, (holders_ref, slots_ref, sems) = refs[:HALVES], refs[HALVES:]
    columns = q_in.shape[1]
    rows = q_in.shape[0] // HALVES
    each = rows // members
    loading = [
        pltpu.make_async_copy(holders_in, holders_ref, sems.at[0]),
        pltpu.make_async_copy(slots_in, slots_ref, sems.at[1]),
    ]
    passing = [
        pltpu.make_async_copy(
            q_in.at[pl.ds((m * HALVES + h) * each, each)],
            out_refs[h].at[pl.ds(m * each, each)],
            sems.at[2 + h * members + m],
        )
        for h in range(HALVES)
        for m in range(members)
    ]
    for copy in loading + passing:
        copy.start()
    for copy in loading:
        copy.wait()
    peers, width = lists_ref.shape
    number = holders_ref.shape[1]
    padded = round_up(peers, 16)
    holder = lax.broadcasted_iota(jnp.int32, (padded, number), 0)
    entry = lax.broadcasted_iota(jnp.int32, (padded, number), 1)
    hot = (holders_ref[...] == holder) & (entry < live_ref[0])
    ones = jnp.where(hot, 1.0, 0.0)
    earlier = lax.broadcasted_iota(jnp.int32, (number, number), 0) < lax.broadcasted_iota(
        jnp.int32, (number, number), 1
    )
    ranks = jnp.dot(
        ones.astype(jnp.bfloat16),
        jnp.where(earlier, 1.0, 0.0).astype(jnp.bfloat16),
        preferred_element_type=jnp.float32,
    )
    rank = jnp.sum(ranks * ones, axis=0, keepdims=True)
    rank = jnp.broadcast_to(rank, (8, number)).T[:, :1].astype(jnp.int32)
    place = lax.broadcasted_iota(jnp.int32, (number, width), 1) == rank
    slots = jnp.where(hot, slots_ref[...], 0).astype(jnp.float32)
    lists = jnp.dot(
        slots.astype(jnp.bfloat16),
        jnp.where(place, 1.0, 0.0).astype(jnp.bfloat16),
        preferred_element_type=jnp.float32,
    )
    counts = jnp.sum(ones, axis=1, keepdims=True)
    last = lax.broadcasted_iota(jnp.int32, (padded, width), 1) == width - 1
    lists = jnp.where(last, counts, lists)[:peers]
    lists_ref[...] = lists.astype(jnp.int32)

    lines = columns // width
    row = lax.broadcasted_iota(jnp.int32, (TAIL, columns), 0)
    tail = jnp.zeros((TAIL, columns), jnp.float32)
    for r in range(-(-peers // lines)):
        line = [lists[h : h + 1] for h in range(r * lines, min(peers, (r + 1) * lines))]
        line += [jnp.zeros((1, width), jnp.float32)] * (lines - len(line))
        tail = jnp.where(row == r, jnp.concatenate(line, axis=1), tail)
    for out_ref in out_refs:
        out_ref[rows:, :] = tail.astype(jnp.bfloat16)
    for copy in passing:
        copy.wait()


def route(live, holders, slots, queries, peers, width, members):
    rows, columns = queries.shape[0] // HALVES, queries.shape[1]
    return pl.pallas_call(
        functools.partial(route_kernel, members),
        out_shape=(
            jax.ShapeDtypeStruct((peers, width), jnp.int32),
            *[jax.ShapeDtypeStruct((rows + TAIL, columns), jnp.bfloat16)] * HALVES,
        ),
        in_specs=[SMEM, HBM, HBM, HBM],
        out_specs=[VMEM] * (1 + HALVES),
        scratch_shapes=[
            pltpu.VMEM(holders.shape, jnp.int32),
            pltpu.VMEM(slots.shape, jnp.int32),
            pltpu.SemaphoreType.DMA((2 + HALVES * members,)),
        ],
        compiler_params=pltpu.CompilerParams(vmem_limit_bytes=62 * 1024 * 1024),
        name="route",
    )(live, holders, slots, queries)


def score(q, keys):
    return lax.dot_general(q, keys, (((1,), (1,)), ((), ())), preferred_element_type=jnp.float32)


def twice(value):
    return jnp.concatenate([value, value], axis=1)


def attend(
    slot, count, store_ref, span_ref, masks, q_ref, k_ref, v_ref, s_ref, ref_ref, acc_ref, rows,
    scale, stored=None,
):
    block_rows, head_dim = store_ref.shape[2:]
    heads = q_ref.shape[0] // rows
    stack = s_ref.shape[0]
    stacks = q_ref.shape[0] // stack
    tiles = (count + TILE - 1) // TILE

    def fetch(tile, into):
        for j in range(TILE):
            index = tile * TILE + j
            here = slot(jnp.minimum(index, count - 1))
            at = slice(j * block_rows, (j + 1) * block_rows)
            k_ref[into, at, :] = store_ref[0, here]
            block = store_ref[1, here]
            v_ref[into, at, :head_dim] = jnp.where(index < count, block, jnp.zeros_like(block))
            v_ref[into, at, head_dim:] = jnp.where(
                index < count, jnp.ones_like(block), jnp.zeros_like(block)
            )

    def one_key(key_row):
        row = key_row.astype(jnp.float32)[:1]
        return score(
            q_ref[...], jnp.broadcast_to(row, (head_dim, head_dim)).astype(jnp.bfloat16)
        )

    def start(exact):
        if span_ref is None:
            acc_ref[...] = jnp.zeros_like(acc_ref)
            if exact:
                ref_ref[...] = jnp.full_like(ref_ref, LOW)
            return
        keys = span_ref.shape[1]
        values = jnp.concatenate(
            [span_ref[1], jnp.ones((keys, head_dim), jnp.bfloat16)], axis=1
        )
        if not exact:
            ref_ref[...] = one_key(span_ref[0, :16, :])
        s = score(q_ref[:rows, :], span_ref[0])
        for g in range(heads):
            at = slice(g * rows, (g + 1) * rows)
            if g + 1 < heads:
                following = score(q_ref[(g + 1) * rows : (g + 2) * rows, :], span_ref[0])
            mask = masks[g * HALVES // heads]
            if exact:
                top = jnp.max(jnp.where(mask, s, LOW), axis=1, keepdims=True)
                ref_ref[at, :] = jnp.broadcast_to(top, (rows, head_dim))
            p = jnp.exp2((s - jnp.concatenate([ref_ref[at, :]] * (keys // head_dim), axis=1)) * scale)
            p = jnp.where(mask, p, 0.0).astype(jnp.bfloat16)
            acc_ref[at, :] = jnp.dot(p, values, preferred_element_type=jnp.float32)
            s = following

    start(False)
    if stored is not None:
        stored()

    @pl.when(count > 0)
    def _():
        fetch(0, 0)
        if span_ref is None:
            ref_ref[...] = one_key(k_ref[0, :16, :])
        s_ref[...] = score(q_ref[:stack, :], k_ref[0])

        def step(tile, carry):
            now = lax.rem(tile, 2)
            later = 1 - now
            keys, values = k_ref[now], v_ref[now]
            s = s_ref[...]
            fetch(tile + 1, later)
            for c in range(stacks):
                at = slice(c * stack, (c + 1) * stack)
                if c + 1 < stacks:
                    following = score(q_ref[(c + 1) * stack : (c + 2) * stack, :], keys)
                else:
                    s_ref[...] = score(q_ref[:stack, :], k_ref[later])
                p = jnp.exp2((s - twice(ref_ref[at, :])) * scale).astype(jnp.bfloat16)
                acc_ref[at, :] += jnp.dot(p, values, preferred_element_type=jnp.float32)
                s = following
            return carry

        lax.fori_loop(0, tiles, step, 0)
    beyond = jnp.max(jnp.where(acc_ref[:, head_dim:] < TOP, 0.0, 1.0))

    @pl.when(beyond > 0.0)
    def _():
        start(True)

        def careful(tile, carry):
            fetch(tile, 0)

            def head(g, inner):
                at = pl.ds(pl.multiple_of(g * rows, rows), rows)
                s = score(q_ref[at, :], k_ref[0])
                old = ref_ref[at, :]
                new = jnp.maximum(old, jnp.max(s, axis=1, keepdims=True))
                p = jnp.exp2((s - twice(new)) * scale).astype(jnp.bfloat16)
                update = jnp.dot(p, v_ref[0], preferred_element_type=jnp.float32)
                acc_ref[at, :] = acc_ref[at, :] * twice(jnp.exp2((old - new) * scale)) + update
                ref_ref[at, :] = new
                return inner

            return lax.fori_loop(0, heads, head, carry)

        lax.fori_loop(0, tiles, careful, 0)


def stack_heads(queries_ref, q_ref, rows, first=0):
    head_dim = q_ref.shape[1]
    for g in range(queries_ref.shape[1] // head_dim):
        q_ref[(first + g) * rows : (first + g + 1) * rows, :] = queries_ref[
            :rows, g * head_dim : (g + 1) * head_dim
        ]


def write_logs(out_ref, logs):
    heads, rows = logs.shape
    first = logs.astype(jnp.bfloat16).astype(jnp.float32)
    rest = logs - first
    second = rest.astype(jnp.bfloat16).astype(jnp.float32)
    third = rest - second
    spare = jnp.zeros((heads, out_ref.shape[1] - 3 * rows), jnp.float32)
    lines = jnp.concatenate([first, second, third, spare], axis=1)
    if heads < TAIL:
        more = jnp.zeros((TAIL - heads, out_ref.shape[1]), jnp.float32)
        lines = jnp.concatenate([lines, more], axis=0)
    out_ref[rows:, :] = lines.astype(jnp.bfloat16)


def read_logs(part_ref, heads, rows):
    lines = part_ref[rows:, :].astype(jnp.float32)[:heads]
    return lines[:, :rows] + lines[:, rows : 2 * rows] + lines[:, 2 * rows : 3 * rows]


def finish(out_refs, ref_ref, acc_ref, rows, scale):
    head_dim = ref_ref.shape[1]
    heads = ref_ref.shape[0] // rows // len(out_refs)
    lane = lax.broadcasted_iota(jnp.int32, (rows, head_dim), 1)
    for h, out_ref in enumerate(out_refs):
        totals = jnp.ones((rows, head_dim), jnp.float32)
        tops = jnp.zeros((rows, head_dim), jnp.float32)
        for g in range(heads):
            at = slice((h * heads + g) * rows, (h * heads + g + 1) * rows)
            total = acc_ref[at, head_dim:]
            inverse = pl.reciprocal(total, approx=True)
            inverse = inverse * (2.0 - total * inverse)
            out_ref[:rows, g * head_dim : (g + 1) * head_dim] = (
                acc_ref[at, :head_dim] * inverse
            ).astype(jnp.bfloat16)
            totals = jnp.where(lane == g, total, totals)
            tops = jnp.where(lane == g, ref_ref[at, :], tops)
        logs = tops * scale + jnp.log2(totals)
        write_logs(out_ref, logs.T[:heads])


def own_kernel(
    scale, members, me_ref, span_live_ref, lists_ref, queries_in, store_in, span_in, *refs
):
    out_refs = refs[:HALVES]
    queries_ref, store_ref, span_ref, sems, q_ref, k_ref, v_ref, s_ref, ref_ref, acc_ref = refs[
        HALVES:
    ]
    me = me_ref[0]
    rows = queries_ref.shape[1]
    each = rows // members
    copies = [
        pltpu.make_async_copy(span_in, span_ref, sems.at[0]),
        pltpu.make_async_copy(store_in, store_ref, sems.at[1]),
    ] + [
        pltpu.make_async_copy(
            queries_in.at[pl.ds((m * HALVES + h) * each, each)],
            queries_ref.at[h, pl.ds(m * each, each)],
            sems.at[2 + h * members + m],
        )
        for h in range(HALVES)
        for m in range(members)
    ]
    for copy in copies:
        copy.start()
    keys = span_ref.shape[1]
    key = lax.broadcasted_iota(jnp.int32, (rows, keys), 1)
    row = lax.broadcasted_iota(jnp.int32, (rows, keys), 0)
    masks = [
        (key <= original_row(row, h, members, each * HALVES)) & (key < span_live_ref[0])
        for h in range(HALVES)
    ]
    for copy in copies[2:]:
        copy.wait()
    for h in range(HALVES):
        stack_heads(queries_ref.at[h], q_ref, rows, h * queries_ref.shape[2] // q_ref.shape[1])
    copies[0].wait()
    attend(
        lambda index: lists_ref[me, index], lists_ref[me, lists_ref.shape[1] - 1], store_ref,
        span_ref, masks, q_ref, k_ref, v_ref, s_ref, ref_ref, acc_ref, rows, scale,
        copies[1].wait,
    )
    finish(out_refs, ref_ref, acc_ref, rows, scale)


def guest_kernel(scale, width, rows, number, me_ref, *refs):
    loaded_refs, store_ref = refs[:number], refs[number]
    out_refs = refs[number + 2 : 2 * number + 2]
    wide_ref, list_ref, sem_ref, q_ref, k_ref, v_ref, s_ref, ref_ref, acc_ref = refs[
        2 * number + 2 :
    ]
    each = loaded_refs[0].shape[1] // width
    me = me_ref[0]
    lane = pl.multiple_of(lax.rem(me, each) * width, 128)
    for which, loaded_ref in enumerate(loaded_refs):
        riders = loaded_ref[rows:, pl.ds(lane, width)].astype(jnp.float32)
        row = lax.broadcasted_iota(jnp.int32, riders.shape, 0)
        mine = jnp.sum(jnp.where(row == me // each, riders, 0.0), axis=0, keepdims=True)
        wide_ref[which : which + 1, :] = mine.astype(jnp.int32)
    copy = pltpu.make_async_copy(wide_ref, list_ref, sem_ref)
    copy.start()
    stack_heads(loaded_refs[0], q_ref, rows)
    copy.wait()
    for which, (loaded_ref, out_ref) in enumerate(zip(loaded_refs, out_refs)):
        count = list_ref[which, width - 1]

        @pl.when(count > 0)
        def _():
            if which:
                stack_heads(loaded_ref, q_ref, rows)
            attend(
                lambda index: list_ref[which, index], count, store_ref, None, None,
                q_ref, k_ref, v_ref, s_ref, ref_ref, acc_ref, rows, scale,
            )
            finish([out_ref], ref_ref, acc_ref, rows, scale)

        @pl.when(count == 0)
        def _():
            out_ref[...] = jnp.zeros_like(out_ref)
            write_logs(out_ref, jnp.full((q_ref.shape[0] // rows, rows), LOW, jnp.float32))


def attention_scratch(heads, rows, head_dim, block_rows):
    keys = TILE * block_rows
    return [
        pltpu.VMEM((heads * rows, head_dim), jnp.bfloat16),
        pltpu.VMEM((2, keys, head_dim), jnp.bfloat16),
        pltpu.VMEM((2, keys, 2 * head_dim), jnp.bfloat16),
        pltpu.VMEM((math.gcd(heads * rows, STACK), keys), jnp.float32),
        pltpu.VMEM((heads * rows, head_dim), jnp.float32),
        pltpu.VMEM((heads * rows, 2 * head_dim), jnp.float32),
    ]


def attention_cost(rows, keys, head_dim, heads):
    return pl.CostEstimate(
        flops=4 * rows * keys * head_dim * heads,
        bytes_accessed=64 * 1024,
        transcendentals=rows * keys * heads,
    )


def merged(parts, heads, rows):
    logs = [read_logs(part, heads, rows) for part in parts]
    top = functools.reduce(jnp.maximum, logs)
    weights = [jnp.exp2(log - top) for log in logs]
    total = functools.reduce(jnp.add, weights)
    return [weight / total for weight in weights], top + jnp.log2(total)


def weighted(parts, weights, g, head_dim, rows):
    total = jnp.zeros((rows, head_dim), jnp.float32)
    for part, weight in zip(parts, weights):
        part_rows = part[:rows, g * head_dim : (g + 1) * head_dim]
        total += part_rows.astype(jnp.float32) * weight[:, g : g + 1]
    return total.astype(jnp.bfloat16)


def merge_kernel(heads, number, *refs):
    parts, out_ref = refs[:number], refs[number + 1]
    rows = out_ref.shape[0] - TAIL
    head_dim = out_ref.shape[1] // heads
    weights, logs = merged(parts, heads, rows)
    weights = [weight.T for weight in weights]
    for g in range(heads):
        out_ref[:rows, g * head_dim : (g + 1) * head_dim] = weighted(
            parts, weights, g, head_dim, rows
        )
    write_logs(out_ref, logs)


def project_kernel(heads, number, h, members, cuts, turn_ref, span_live_ref, *refs):
    parts = refs[:number]
    weight_ref, after_ref, near_ref, *away_refs = refs[number : number + 3 + cuts]
    keep_ref, att_ref, sorted_ref, held_ref, sems = refs[number + 3 + cuts :]
    rows, features = att_ref.shape
    chunks, _, width = held_ref.shape
    head_dim = features // heads
    copies = [
        pltpu.make_async_copy(weight_ref.at[:, pl.ds(i * width, width)], held_ref.at[i], sems.at[i])
        for i in range(chunks)
    ]
    for copy in copies:
        copy.start()

    row = lax.broadcasted_iota(jnp.int32, (heads, rows), 1)
    live = original_row(row, h, members, rows * HALVES // members) < span_live_ref[0]
    weights, _ = merged(parts, heads, rows)
    weights = [jnp.where(live, weight, 0.0).T for weight in weights]
    for g in range(heads):
        att_ref[:, g * head_dim : (g + 1) * head_dim] = weighted(
            parts, weights, g, head_dim, rows
        )

    chips = keep_ref.shape[0]
    block = keep_ref.shape[1]
    chip, core = turn_ref[0] // 2, lax.rem(turn_ref[0], 2)
    for side, wanted in enumerate((1 - core, core)):
        for k in range(chips):
            owner = 2 * lax.rem(chip + k, chips) + wanted
            at = (side * chips + k) * block
            sorted_ref[at : at + block, :] = att_ref[
                pl.ds(pl.multiple_of(owner * block, block), block), :
            ]
    for i in range(chunks):
        copies[i].wait()
        at = slice(i * width, (i + 1) * width)
        product = jnp.dot(
            sorted_ref[...], held_ref[i], preferred_element_type=jnp.float32
        ).astype(jnp.bfloat16)
        for k in range(chips):
            leaving = product[k * block : (k + 1) * block]
            if k:
                cut = i * cuts // chunks
                first = i * width - cut * away_refs[cut].shape[2]
                away_refs[cut][k - 1, :, first : first + width] = leaving
            else:
                near_ref[:, at] = leaving
            keep_ref[k, :, at] = product[(chips + k) * block : (chips + k + 1) * block]


def project(turn, span_live, parts, out_weight, after, heads, h, members, cuts):
    features, outputs = out_weight.shape
    rows = parts[0].shape[0] - TAIL
    width = 512
    chunks = outputs // width
    chips, block = members // 2, rows // members
    return pl.pallas_call(
        functools.partial(project_kernel, heads, len(parts), h, members, cuts),
        out_shape=[
            jax.ShapeDtypeStruct(shape, jnp.bfloat16)
            for shape in (
                (block, outputs),
                *[(chips - 1, block, outputs // cuts)] * cuts,
                (chips, block, outputs),
            )
        ],
        in_specs=[SMEM, SMEM] + [VMEM] * len(parts) + [HBM, pl.BlockSpec(memory_space=pl.ANY)],
        out_specs=[VMEM] * (2 + cuts),
        scratch_shapes=[
            pltpu.VMEM((rows, features), jnp.bfloat16),
            pltpu.VMEM((rows, features), jnp.bfloat16),
            pltpu.VMEM((chunks, features, width), jnp.bfloat16),
            pltpu.SemaphoreType.DMA((chunks,)),
        ],
        compiler_params=pltpu.CompilerParams(vmem_limit_bytes=48 * 1024 * 1024),
        cost_estimate=pl.CostEstimate(
            flops=2 * rows * features * outputs,
            bytes_accessed=2 * (features + rows) * outputs,
            transcendentals=0,
        ),
        name="project",
    )(turn, span_live, *parts, out_weight, after)


def add_kernel(cuts, kept_ref, *refs):
    come_refs, out_refs = refs[:cuts], refs[cuts:]
    width = kept_ref.shape[2] // cuts
    for k in range(kept_ref.shape[0] - 1):
        for cut, come_ref in enumerate(come_refs):
            kept = kept_ref[k + 1, :, cut * width : (cut + 1) * width].astype(jnp.float32)
            out_refs[k * cuts + cut][...] = (kept + come_ref[k].astype(jnp.float32)).astype(
                jnp.bfloat16
            )


def total_kernel(counts, *refs):
    out_ref = refs[-1]
    block, width = out_ref.shape[0] // HALVES, out_ref.shape[1]
    first = 0
    for h, (others, cuts) in enumerate(counts):
        kept_ref, near_ref = refs[first : first + 2]
        arrived = refs[first + 2 : first + 2 + others]
        first += 2 + others
        for cut in range(cuts):
            at = slice(cut * width // cuts, (cut + 1) * width // cuts)
            total = kept_ref[0, :, at].astype(jnp.float32) + near_ref[:, at].astype(jnp.float32)
            for ref in arrived[cut::cuts]:
                total += ref[...].astype(jnp.float32)
            out_ref[h * block : (h + 1) * block, at] = total.astype(jnp.bfloat16)


def add_cores(near, aways, keep, members):
    chips, block, outputs = keep.shape
    cuts = len(aways)
    shape = jax.ShapeDtypeStruct((block, outputs // cuts), jnp.bfloat16)
    pairs = [(i, i ^ 1) for i in range(members)]
    come = [lax.ppermute(away, "tp", pairs) for away in aways]
    near = lax.ppermute(near, "tp", pairs)
    sums = pl.pallas_call(
        functools.partial(add_kernel, cuts),
        out_shape=[shape] * ((chips - 1) * cuts),
        in_specs=[VMEM] * (1 + cuts),
        out_specs=[VMEM] * ((chips - 1) * cuts),
        compiler_params=pltpu.CompilerParams(vmem_limit_bytes=VMEM_LIMIT),
        name="add_cores",
    )(keep, *come)
    return near, sums


def add_chips(sums, cuts, members):
    return [
        lax.ppermute(
            each, "tp", [(i, (i + 2 * (n // cuts + 1)) % members) for i in range(members)]
        )
        for n, each in enumerate(sums)
    ]


def total_sums(terms, counts, block, outputs):
    return pl.pallas_call(
        functools.partial(total_kernel, counts),
        out_shape=jax.ShapeDtypeStruct((HALVES * block, outputs), jnp.bfloat16),
        in_specs=[VMEM] * len(terms),
        out_specs=VMEM,
        compiler_params=pltpu.CompilerParams(vmem_limit_bytes=VMEM_LIMIT),
        name="total",
    )(*terms)


def pack_kernel(me_ref, span_live_ref, owners_ref, span_ref, *refs):
    out_refs, (out_ref, counts_ref) = refs[:-2], refs[-2:]
    peers = out_ref.shape[0]
    block_rows, head_dim = out_ref.shape[3:]
    out_ref[...] = jnp.zeros_like(out_ref)
    for k in range(peers):
        counts_ref[k] = 0
    row = lax.broadcasted_iota(jnp.int32, (block_rows, head_dim), 0)
    for b in range(span_ref.shape[1] // block_rows):
        owner = owners_ref[b]
        rank = counts_ref[owner]
        counts_ref[owner] = rank + 1
        keep = row + b * block_rows < span_live_ref[0]
        for side in range(2):
            block = span_ref[side, b * block_rows : (b + 1) * block_rows, :]
            out_ref[owner, side, rank] = jnp.where(keep, block, jnp.zeros_like(block))
    for k, each_ref in enumerate(out_refs):
        each_ref[...] = out_ref[me_ref[0] ^ k]


def unpack_kernel(me_ref, *refs):
    for k, each_ref in enumerate(refs[:-1]):
        refs[-1][:, me_ref[0] ^ k] = each_ref[...]


def shards(
    queries,
    cache_store,
    span_cache,
    out_weight,
    prefix_blocks,
    span_lengths,
    hit_holders,
    hit_slots,
    store_owners,
):
    peers = lax.axis_size("inst")
    block_rows, head_dim = cache_store.shape[2:]
    rows, columns = queries.shape
    heads = columns // head_dim
    block_max = hit_slots.shape[1]
    cap = max(2, block_max * 5 // (4 * peers))
    new_count = rows // block_rows
    push_cap = max(2, 2 * new_count // peers)
    scale = math.log2(math.e) / math.sqrt(head_dim)
    me = lax.axis_index("inst").reshape(1)
    width = round_up(cap + 1, 128)
    members = lax.axis_size("tp")
    some = rows // HALVES
    part_shape = jax.ShapeDtypeStruct((some + TAIL, columns), jnp.bfloat16)
    params = pltpu.CompilerParams(vmem_limit_bytes=VMEM_LIMIT)
    anywhere = pl.BlockSpec(memory_space=pl.ANY)

    def exchange(value, bit):
        return lax.ppermute(value, "inst", [(i, i ^ bit) for i in range(peers)])

    order = sorted(range(1, peers), key=lambda k: -(k & -k))

    def spread(loaded, after, near=None):
        held = {0: loaded}
        for k in order:
            if k == 1 and near is not None:
                held[k] = near
                continue
            source = held[k & (k - 1)]
            if k & (k - 1):
                source, after = lax.optimization_barrier((source, after))
            held[k] = exchange(source, k & -k)
        return held, after

    def guests(held, group, after):
        return pl.pallas_call(
            functools.partial(guest_kernel, scale, width, some, len(group)),
            out_shape=[part_shape] * len(group),
            in_specs=[SMEM] + [VMEM] * (len(group) + 1) + [anywhere],
            out_specs=[VMEM] * len(group),
            scratch_shapes=[
                pltpu.VMEM((len(group), width), jnp.int32),
                pltpu.SMEM((len(group), width), jnp.int32),
                pltpu.SemaphoreType.DMA,
                *attention_scratch(heads, some, head_dim, block_rows),
            ],
            compiler_params=params,
            cost_estimate=attention_cost(some, rows // 2, head_dim, heads),
            name="guest_attention",
        )(me, *[held[k] for k in group], cache_store, after)

    def gather_back(parts, after):
        parts = dict(parts)
        for k in reversed(order):
            arrived = [exchange(parts[c], c & -c) for c in order if c & (c - 1) == k]
            if arrived:
                parts[k] = after = pl.pallas_call(
                    functools.partial(merge_kernel, heads, len(arrived) + 1),
                    out_shape=part_shape,
                    in_specs=[VMEM] * (len(arrived) + 1) + [anywhere],
                    out_specs=VMEM,
                    compiler_params=params,
                    name="merge",
                )(parts[k], *arrived, after)
        parts[1], after = lax.optimization_barrier((parts[1], after))
        return [exchange(parts[k], k) for k in order if k & (k - 1) == 0], after

    lists, *loaded = route(
        prefix_blocks, hit_holders.reshape(1, -1), hit_slots, queries, peers, width, members
    )
    own = pl.pallas_call(
        functools.partial(own_kernel, scale, members),
        out_shape=[part_shape] * HALVES,
        in_specs=[SMEM, SMEM, SMEM, HBM, HBM, HBM],
        out_specs=[VMEM] * HALVES,
        scratch_shapes=[
            pltpu.VMEM((HALVES, some, columns), jnp.bfloat16),
            pltpu.VMEM(cache_store.shape, jnp.bfloat16),
            pltpu.VMEM(span_cache.shape, jnp.bfloat16),
            pltpu.SemaphoreType.DMA((2 + HALVES * members,)),
            *attention_scratch(heads, rows, head_dim, block_rows),
        ],
        compiler_params=params,
        cost_estimate=attention_cost(rows, 8 * rows, head_dim, heads),
        name="own_attention",
    )(me, span_lengths, lists, queries, cache_store, span_cache)

    own = list(own)
    before, arrived = None, []
    held, after = spread(loaded[0], own[0])
    nears = [None] + [exchange(each, 1) for each in loaded[1:]]
    *loaded[1:], after = lax.optimization_barrier((*loaded[1:], after))
    for h in range(HALVES):
        if h + 1 < HALVES:
            groups = [order[i : i + 2] for i in range(0, peers - 1, 2)]
        else:
            groups = [[k] for k in reversed(order) if k > 1] + [[1]]
            held[1], after = lax.optimization_barrier((held[1], after))
        parts, following = {}, None
        for index, group in enumerate(groups):
            results = guests(held, group, after)
            after = results[0]
            parts.update(zip(group, results))
            if index == 0 and h + 1 < HALVES:
                following, after = spread(loaded[h + 1], after, nears[h + 1])
            if index == 0 and before is not None:
                back, after = gather_back(before, after)
                arrived.append(back)
        before, held = parts, following
    back, after = gather_back(before, after)
    arrived.append(back)

    turn = lax.axis_index("tp").reshape(1)
    terms, counts = [], []
    for h in range(HALVES):
        parts = [own[h], *arrived[h]]
        cuts = 1
        near, *aways, keep = project(
            turn, span_lengths, parts, out_weight, after, heads, h, members, cuts
        )
        near, sums = add_cores(near, aways, keep, members)
        if h + 1 == HALVES:
            near, *sums = lax.optimization_barrier((near, *sums))
        crossed = add_chips(sums, cuts, members)
        if h + 1 < HALVES:
            own[h + 1], near, after = lax.optimization_barrier((own[h + 1], near, sums[0]))
        if h + 1 == HALVES:
            keep, span_cache = lax.optimization_barrier((keep, span_cache))
        terms += [keep, near, *crossed]
        counts.append((len(crossed), cuts))
    projected = total_sums(terms, counts, some // members, out_weight.shape[1])

    push_shape = jax.ShapeDtypeStruct((2, push_cap, block_rows, head_dim), jnp.bfloat16)
    outgoing = pl.pallas_call(
        pack_kernel,
        out_shape=[push_shape] * peers,
        in_specs=[SMEM, SMEM, SMEM, VMEM],
        out_specs=[VMEM] * peers,
        scratch_shapes=[
            pltpu.VMEM((peers, *push_shape.shape), jnp.bfloat16),
            pltpu.SMEM((peers,), jnp.int32),
        ],
        compiler_params=params,
        name="pack_blocks",
    )(me, span_lengths, store_owners.reshape(-1), span_cache)
    incoming = [outgoing[0], *[exchange(outgoing[k], k) for k in range(1, peers)]]
    pushed_blocks = pl.pallas_call(
        unpack_kernel,
        out_shape=jax.ShapeDtypeStruct(
            (2, peers, push_cap, block_rows, head_dim), jnp.bfloat16
        ),
        in_specs=[SMEM] + [VMEM] * peers,
        out_specs=VMEM,
        compiler_params=params,
        name="unpack_blocks",
    )(me, *incoming).reshape(2, peers * push_cap, block_rows, head_dim)
    return (projected, pushed_blocks)


def solution(mesh):
    return jax.shard_map(
        shards,
        mesh=mesh,
        in_specs=(
            P(("pods", "inst"), "tp"),
            P(None, ("pods", "inst"), None, "tp"),
            P(None, ("pods", "inst"), "tp"),
            P("tp", None),
            P(("pods", "inst")),
            P(("pods", "inst")),
            P(("pods", "inst"), None, None),
            P(("pods", "inst"), None),
            P(("pods", "inst"), None, None),
        ),
        out_specs=(P(("pods", "inst", "tp"), None), P(None, ("pods", "inst"), None, "tp")),
        check_vma=False,
    )
```

```python
import functools
import math

import jax
import jax.numpy as jnp
from jax import lax
from jax.experimental import pallas as pl
from jax.experimental.pallas import tpu as pltpu
from jax.sharding import PartitionSpec as P

LOW = -1e30
TOP = 2.0**100
TILE = 32
STACK = 512
HALVES = 2
TAIL = 8
VMEM_LIMIT = 20 * 1024 * 1024

SMEM = pl.BlockSpec(memory_space=pltpu.SMEM)
VMEM = pl.BlockSpec(memory_space=pltpu.VMEM)
HBM = pl.BlockSpec(memory_space=pltpu.HBM)


def round_up(number, step):
    return -(-number // step) * step


def original_row(row, h, members, own_rows):
    each = own_rows // HALVES
    member = sum((row >= m * each).astype(jnp.int32) for m in range(1, members))
    return row + member * (own_rows - each) + h * each


def route_kernel(
    members, live_ref, holders_in, slots_in, q_in, lists_ref, *refs
):
    out_refs, (holders_ref, slots_ref, sems) = refs[:HALVES], refs[HALVES:]
    columns = q_in.shape[1]
    rows = q_in.shape[0] // HALVES
    each = rows // members
    loading = [
        pltpu.make_async_copy(holders_in, holders_ref, sems.at[0]),
        pltpu.make_async_copy(slots_in, slots_ref, sems.at[1]),
    ]
    passing = [
        pltpu.make_async_copy(
            q_in.at[pl.ds((m * HALVES + h) * each, each)],
            out_refs[h].at[pl.ds(m * each, each)],
            sems.at[2 + h * members + m],
        )
        for h in range(HALVES)
        for m in range(members)
    ]
    for copy in loading + passing:
        copy.start()
    for copy in loading:
        copy.wait()
    peers, width = lists_ref.shape
    number = holders_ref.shape[1]
    padded = round_up(peers, 16)
    holder = lax.broadcasted_iota(jnp.int32, (padded, number), 0)
    entry = lax.broadcasted_iota(jnp.int32, (padded, number), 1)
    hot = (holders_ref[...] == holder) & (entry < live_ref[0])
    ones = jnp.where(hot, 1.0, 0.0)
    earlier = lax.broadcasted_iota(jnp.int32, (number, number), 0) < lax.broadcasted_iota(
        jnp.int32, (number, number), 1
    )
    ranks = jnp.dot(
        ones.astype(jnp.bfloat16),
        jnp.where(earlier, 1.0, 0.0).astype(jnp.bfloat16),
        preferred_element_type=jnp.float32,
    )
    rank = jnp.sum(ranks * ones, axis=0, keepdims=True)
    rank = jnp.broadcast_to(rank, (8, number)).T[:, :1].astype(jnp.int32)
    place = lax.broadcasted_iota(jnp.int32, (number, width), 1) == rank
    slots = jnp.where(hot, slots_ref[...], 0).astype(jnp.float32)
    lists = jnp.dot(
        slots.astype(jnp.bfloat16),
        jnp.where(place, 1.0, 0.0).astype(jnp.bfloat16),
        preferred_element_type=jnp.float32,
    )
    counts = jnp.sum(ones, axis=1, keepdims=True)
    last = lax.broadcasted_iota(jnp.int32, (padded, width), 1) == width - 1
    lists = jnp.where(last, counts, lists)[:peers]
    lists_ref[...] = lists.astype(jnp.int32)

    lines = columns // width
    row = lax.broadcasted_iota(jnp.int32, (TAIL, columns), 0)
    tail = jnp.zeros((TAIL, columns), jnp.float32)
    for r in range(-(-peers // lines)):
        line = [lists[h : h + 1] for h in range(r * lines, min(peers, (r + 1) * lines))]
        line += [jnp.zeros((1, width), jnp.float32)] * (lines - len(line))
        tail = jnp.where(row == r, jnp.concatenate(line, axis=1), tail)
    for out_ref in out_refs:
        out_ref[rows:, :] = tail.astype(jnp.bfloat16)
    for copy in passing:
        copy.wait()


def route(live, holders, slots, queries, peers, width, members):
    rows, columns = queries.shape[0] // HALVES, queries.shape[1]
    return pl.pallas_call(
        functools.partial(route_kernel, members),
        out_shape=(
            jax.ShapeDtypeStruct((peers, width), jnp.int32),
            *[jax.ShapeDtypeStruct((rows + TAIL, columns), jnp.bfloat16)] * HALVES,
        ),
        in_specs=[SMEM, HBM, HBM, HBM],
        out_specs=[VMEM] * (1 + HALVES),
        scratch_shapes=[
            pltpu.VMEM(holders.shape, jnp.int32),
            pltpu.VMEM(slots.shape, jnp.int32),
            pltpu.SemaphoreType.DMA((2 + HALVES * members,)),
        ],
        compiler_params=pltpu.CompilerParams(vmem_limit_bytes=62 * 1024 * 1024),
        name="route",
    )(live, holders, slots, queries)


def score(q, keys):
    return lax.dot_general(q, keys, (((1,), (1,)), ((), ())), preferred_element_type=jnp.float32)


def wide(value, width):
    return jnp.concatenate([value] * (width // value.shape[1]), axis=1)


def attend(
    slot, count, store_ref, span_ref, masks, q_ref, k_ref, v_ref, s_ref, ref_ref, acc_ref, rows,
    scale, stored=None,
):
    block_rows, head_dim = store_ref.shape[2:]
    heads = q_ref.shape[0] // rows
    stack = s_ref.shape[0]
    stacks = q_ref.shape[0] // stack
    tiles = (count + TILE - 1) // TILE

    def fetch(tile, into):
        for j in range(TILE):
            index = tile * TILE + j
            here = slot(jnp.minimum(index, count - 1))
            at = slice(j * block_rows, (j + 1) * block_rows)
            k_ref[into, at, :] = store_ref[0, here]
            block = store_ref[1, here]
            v_ref[into, at, :head_dim] = jnp.where(index < count, block, jnp.zeros_like(block))
            v_ref[into, at, head_dim:] = jnp.where(
                index < count, jnp.ones_like(block), jnp.zeros_like(block)
            )

    def one_key(key_row):
        row = key_row.astype(jnp.float32)[:1]
        return score(
            q_ref[...], jnp.broadcast_to(row, (head_dim, head_dim)).astype(jnp.bfloat16)
        )

    def start(exact):
        if span_ref is None:
            acc_ref[...] = jnp.zeros_like(acc_ref)
            if exact:
                ref_ref[...] = jnp.full_like(ref_ref, LOW)
            return
        keys = span_ref.shape[1]
        values = jnp.concatenate(
            [span_ref[1], jnp.ones((keys, head_dim), jnp.bfloat16)], axis=1
        )
        if not exact:
            ref_ref[...] = one_key(span_ref[0, :16, :])
        s = score(q_ref[:rows, :], span_ref[0])
        for g in range(heads):
            at = slice(g * rows, (g + 1) * rows)
            if g + 1 < heads:
                following = score(q_ref[(g + 1) * rows : (g + 2) * rows, :], span_ref[0])
            mask = masks[g * HALVES // heads]
            if exact:
                top = jnp.max(jnp.where(mask, s, LOW), axis=1, keepdims=True)
                ref_ref[at, :] = jnp.broadcast_to(top, (rows, head_dim))
            p = jnp.exp2((s - wide(ref_ref[at, :], keys)) * scale)
            p = jnp.where(mask, p, 0.0).astype(jnp.bfloat16)
            acc_ref[at, :] = jnp.dot(p, values, preferred_element_type=jnp.float32)
            s = following

    start(False)
    if stored is not None:
        stored()

    @pl.when(count > 0)
    def _():
        fetch(0, 0)
        if span_ref is None:
            ref_ref[...] = one_key(k_ref[0, :16, :])
        s_ref[...] = score(q_ref[:stack, :], k_ref[0])

        def step(tile, carry):
            now = lax.rem(tile, 2)
            later = 1 - now
            keys, values = k_ref[now], v_ref[now]
            s = s_ref[...]
            fetch(tile + 1, later)
            for c in range(stacks):
                at = slice(c * stack, (c + 1) * stack)
                if c + 1 < stacks:
                    following = score(q_ref[(c + 1) * stack : (c + 2) * stack, :], keys)
                else:
                    s_ref[...] = score(q_ref[:stack, :], k_ref[later])
                p = jnp.exp2((s - wide(ref_ref[at, :], s.shape[1])) * scale).astype(jnp.bfloat16)
                acc_ref[at, :] += jnp.dot(p, values, preferred_element_type=jnp.float32)
                s = following
            return carry

        lax.fori_loop(0, tiles, step, 0)
    beyond = jnp.max(jnp.where(acc_ref[:, head_dim:] < TOP, 0.0, 1.0))

    @pl.when(beyond > 0.0)
    def _():
        start(True)

        def careful(tile, carry):
            fetch(tile, 0)

            def head(g, inner):
                at = pl.ds(pl.multiple_of(g * rows, rows), rows)
                s = score(q_ref[at, :], k_ref[0])
                old = ref_ref[at, :]
                new = jnp.maximum(old, jnp.max(s, axis=1, keepdims=True))
                p = jnp.exp2((s - wide(new, s.shape[1])) * scale).astype(jnp.bfloat16)
                update = jnp.dot(p, v_ref[0], preferred_element_type=jnp.float32)
                acc_ref[at, :] = acc_ref[at, :] * wide(jnp.exp2((old - new) * scale), 2 * head_dim) + update
                ref_ref[at, :] = new
                return inner

            return lax.fori_loop(0, heads, head, carry)

        lax.fori_loop(0, tiles, careful, 0)


def stack_heads(queries_ref, q_ref, rows, first=0):
    head_dim = q_ref.shape[1]
    for g in range(queries_ref.shape[1] // head_dim):
        q_ref[(first + g) * rows : (first + g + 1) * rows, :] = queries_ref[
            :rows, g * head_dim : (g + 1) * head_dim
        ]


def write_logs(out_ref, logs):
    heads, rows = logs.shape
    first = logs.astype(jnp.bfloat16).astype(jnp.float32)
    rest = logs - first
    second = rest.astype(jnp.bfloat16).astype(jnp.float32)
    third = rest - second
    spare = jnp.zeros((heads, out_ref.shape[1] - 3 * rows), jnp.float32)
    lines = jnp.concatenate([first, second, third, spare], axis=1)
    if heads < TAIL:
        more = jnp.zeros((TAIL - heads, out_ref.shape[1]), jnp.float32)
        lines = jnp.concatenate([lines, more], axis=0)
    out_ref[rows:, :] = lines.astype(jnp.bfloat16)


def read_logs(part_ref, heads, rows):
    lines = part_ref[rows:, :].astype(jnp.float32)[:heads]
    return lines[:, :rows] + lines[:, rows : 2 * rows] + lines[:, 2 * rows : 3 * rows]


def finish(out_refs, ref_ref, acc_ref, rows, scale):
    head_dim = ref_ref.shape[1]
    heads = ref_ref.shape[0] // rows // len(out_refs)
    lane = lax.broadcasted_iota(jnp.int32, (rows, head_dim), 1)
    for h, out_ref in enumerate(out_refs):
        totals = jnp.ones((rows, head_dim), jnp.float32)
        tops = jnp.zeros((rows, head_dim), jnp.float32)
        for g in range(heads):
            at = slice((h * heads + g) * rows, (h * heads + g + 1) * rows)
            total = acc_ref[at, head_dim:]
            inverse = pl.reciprocal(total, approx=True)
            inverse = inverse * (2.0 - total * inverse)
            out_ref[:rows, g * head_dim : (g + 1) * head_dim] = (
                acc_ref[at, :head_dim] * inverse
            ).astype(jnp.bfloat16)
            totals = jnp.where(lane == g, total, totals)
            tops = jnp.where(lane == g, ref_ref[at, :], tops)
        logs = tops * scale + jnp.log2(totals)
        write_logs(out_ref, logs.T[:heads])


def own_kernel(
    scale, members, me_ref, span_live_ref, lists_ref, queries_in, store_in, span_in, *refs
):
    out_refs = refs[:HALVES]
    queries_ref, store_ref, span_ref, sems, q_ref, k_ref, v_ref, s_ref, ref_ref, acc_ref = refs[
        HALVES:
    ]
    me = me_ref[0]
    rows = queries_ref.shape[1]
    each = rows // members
    copies = [
        pltpu.make_async_copy(span_in, span_ref, sems.at[0]),
        pltpu.make_async_copy(store_in, store_ref, sems.at[1]),
    ] + [
        pltpu.make_async_copy(
            queries_in.at[pl.ds((m * HALVES + h) * each, each)],
            queries_ref.at[h, pl.ds(m * each, each)],
            sems.at[2 + h * members + m],
        )
        for h in range(HALVES)
        for m in range(members)
    ]
    for copy in copies:
        copy.start()
    keys = span_ref.shape[1]
    key = lax.broadcasted_iota(jnp.int32, (rows, keys), 1)
    row = lax.broadcasted_iota(jnp.int32, (rows, keys), 0)
    masks = [
        (key <= original_row(row, h, members, each * HALVES)) & (key < span_live_ref[0])
        for h in range(HALVES)
    ]
    for copy in copies[2:]:
        copy.wait()
    for h in range(HALVES):
        stack_heads(queries_ref.at[h], q_ref, rows, h * queries_ref.shape[2] // q_ref.shape[1])
    copies[0].wait()
    attend(
        lambda index: lists_ref[me, index], lists_ref[me, lists_ref.shape[1] - 1], store_ref,
        span_ref, masks, q_ref, k_ref, v_ref, s_ref, ref_ref, acc_ref, rows, scale,
        copies[1].wait,
    )
    finish(out_refs, ref_ref, acc_ref, rows, scale)


def guest_kernel(scale, width, rows, number, me_ref, *refs):
    loaded_refs, store_ref = refs[:number], refs[number]
    out_refs = refs[number + 2 : 2 * number + 2]
    wide_ref, list_ref, sem_ref, q_ref, k_ref, v_ref, s_ref, ref_ref, acc_ref = refs[
        2 * number + 2 :
    ]
    each = loaded_refs[0].shape[1] // width
    me = me_ref[0]
    lane = pl.multiple_of(lax.rem(me, each) * width, 128)
    for which, loaded_ref in enumerate(loaded_refs):
        riders = loaded_ref[rows:, pl.ds(lane, width)].astype(jnp.float32)
        row = lax.broadcasted_iota(jnp.int32, riders.shape, 0)
        mine = jnp.sum(jnp.where(row == me // each, riders, 0.0), axis=0, keepdims=True)
        wide_ref[which : which + 1, :] = mine.astype(jnp.int32)
    copy = pltpu.make_async_copy(wide_ref, list_ref, sem_ref)
    copy.start()
    stack_heads(loaded_refs[0], q_ref, rows)
    copy.wait()
    for which, (loaded_ref, out_ref) in enumerate(zip(loaded_refs, out_refs)):
        count = list_ref[which, width - 1]

        @pl.when(count > 0)
        def _():
            if which:
                stack_heads(loaded_ref, q_ref, rows)
            attend(
                lambda index: list_ref[which, index], count, store_ref, None, None,
                q_ref, k_ref, v_ref, s_ref, ref_ref, acc_ref, rows, scale,
            )
            finish([out_ref], ref_ref, acc_ref, rows, scale)

        @pl.when(count == 0)
        def _():
            out_ref[...] = jnp.zeros_like(out_ref)
            write_logs(out_ref, jnp.full((q_ref.shape[0] // rows, rows), LOW, jnp.float32))


def attention_scratch(heads, rows, head_dim, block_rows):
    keys = TILE * block_rows
    return [
        pltpu.VMEM((heads * rows, head_dim), jnp.bfloat16),
        pltpu.VMEM((2, keys, head_dim), jnp.bfloat16),
        pltpu.VMEM((2, keys, 2 * head_dim), jnp.bfloat16),
        pltpu.VMEM((math.gcd(heads * rows, STACK), keys), jnp.float32),
        pltpu.VMEM((heads * rows, head_dim), jnp.float32),
        pltpu.VMEM((heads * rows, 2 * head_dim), jnp.float32),
    ]


def attention_cost(rows, keys, head_dim, heads):
    return pl.CostEstimate(
        flops=4 * rows * keys * head_dim * heads,
        bytes_accessed=64 * 1024,
        transcendentals=rows * keys * heads,
    )


def merged(parts, heads, rows):
    logs = [read_logs(part, heads, rows) for part in parts]
    top = functools.reduce(jnp.maximum, logs)
    weights = [jnp.exp2(log - top) for log in logs]
    total = functools.reduce(jnp.add, weights)
    return [weight / total for weight in weights], top + jnp.log2(total)


def weighted(parts, weights, g, head_dim, rows):
    total = jnp.zeros((rows, head_dim), jnp.float32)
    for part, weight in zip(parts, weights):
        part_rows = part[:rows, g * head_dim : (g + 1) * head_dim]
        total += part_rows.astype(jnp.float32) * weight[:, g : g + 1]
    return total.astype(jnp.bfloat16)


def merge_kernel(heads, number, *refs):
    parts, out_ref = refs[:number], refs[number + 1]
    rows = out_ref.shape[0] - TAIL
    head_dim = out_ref.shape[1] // heads
    weights, logs = merged(parts, heads, rows)
    weights = [weight.T for weight in weights]
    for g in range(heads):
        out_ref[:rows, g * head_dim : (g + 1) * head_dim] = weighted(
            parts, weights, g, head_dim, rows
        )
    write_logs(out_ref, logs)


def project_kernel(heads, number, h, members, cuts, turn_ref, span_live_ref, *refs):
    parts = refs[:number]
    weight_ref, after_ref, near_ref, *away_refs = refs[number : number + 3 + cuts]
    keep_ref, att_ref, sorted_ref, held_ref, sems = refs[number + 3 + cuts :]
    rows, features = att_ref.shape
    chunks, _, width = held_ref.shape
    head_dim = features // heads
    copies = [
        pltpu.make_async_copy(weight_ref.at[:, pl.ds(i * width, width)], held_ref.at[i], sems.at[i])
        for i in range(chunks)
    ]
    for copy in copies:
        copy.start()

    row = lax.broadcasted_iota(jnp.int32, (heads, rows), 1)
    live = original_row(row, h, members, rows * HALVES // members) < span_live_ref[0]
    weights, _ = merged(parts, heads, rows)
    weights = [jnp.where(live, weight, 0.0).T for weight in weights]
    for g in range(heads):
        att_ref[:, g * head_dim : (g + 1) * head_dim] = weighted(
            parts, weights, g, head_dim, rows
        )

    chips = keep_ref.shape[0]
    block = keep_ref.shape[1]
    chip, core = turn_ref[0] // 2, lax.rem(turn_ref[0], 2)
    for side, wanted in enumerate((1 - core, core)):
        for k in range(chips):
            owner = 2 * lax.rem(chip + k, chips) + wanted
            at = (side * chips + k) * block
            sorted_ref[at : at + block, :] = att_ref[
                pl.ds(pl.multiple_of(owner * block, block), block), :
            ]
    for i in range(chunks):
        copies[i].wait()
        at = slice(i * width, (i + 1) * width)
        product = jnp.dot(
            sorted_ref[...], held_ref[i], preferred_element_type=jnp.float32
        ).astype(jnp.bfloat16)
        for k in range(chips):
            leaving = product[k * block : (k + 1) * block]
            if k:
                cut = i * cuts // chunks
                first = i * width - cut * away_refs[cut].shape[2]
                away_refs[cut][k - 1, :, first : first + width] = leaving
            else:
                near_ref[:, at] = leaving
            keep_ref[k, :, at] = product[(chips + k) * block : (chips + k + 1) * block]


def project(turn, span_live, parts, out_weight, after, heads, h, members, cuts):
    features, outputs = out_weight.shape
    rows = parts[0].shape[0] - TAIL
    width = 512
    chunks = outputs // width
    chips, block = members // 2, rows // members
    return pl.pallas_call(
        functools.partial(project_kernel, heads, len(parts), h, members, cuts),
        out_shape=[
            jax.ShapeDtypeStruct(shape, jnp.bfloat16)
            for shape in (
                (block, outputs),
                *[(chips - 1, block, outputs // cuts)] * cuts,
                (chips, block, outputs),
            )
        ],
        in_specs=[SMEM, SMEM] + [VMEM] * len(parts) + [HBM, pl.BlockSpec(memory_space=pl.ANY)],
        out_specs=[VMEM] * (2 + cuts),
        scratch_shapes=[
            pltpu.VMEM((rows, features), jnp.bfloat16),
            pltpu.VMEM((rows, features), jnp.bfloat16),
            pltpu.VMEM((chunks, features, width), jnp.bfloat16),
            pltpu.SemaphoreType.DMA((chunks,)),
        ],
        compiler_params=pltpu.CompilerParams(vmem_limit_bytes=48 * 1024 * 1024),
        cost_estimate=pl.CostEstimate(
            flops=2 * rows * features * outputs,
            bytes_accessed=2 * (features + rows) * outputs,
            transcendentals=0,
        ),
        name="project",
    )(turn, span_live, *parts, out_weight, after)


def add_kernel(cuts, kept_ref, *refs):
    come_refs, out_refs = refs[:cuts], refs[cuts:]
    width = kept_ref.shape[2] // cuts
    for k in range(kept_ref.shape[0] - 1):
        for cut, come_ref in enumerate(come_refs):
            kept = kept_ref[k + 1, :, cut * width : (cut + 1) * width].astype(jnp.float32)
            out_refs[k * cuts + cut][...] = (kept + come_ref[k].astype(jnp.float32)).astype(
                jnp.bfloat16
            )


def total_kernel(counts, *refs):
    out_ref = refs[-1]
    block, width = out_ref.shape[0] // HALVES, out_ref.shape[1]
    first = 0
    for h, (others, cuts) in enumerate(counts):
        kept_ref, near_ref = refs[first : first + 2]
        arrived = refs[first + 2 : first + 2 + others]
        first += 2 + others
        for cut in range(cuts):
            at = slice(cut * width // cuts, (cut + 1) * width // cuts)
            total = kept_ref[0, :, at].astype(jnp.float32) + near_ref[:, at].astype(jnp.float32)
            for ref in arrived[cut::cuts]:
                total += ref[...].astype(jnp.float32)
            out_ref[h * block : (h + 1) * block, at] = total.astype(jnp.bfloat16)


def add_cores(near, aways, keep, members):
    chips, block, outputs = keep.shape
    cuts = len(aways)
    shape = jax.ShapeDtypeStruct((block, outputs // cuts), jnp.bfloat16)
    pairs = [(i, i ^ 1) for i in range(members)]
    come = [lax.ppermute(away, "tp", pairs) for away in aways]
    near = lax.ppermute(near, "tp", pairs)
    sums = pl.pallas_call(
        functools.partial(add_kernel, cuts),
        out_shape=[shape] * ((chips - 1) * cuts),
        in_specs=[VMEM] * (1 + cuts),
        out_specs=[VMEM] * ((chips - 1) * cuts),
        compiler_params=pltpu.CompilerParams(vmem_limit_bytes=VMEM_LIMIT),
        name="add_cores",
    )(keep, *come)
    return near, sums


def add_chips(sums, cuts, members):
    return [
        lax.ppermute(
            each, "tp", [(i, (i + 2 * (n // cuts + 1)) % members) for i in range(members)]
        )
        for n, each in enumerate(sums)
    ]


def total_sums(terms, counts, block, outputs):
    return pl.pallas_call(
        functools.partial(total_kernel, counts),
        out_shape=jax.ShapeDtypeStruct((HALVES * block, outputs), jnp.bfloat16),
        in_specs=[VMEM] * len(terms),
        out_specs=VMEM,
        compiler_params=pltpu.CompilerParams(vmem_limit_bytes=VMEM_LIMIT),
        name="total",
    )(*terms)


def pack_kernel(me_ref, span_live_ref, owners_ref, span_ref, *refs):
    out_refs, (out_ref, counts_ref) = refs[:-2], refs[-2:]
    peers = out_ref.shape[0]
    block_rows, head_dim = out_ref.shape[3:]
    out_ref[...] = jnp.zeros_like(out_ref)
    for k in range(peers):
        counts_ref[k] = 0
    row = lax.broadcasted_iota(jnp.int32, (block_rows, head_dim), 0)
    for b in range(span_ref.shape[1] // block_rows):
        owner = owners_ref[b]
        rank = counts_ref[owner]
        counts_ref[owner] = rank + 1
        keep = row + b * block_rows < span_live_ref[0]
        for side in range(2):
            block = span_ref[side, b * block_rows : (b + 1) * block_rows, :]
            out_ref[owner, side, rank] = jnp.where(keep, block, jnp.zeros_like(block))
    for k, each_ref in enumerate(out_refs):
        each_ref[...] = out_ref[me_ref[0] ^ k]


def unpack_kernel(me_ref, *refs):
    for k, each_ref in enumerate(refs[:-1]):
        refs[-1][:, me_ref[0] ^ k] = each_ref[...]


def shards(
    queries,
    cache_store,
    span_cache,
    out_weight,
    prefix_blocks,
    span_lengths,
    hit_holders,
    hit_slots,
    store_owners,
):
    peers = lax.axis_size("inst")
    block_rows, head_dim = cache_store.shape[2:]
    rows, columns = queries.shape
    heads = columns // head_dim
    block_max = hit_slots.shape[1]
    cap = max(2, block_max * 5 // (4 * peers))
    new_count = rows // block_rows
    push_cap = max(2, 2 * new_count // peers)
    scale = math.log2(math.e) / math.sqrt(head_dim)
    me = lax.axis_index("inst").reshape(1)
    width = round_up(cap + 1, 128)
    members = lax.axis_size("tp")
    some = rows // HALVES
    part_shape = jax.ShapeDtypeStruct((some + TAIL, columns), jnp.bfloat16)
    params = pltpu.CompilerParams(vmem_limit_bytes=VMEM_LIMIT)
    anywhere = pl.BlockSpec(memory_space=pl.ANY)

    def exchange(value, bit):
        return lax.ppermute(value, "inst", [(i, i ^ bit) for i in range(peers)])

    order = sorted(range(1, peers), key=lambda k: -(k & -k))

    def spread(loaded, after, near=None):
        held = {0: loaded}
        for k in order:
            if k == 1 and near is not None:
                held[k] = near
                continue
            source = held[k & (k - 1)]
            if k & (k - 1):
                source, after = lax.optimization_barrier((source, after))
            held[k] = exchange(source, k & -k)
        return held, after

    def guests(held, group, after):
        return pl.pallas_call(
            functools.partial(guest_kernel, scale, width, some, len(group)),
            out_shape=[part_shape] * len(group),
            in_specs=[SMEM] + [VMEM] * (len(group) + 1) + [anywhere],
            out_specs=[VMEM] * len(group),
            scratch_shapes=[
                pltpu.VMEM((len(group), width), jnp.int32),
                pltpu.SMEM((len(group), width), jnp.int32),
                pltpu.SemaphoreType.DMA,
                *attention_scratch(heads, some, head_dim, block_rows),
            ],
            compiler_params=params,
            cost_estimate=attention_cost(some, rows // 2, head_dim, heads),
            name="guest_attention",
        )(me, *[held[k] for k in group], cache_store, after)

    def gather_back(parts, after):
        parts = dict(parts)
        for k in reversed(order):
            arrived = [exchange(parts[c], c & -c) for c in order if c & (c - 1) == k]
            if arrived:
                parts[k] = after = pl.pallas_call(
                    functools.partial(merge_kernel, heads, len(arrived) + 1),
                    out_shape=part_shape,
                    in_specs=[VMEM] * (len(arrived) + 1) + [anywhere],
                    out_specs=VMEM,
                    compiler_params=params,
                    name="merge",
                )(parts[k], *arrived, after)
        parts[1], after = lax.optimization_barrier((parts[1], after))
        return [exchange(parts[k], k) for k in order if k & (k - 1) == 0], after

    lists, *loaded = route(
        prefix_blocks, hit_holders.reshape(1, -1), hit_slots, queries, peers, width, members
    )
    own = pl.pallas_call(
        functools.partial(own_kernel, scale, members),
        out_shape=[part_shape] * HALVES,
        in_specs=[SMEM, SMEM, SMEM, HBM, HBM, HBM],
        out_specs=[VMEM] * HALVES,
        scratch_shapes=[
            pltpu.VMEM((HALVES, some, columns), jnp.bfloat16),
            pltpu.VMEM(cache_store.shape, jnp.bfloat16),
            pltpu.VMEM(span_cache.shape, jnp.bfloat16),
            pltpu.SemaphoreType.DMA((2 + HALVES * members,)),
            *attention_scratch(heads, rows, head_dim, block_rows),
        ],
        compiler_params=params,
        cost_estimate=attention_cost(rows, 8 * rows, head_dim, heads),
        name="own_attention",
    )(me, span_lengths, lists, queries, cache_store, span_cache)

    own = list(own)
    before, arrived = None, []
    held, after = spread(loaded[0], own[0])
    nears = [None] + [exchange(each, 1) for each in loaded[1:]]
    *loaded[1:], after = lax.optimization_barrier((*loaded[1:], after))
    for h in range(HALVES):
        if h + 1 < HALVES:
            groups = [order[i : i + 2] for i in range(0, peers - 1, 2)]
        else:
            groups = [[k] for k in reversed(order) if k > 1] + [[1]]
            held[1], after = lax.optimization_barrier((held[1], after))
        parts, following = {}, None
        for index, group in enumerate(groups):
            results = guests(held, group, after)
            after = results[0]
            parts.update(zip(group, results))
            if index == 0 and h + 1 < HALVES:
                following, after = spread(loaded[h + 1], after, nears[h + 1])
            if index == 0 and before is not None:
                back, after = gather_back(before, after)
                arrived.append(back)
        before, held = parts, following
    back, after = gather_back(before, after)
    arrived.append(back)

    turn = lax.axis_index("tp").reshape(1)
    terms, counts = [], []
    for h in range(HALVES):
        parts = [own[h], *arrived[h]]
        cuts = 1
        near, *aways, keep = project(
            turn, span_lengths, parts, out_weight, after, heads, h, members, cuts
        )
        near, sums = add_cores(near, aways, keep, members)
        if h + 1 == HALVES:
            near, *sums = lax.optimization_barrier((near, *sums))
        crossed = add_chips(sums, cuts, members)
        if h + 1 < HALVES:
            own[h + 1], near, after = lax.optimization_barrier((own[h + 1], near, sums[0]))
        if h + 1 == HALVES:
            keep, span_cache = lax.optimization_barrier((keep, span_cache))
        terms += [keep, near, *crossed]
        counts.append((len(crossed), cuts))
    projected = total_sums(terms, counts, some // members, out_weight.shape[1])

    push_shape = jax.ShapeDtypeStruct((2, push_cap, block_rows, head_dim), jnp.bfloat16)
    outgoing = pl.pallas_call(
        pack_kernel,
        out_shape=[push_shape] * peers,
        in_specs=[SMEM, SMEM, SMEM, VMEM],
        out_specs=[VMEM] * peers,
        scratch_shapes=[
            pltpu.VMEM((peers, *push_shape.shape), jnp.bfloat16),
            pltpu.SMEM((peers,), jnp.int32),
        ],
        compiler_params=params,
        name="pack_blocks",
    )(me, span_lengths, store_owners.reshape(-1), span_cache)
    incoming = [outgoing[0], *[exchange(outgoing[k], k) for k in range(1, peers)]]
    pushed_blocks = pl.pallas_call(
        unpack_kernel,
        out_shape=jax.ShapeDtypeStruct(
            (2, peers, push_cap, block_rows, head_dim), jnp.bfloat16
        ),
        in_specs=[SMEM] + [VMEM] * peers,
        out_specs=VMEM,
        compiler_params=params,
        name="unpack_blocks",
    )(me, *incoming).reshape(2, peers * push_cap, block_rows, head_dim)
    return (projected, pushed_blocks)


def solution(mesh):
    return jax.shard_map(
        shards,
        mesh=mesh,
        in_specs=(
            P(("pods", "inst"), "tp"),
            P(None, ("pods", "inst"), None, "tp"),
            P(None, ("pods", "inst"), "tp"),
            P("tp", None),
            P(("pods", "inst")),
            P(("pods", "inst")),
            P(("pods", "inst"), None, None),
            P(("pods", "inst"), None),
            P(("pods", "inst"), None, None),
        ),
        out_specs=(P(("pods", "inst", "tp"), None), P(None, ("pods", "inst"), None, "tp")),
        check_vma=False,
    )
```

```python
import functools
import math

import jax
import jax.numpy as jnp
from jax import lax
from jax.experimental import pallas as pl
from jax.experimental.pallas import tpu as pltpu
from jax.sharding import PartitionSpec as P

LOW = -1e30
TOP = 2.0**100
TILE = 32
STACK = 512
HALVES = 2
TAIL = 8
VMEM_LIMIT = 20 * 1024 * 1024

SMEM = pl.BlockSpec(memory_space=pltpu.SMEM)
VMEM = pl.BlockSpec(memory_space=pltpu.VMEM)
HBM = pl.BlockSpec(memory_space=pltpu.HBM)


def round_up(number, step):
    return -(-number // step) * step


def original_row(row, h, members, own_rows):
    each = own_rows // HALVES
    member = sum((row >= m * each).astype(jnp.int32) for m in range(1, members))
    return row + member * (own_rows - each) + h * each


def route_kernel(
    members, live_ref, holders_in, slots_in, q_in, lists_ref, *refs
):
    out_refs, (holders_ref, slots_ref, sems) = refs[:HALVES], refs[HALVES:]
    columns = q_in.shape[1]
    rows = q_in.shape[0] // HALVES
    each = rows // members
    loading = [
        pltpu.make_async_copy(holders_in, holders_ref, sems.at[0]),
        pltpu.make_async_copy(slots_in, slots_ref, sems.at[1]),
    ]
    passing = [
        pltpu.make_async_copy(
            q_in.at[pl.ds((m * HALVES + h) * each, each)],
            out_refs[h].at[pl.ds(m * each, each)],
            sems.at[2 + h * members + m],
        )
        for h in range(HALVES)
        for m in range(members)
    ]
    for copy in loading + passing:
        copy.start()
    for copy in loading:
        copy.wait()
    peers, width = lists_ref.shape
    number = holders_ref.shape[1]
    padded = round_up(peers, 16)
    holder = lax.broadcasted_iota(jnp.int32, (padded, number), 0)
    entry = lax.broadcasted_iota(jnp.int32, (padded, number), 1)
    hot = (holders_ref[...] == holder) & (entry < live_ref[0])
    ones = jnp.where(hot, 1.0, 0.0)
    earlier = lax.broadcasted_iota(jnp.int32, (number, number), 0) < lax.broadcasted_iota(
        jnp.int32, (number, number), 1
    )
    ranks = jnp.dot(
        ones.astype(jnp.bfloat16),
        jnp.where(earlier, 1.0, 0.0).astype(jnp.bfloat16),
        preferred_element_type=jnp.float32,
    )
    rank = jnp.sum(ranks * ones, axis=0, keepdims=True)
    rank = jnp.broadcast_to(rank, (8, number)).T[:, :1].astype(jnp.int32)
    place = lax.broadcasted_iota(jnp.int32, (number, width), 1) == rank
    slots = jnp.where(hot, slots_ref[...], 0).astype(jnp.float32)
    lists = jnp.dot(
        slots.astype(jnp.bfloat16),
        jnp.where(place, 1.0, 0.0).astype(jnp.bfloat16),
        preferred_element_type=jnp.float32,
    )
    counts = jnp.sum(ones, axis=1, keepdims=True)
    last = lax.broadcasted_iota(jnp.int32, (padded, width), 1) == width - 1
    lists = jnp.where(last, counts, lists)[:peers]
    lists_ref[...] = lists.astype(jnp.int32)

    lines = columns // width
    row = lax.broadcasted_iota(jnp.int32, (TAIL, columns), 0)
    tail = jnp.zeros((TAIL, columns), jnp.float32)
    for r in range(-(-peers // lines)):
        line = [lists[h : h + 1] for h in range(r * lines, min(peers, (r + 1) * lines))]
        line += [jnp.zeros((1, width), jnp.float32)] * (lines - len(line))
        tail = jnp.where(row == r, jnp.concatenate(line, axis=1), tail)
    for out_ref in out_refs:
        out_ref[rows:, :] = tail.astype(jnp.bfloat16)
    for copy in passing:
        copy.wait()


def route(live, holders, slots, queries, peers, width, members):
    rows, columns = queries.shape[0] // HALVES, queries.shape[1]
    return pl.pallas_call(
        functools.partial(route_kernel, members),
        out_shape=(
            jax.ShapeDtypeStruct((peers, width), jnp.int32),
            *[jax.ShapeDtypeStruct((rows + TAIL, columns), jnp.bfloat16)] * HALVES,
        ),
        in_specs=[SMEM, HBM, HBM, HBM],
        out_specs=[VMEM] * (1 + HALVES),
        scratch_shapes=[
            pltpu.VMEM(holders.shape, jnp.int32),
            pltpu.VMEM(slots.shape, jnp.int32),
            pltpu.SemaphoreType.DMA((2 + HALVES * members,)),
        ],
        compiler_params=pltpu.CompilerParams(vmem_limit_bytes=62 * 1024 * 1024),
        name="route",
    )(live, holders, slots, queries)


def score(q, keys):
    return lax.dot_general(q, keys, (((1,), (1,)), ((), ())), preferred_element_type=jnp.float32)


def wide(value, width):
    return jnp.concatenate([value] * (width // value.shape[1]), axis=1)


def attend(
    slot, count, store_ref, span_ref, masks, q_ref, k_ref, v_ref, s_ref, ref_ref, acc_ref, rows,
    scale, stored=None,
):
    block_rows, head_dim = store_ref.shape[2:]
    heads = q_ref.shape[0] // rows
    stack = s_ref.shape[0]
    stacks = q_ref.shape[0] // stack
    tiles = (count + TILE - 1) // TILE

    def fetch(tile, into):
        for j in range(TILE):
            index = tile * TILE + j
            here = slot(jnp.minimum(index, count - 1))
            at = slice(j * block_rows, (j + 1) * block_rows)
            k_ref[into, at, :] = store_ref[0, here]
            block = store_ref[1, here]
            v_ref[into, at, :head_dim] = jnp.where(index < count, block, jnp.zeros_like(block))
            v_ref[into, at, head_dim:] = jnp.where(
                index < count, jnp.ones_like(block), jnp.zeros_like(block)
            )

    def one_key(key_row):
        row = key_row.astype(jnp.float32)[:1]
        return score(
            q_ref[...], jnp.broadcast_to(row, (head_dim, head_dim)).astype(jnp.bfloat16)
        )

    def start(exact):
        if span_ref is None:
            acc_ref[...] = jnp.zeros_like(acc_ref)
            if exact:
                ref_ref[...] = jnp.full_like(ref_ref, LOW)
            return
        keys = span_ref.shape[1]
        values = jnp.concatenate(
            [span_ref[1], jnp.ones((keys, head_dim), jnp.bfloat16)], axis=1
        )
        if not exact:
            ref_ref[...] = one_key(span_ref[0, :16, :])
        s = score(q_ref[:rows, :], span_ref[0])
        for g in range(heads):
            at = slice(g * rows, (g + 1) * rows)
            if g + 1 < heads:
                following = score(q_ref[(g + 1) * rows : (g + 2) * rows, :], span_ref[0])
            mask = masks[g * HALVES // heads]
            if exact:
                top = jnp.max(jnp.where(mask, s, LOW), axis=1, keepdims=True)
                ref_ref[at, :] = jnp.broadcast_to(top, (rows, head_dim))
            p = jnp.exp2((s - wide(ref_ref[at, :], keys)) * scale)
            p = jnp.where(mask, p, 0.0).astype(jnp.bfloat16)
            acc_ref[at, :] = jnp.dot(p, values, preferred_element_type=jnp.float32)
            s = following

    start(False)
    if stored is not None:
        stored()

    @pl.when(count > 0)
    def _():
        fetch(0, 0)
        if span_ref is None:
            ref_ref[...] = one_key(k_ref[0, :16, :])
        s_ref[...] = score(q_ref[:stack, :], k_ref[0])

        def step(tile, carry):
            now = lax.rem(tile, 2)
            later = 1 - now
            keys, values = k_ref[now], v_ref[now]
            s = s_ref[...]
            fetch(tile + 1, later)
            for c in range(stacks):
                at = slice(c * stack, (c + 1) * stack)
                if c + 1 < stacks:
                    following = score(q_ref[(c + 1) * stack : (c + 2) * stack, :], keys)
                else:
                    s_ref[...] = score(q_ref[:stack, :], k_ref[later])
                p = jnp.exp2((s - wide(ref_ref[at, :], s.shape[1])) * scale).astype(jnp.bfloat16)
                acc_ref[at, :] += jnp.dot(p, values, preferred_element_type=jnp.float32)
                s = following
            return carry

        lax.fori_loop(0, tiles, step, 0)
    beyond = jnp.max(jnp.where(acc_ref[:, head_dim:] < TOP, 0.0, 1.0))

    @pl.when(beyond > 0.0)
    def _():
        start(True)

        def careful(tile, carry):
            fetch(tile, 0)

            def head(g, inner):
                at = pl.ds(pl.multiple_of(g * rows, rows), rows)
                s = score(q_ref[at, :], k_ref[0])
                old = ref_ref[at, :]
                new = jnp.maximum(old, jnp.max(s, axis=1, keepdims=True))
                p = jnp.exp2((s - wide(new, s.shape[1])) * scale).astype(jnp.bfloat16)
                update = jnp.dot(p, v_ref[0], preferred_element_type=jnp.float32)
                acc_ref[at, :] = acc_ref[at, :] * wide(jnp.exp2((old - new) * scale), 2 * head_dim) + update
                ref_ref[at, :] = new
                return inner

            return lax.fori_loop(0, heads, head, carry)

        lax.fori_loop(0, tiles, careful, 0)


def stack_heads(queries_ref, q_ref, rows, first=0):
    head_dim = q_ref.shape[1]
    for g in range(queries_ref.shape[1] // head_dim):
        q_ref[(first + g) * rows : (first + g + 1) * rows, :] = queries_ref[
            :rows, g * head_dim : (g + 1) * head_dim
        ]


def write_logs(out_ref, logs):
    heads, rows = logs.shape
    first = logs.astype(jnp.bfloat16).astype(jnp.float32)
    rest = logs - first
    second = rest.astype(jnp.bfloat16).astype(jnp.float32)
    third = rest - second
    spare = jnp.zeros((heads, out_ref.shape[1] - 3 * rows), jnp.float32)
    lines = jnp.concatenate([first, second, third, spare], axis=1)
    if heads < TAIL:
        more = jnp.zeros((TAIL - heads, out_ref.shape[1]), jnp.float32)
        lines = jnp.concatenate([lines, more], axis=0)
    out_ref[rows:, :] = lines.astype(jnp.bfloat16)


def read_logs(part_ref, heads, rows):
    lines = part_ref[rows:, :].astype(jnp.float32)[:heads]
    return lines[:, :rows] + lines[:, rows : 2 * rows] + lines[:, 2 * rows : 3 * rows]


def finish(out_refs, ref_ref, acc_ref, rows, scale):
    head_dim = ref_ref.shape[1]
    heads = ref_ref.shape[0] // rows // len(out_refs)
    lane = lax.broadcasted_iota(jnp.int32, (rows, head_dim), 1)
    for h, out_ref in enumerate(out_refs):
        totals = jnp.ones((rows, head_dim), jnp.float32)
        tops = jnp.zeros((rows, head_dim), jnp.float32)
        for g in range(heads):
            at = slice((h * heads + g) * rows, (h * heads + g + 1) * rows)
            total = acc_ref[at, head_dim:]
            inverse = pl.reciprocal(total, approx=True)
            inverse = inverse * (2.0 - total * inverse)
            out_ref[:rows, g * head_dim : (g + 1) * head_dim] = (
                acc_ref[at, :head_dim] * inverse
            ).astype(jnp.bfloat16)
            totals = jnp.where(lane == g, total, totals)
            tops = jnp.where(lane == g, ref_ref[at, :], tops)
        logs = tops * scale + jnp.log2(totals)
        write_logs(out_ref, logs.T[:heads])


def own_kernel(
    scale, members, me_ref, span_live_ref, lists_ref, queries_in, store_in, span_in, *refs
):
    out_refs = refs[:HALVES]
    queries_ref, store_ref, span_ref, sems, q_ref, k_ref, v_ref, s_ref, ref_ref, acc_ref = refs[
        HALVES:
    ]
    me = me_ref[0]
    rows = queries_ref.shape[1]
    each = rows // members
    copies = [
        pltpu.make_async_copy(span_in, span_ref, sems.at[0]),
        pltpu.make_async_copy(store_in, store_ref, sems.at[1]),
    ] + [
        pltpu.make_async_copy(
            queries_in.at[pl.ds((m * HALVES + h) * each, each)],
            queries_ref.at[h, pl.ds(m * each, each)],
            sems.at[2 + h * members + m],
        )
        for h in range(HALVES)
        for m in range(members)
    ]
    for copy in copies:
        copy.start()
    keys = span_ref.shape[1]
    key = lax.broadcasted_iota(jnp.int32, (rows, keys), 1)
    row = lax.broadcasted_iota(jnp.int32, (rows, keys), 0)
    masks = [
        (key <= original_row(row, h, members, each * HALVES)) & (key < span_live_ref[0])
        for h in range(HALVES)
    ]
    for copy in copies[2:]:
        copy.wait()
    for h in range(HALVES):
        stack_heads(queries_ref.at[h], q_ref, rows, h * queries_ref.shape[2] // q_ref.shape[1])
    copies[0].wait()
    attend(
        lambda index: lists_ref[me, index], lists_ref[me, lists_ref.shape[1] - 1], store_ref,
        span_ref, masks, q_ref, k_ref, v_ref, s_ref, ref_ref, acc_ref, rows, scale,
        copies[1].wait,
    )
    finish(out_refs, ref_ref, acc_ref, rows, scale)


def guest_kernel(scale, width, rows, number, me_ref, *refs):
    loaded_refs, store_ref = refs[:number], refs[number]
    out_refs = refs[number + 2 : 2 * number + 2]
    wide_ref, list_ref, sem_ref, q_ref, k_ref, v_ref, s_ref, ref_ref, acc_ref = refs[
        2 * number + 2 :
    ]
    each = loaded_refs[0].shape[1] // width
    me = me_ref[0]
    lane = pl.multiple_of(lax.rem(me, each) * width, 128)
    for which, loaded_ref in enumerate(loaded_refs):
        riders = loaded_ref[rows:, pl.ds(lane, width)].astype(jnp.float32)
        row = lax.broadcasted_iota(jnp.int32, riders.shape, 0)
        mine = jnp.sum(jnp.where(row == me // each, riders, 0.0), axis=0, keepdims=True)
        wide_ref[which : which + 1, :] = mine.astype(jnp.int32)
    copy = pltpu.make_async_copy(wide_ref, list_ref, sem_ref)
    copy.start()
    stack_heads(loaded_refs[0], q_ref, rows)
    copy.wait()
    for which, (loaded_ref, out_ref) in enumerate(zip(loaded_refs, out_refs)):
        count = list_ref[which, width - 1]

        @pl.when(count > 0)
        def _():
            if which:
                stack_heads(loaded_ref, q_ref, rows)
            attend(
                lambda index: list_ref[which, index], count, store_ref, None, None,
                q_ref, k_ref, v_ref, s_ref, ref_ref, acc_ref, rows, scale,
            )
            finish([out_ref], ref_ref, acc_ref, rows, scale)

        @pl.when(count == 0)
        def _():
            out_ref[...] = jnp.zeros_like(out_ref)
            write_logs(out_ref, jnp.full((q_ref.shape[0] // rows, rows), LOW, jnp.float32))


def attention_scratch(heads, rows, head_dim, block_rows):
    keys = TILE * block_rows
    return [
        pltpu.VMEM((heads * rows, head_dim), jnp.bfloat16),
        pltpu.VMEM((2, keys, head_dim), jnp.bfloat16),
        pltpu.VMEM((2, keys, 2 * head_dim), jnp.bfloat16),
        pltpu.VMEM((math.gcd(heads * rows, STACK), keys), jnp.float32),
        pltpu.VMEM((heads * rows, head_dim), jnp.float32),
        pltpu.VMEM((heads * rows, 2 * head_dim), jnp.float32),
    ]


def attention_cost(rows, keys, head_dim, heads):
    return pl.CostEstimate(
        flops=4 * rows * keys * head_dim * heads,
        bytes_accessed=64 * 1024,
        transcendentals=rows * keys * heads,
    )


def merged(parts, heads, rows):
    logs = [read_logs(part, heads, rows) for part in parts]
    top = functools.reduce(jnp.maximum, logs)
    weights = [jnp.exp2(log - top) for log in logs]
    total = functools.reduce(jnp.add, weights)
    return [weight / total for weight in weights], top + jnp.log2(total)


def weighted(parts, weights, g, head_dim, rows):
    total = jnp.zeros((rows, head_dim), jnp.float32)
    for part, weight in zip(parts, weights):
        part_rows = part[:rows, g * head_dim : (g + 1) * head_dim]
        total += part_rows.astype(jnp.float32) * weight[:, g : g + 1]
    return total.astype(jnp.bfloat16)


def merge_kernel(heads, number, *refs):
    parts, out_ref = refs[:number], refs[number + 1]
    rows = out_ref.shape[0] - TAIL
    head_dim = out_ref.shape[1] // heads
    weights, logs = merged(parts, heads, rows)
    weights = [weight.T for weight in weights]
    for g in range(heads):
        out_ref[:rows, g * head_dim : (g + 1) * head_dim] = weighted(
            parts, weights, g, head_dim, rows
        )
    write_logs(out_ref, logs)


def project_kernel(heads, number, h, members, cuts, turn_ref, span_live_ref, *refs):
    parts = refs[:number]
    weight_ref, after_ref, near_ref, *away_refs = refs[number : number + 3 + cuts]
    keep_ref, att_ref, sorted_ref, held_ref, sems = refs[number + 3 + cuts :]
    rows, features = att_ref.shape
    chunks, _, width = held_ref.shape
    head_dim = features // heads
    copies = [
        pltpu.make_async_copy(weight_ref.at[:, pl.ds(i * width, width)], held_ref.at[i], sems.at[i])
        for i in range(chunks)
    ]
    for copy in copies:
        copy.start()

    row = lax.broadcasted_iota(jnp.int32, (heads, rows), 1)
    live = original_row(row, h, members, rows * HALVES // members) < span_live_ref[0]
    weights, _ = merged(parts, heads, rows)
    weights = [jnp.where(live, weight, 0.0).T for weight in weights]
    for g in range(heads):
        att_ref[:, g * head_dim : (g + 1) * head_dim] = weighted(
            parts, weights, g, head_dim, rows
        )

    chips = keep_ref.shape[0]
    block = keep_ref.shape[1]
    chip, core = turn_ref[0] // 2, lax.rem(turn_ref[0], 2)
    for side, wanted in enumerate((1 - core, core)):
        for k in range(chips):
            owner = 2 * lax.rem(chip + k, chips) + wanted
            at = (side * chips + k) * block
            sorted_ref[at : at + block, :] = att_ref[
                pl.ds(pl.multiple_of(owner * block, block), block), :
            ]
    for i in range(chunks):
        copies[i].wait()
        at = slice(i * width, (i + 1) * width)
        product = jnp.dot(
            sorted_ref[...], held_ref[i], preferred_element_type=jnp.float32
        ).astype(jnp.bfloat16)
        for k in range(chips):
            leaving = product[k * block : (k + 1) * block]
            if k:
                cut = i * cuts // chunks
                first = i * width - cut * away_refs[cut].shape[2]
                away_refs[cut][k - 1, :, first : first + width] = leaving
            else:
                near_ref[:, at] = leaving
            keep_ref[k, :, at] = product[(chips + k) * block : (chips + k + 1) * block]


def project(turn, span_live, parts, out_weight, after, heads, h, members, cuts):
    features, outputs = out_weight.shape
    rows = parts[0].shape[0] - TAIL
    width = 512
    chunks = outputs // width
    chips, block = members // 2, rows // members
    return pl.pallas_call(
        functools.partial(project_kernel, heads, len(parts), h, members, cuts),
        out_shape=[
            jax.ShapeDtypeStruct(shape, jnp.bfloat16)
            for shape in (
                (block, outputs),
                *[(chips - 1, block, outputs // cuts)] * cuts,
                (chips, block, outputs),
            )
        ],
        in_specs=[SMEM, SMEM] + [VMEM] * len(parts) + [HBM, pl.BlockSpec(memory_space=pl.ANY)],
        out_specs=[VMEM] * (2 + cuts),
        scratch_shapes=[
            pltpu.VMEM((rows, features), jnp.bfloat16),
            pltpu.VMEM((rows, features), jnp.bfloat16),
            pltpu.VMEM((chunks, features, width), jnp.bfloat16),
            pltpu.SemaphoreType.DMA((chunks,)),
        ],
        compiler_params=pltpu.CompilerParams(vmem_limit_bytes=48 * 1024 * 1024),
        cost_estimate=pl.CostEstimate(
            flops=2 * rows * features * outputs,
            bytes_accessed=2 * (features + rows) * outputs,
            transcendentals=0,
        ),
        name="project",
    )(turn, span_live, *parts, out_weight, after)


def add_kernel(cuts, kept_ref, *refs):
    come_refs, out_refs = refs[:cuts], refs[cuts:]
    width = kept_ref.shape[2] // cuts
    for k in range(kept_ref.shape[0] - 1):
        for cut, come_ref in enumerate(come_refs):
            kept = kept_ref[k + 1, :, cut * width : (cut + 1) * width].astype(jnp.float32)
            out_refs[k * cuts + cut][...] = (kept + come_ref[k].astype(jnp.float32)).astype(
                jnp.bfloat16
            )


def total_kernel(counts, *refs):
    out_ref = refs[-1]
    block, width = out_ref.shape[0] // HALVES, out_ref.shape[1]
    first = 0
    for h, (others, cuts) in enumerate(counts):
        kept_ref, near_ref = refs[first : first + 2]
        arrived = refs[first + 2 : first + 2 + others]
        first += 2 + others
        for cut in range(cuts):
            at = slice(cut * width // cuts, (cut + 1) * width // cuts)
            total = kept_ref[0, :, at].astype(jnp.float32) + near_ref[:, at].astype(jnp.float32)
            for ref in arrived[cut::cuts]:
                total += ref[...].astype(jnp.float32)
            out_ref[h * block : (h + 1) * block, at] = total.astype(jnp.bfloat16)


def add_cores(near, aways, keep, members):
    chips, block, outputs = keep.shape
    cuts = len(aways)
    shape = jax.ShapeDtypeStruct((block, outputs // cuts), jnp.bfloat16)
    pairs = [(i, i ^ 1) for i in range(members)]
    come = [lax.ppermute(away, "tp", pairs) for away in aways]
    near = lax.ppermute(near, "tp", pairs)
    sums = pl.pallas_call(
        functools.partial(add_kernel, cuts),
        out_shape=[shape] * ((chips - 1) * cuts),
        in_specs=[VMEM] * (1 + cuts),
        out_specs=[VMEM] * ((chips - 1) * cuts),
        compiler_params=pltpu.CompilerParams(vmem_limit_bytes=VMEM_LIMIT),
        name="add_cores",
    )(keep, *come)
    return near, sums


def add_chips(sums, cuts, members):
    return [
        lax.ppermute(
            each, "tp", [(i, (i + 2 * (n // cuts + 1)) % members) for i in range(members)]
        )
        for n, each in enumerate(sums)
    ]


def total_sums(terms, counts, block, outputs):
    return pl.pallas_call(
        functools.partial(total_kernel, counts),
        out_shape=jax.ShapeDtypeStruct((HALVES * block, outputs), jnp.bfloat16),
        in_specs=[VMEM] * len(terms),
        out_specs=VMEM,
        compiler_params=pltpu.CompilerParams(vmem_limit_bytes=VMEM_LIMIT),
        name="total",
    )(*terms)


def pack_kernel(me_ref, span_live_ref, owners_ref, span_ref, *refs):
    out_refs, (out_ref, counts_ref) = refs[:-2], refs[-2:]
    peers = out_ref.shape[0]
    block_rows, head_dim = out_ref.shape[3:]
    out_ref[...] = jnp.zeros_like(out_ref)
    for k in range(peers):
        counts_ref[k] = 0
    row = lax.broadcasted_iota(jnp.int32, (block_rows, head_dim), 0)
    for b in range(span_ref.shape[1] // block_rows):
        owner = owners_ref[b]
        rank = counts_ref[owner]
        counts_ref[owner] = rank + 1
        keep = row + b * block_rows < span_live_ref[0]
        for side in range(2):
            block = span_ref[side, b * block_rows : (b + 1) * block_rows, :]
            out_ref[owner, side, rank] = jnp.where(keep, block, jnp.zeros_like(block))
    for k, each_ref in enumerate(out_refs):
        each_ref[...] = out_ref[me_ref[0] ^ k]


def unpack_kernel(me_ref, *refs):
    for k, each_ref in enumerate(refs[:-1]):
        refs[-1][:, me_ref[0] ^ k] = each_ref[...]


def shards(
    queries,
    cache_store,
    span_cache,
    out_weight,
    prefix_blocks,
    span_lengths,
    hit_holders,
    hit_slots,
    store_owners,
):
    peers = lax.axis_size("inst")
    block_rows, head_dim = cache_store.shape[2:]
    rows, columns = queries.shape
    heads = columns // head_dim
    block_max = hit_slots.shape[1]
    cap = max(2, block_max * 5 // (4 * peers))
    new_count = rows // block_rows
    push_cap = max(2, 2 * new_count // peers)
    scale = math.log2(math.e) / math.sqrt(head_dim)
    me = lax.axis_index("inst").reshape(1)
    width = round_up(cap + 1, 128)
    members = lax.axis_size("tp")
    some = rows // HALVES
    part_shape = jax.ShapeDtypeStruct((some + TAIL, columns), jnp.bfloat16)
    params = pltpu.CompilerParams(vmem_limit_bytes=VMEM_LIMIT)
    anywhere = pl.BlockSpec(memory_space=pl.ANY)

    def exchange(value, bit):
        return lax.ppermute(value, "inst", [(i, i ^ bit) for i in range(peers)])

    order = sorted(range(1, peers), key=lambda k: -(k & -k))

    def spread(loaded, after, near=None):
        held = {0: loaded}
        for k in order:
            if k == 1 and near is not None:
                held[k] = near
                continue
            source = held[k & (k - 1)]
            if k & (k - 1):
                source, after = lax.optimization_barrier((source, after))
            held[k] = exchange(source, k & -k)
        return held, after

    def guests(held, group, after):
        return pl.pallas_call(
            functools.partial(guest_kernel, scale, width, some, len(group)),
            out_shape=[part_shape] * len(group),
            in_specs=[SMEM] + [VMEM] * (len(group) + 1) + [anywhere],
            out_specs=[VMEM] * len(group),
            scratch_shapes=[
                pltpu.VMEM((len(group), width), jnp.int32),
                pltpu.SMEM((len(group), width), jnp.int32),
                pltpu.SemaphoreType.DMA,
                *attention_scratch(heads, some, head_dim, block_rows),
            ],
            compiler_params=params,
            cost_estimate=attention_cost(some, rows // 2, head_dim, heads),
            name="guest_attention",
        )(me, *[held[k] for k in group], cache_store, after)

    def gather_back(parts, after):
        parts = dict(parts)
        for k in reversed(order):
            arrived = [exchange(parts[c], c & -c) for c in order if c & (c - 1) == k]
            if arrived:
                parts[k] = after = pl.pallas_call(
                    functools.partial(merge_kernel, heads, len(arrived) + 1),
                    out_shape=part_shape,
                    in_specs=[VMEM] * (len(arrived) + 1) + [anywhere],
                    out_specs=VMEM,
                    compiler_params=params,
                    name="merge",
                )(parts[k], *arrived, after)
        parts[1], after = lax.optimization_barrier((parts[1], after))
        return [exchange(parts[k], k) for k in order if k & (k - 1) == 0], after

    lists, *loaded = route(
        prefix_blocks, hit_holders.reshape(1, -1), hit_slots, queries, peers, width, members
    )
    own = pl.pallas_call(
        functools.partial(own_kernel, scale, members),
        out_shape=[part_shape] * HALVES,
        in_specs=[SMEM, SMEM, SMEM, HBM, HBM, HBM],
        out_specs=[VMEM] * HALVES,
        scratch_shapes=[
            pltpu.VMEM((HALVES, some, columns), jnp.bfloat16),
            pltpu.VMEM(cache_store.shape, jnp.bfloat16),
            pltpu.VMEM(span_cache.shape, jnp.bfloat16),
            pltpu.SemaphoreType.DMA((2 + HALVES * members,)),
            *attention_scratch(heads, rows, head_dim, block_rows),
        ],
        compiler_params=params,
        cost_estimate=attention_cost(rows, 8 * rows, head_dim, heads),
        name="own_attention",
    )(me, span_lengths, lists, queries, cache_store, span_cache)

    own = list(own)
    before, arrived = None, []
    held, after = spread(loaded[0], own[0])
    nears = [None] + [exchange(each, 1) for each in loaded[1:]]
    *loaded[1:], after = lax.optimization_barrier((*loaded[1:], after))
    for h in range(HALVES):
        if h + 1 < HALVES:
            groups = [order[i : i + 2] for i in range(0, peers - 1, 2)]
        else:
            groups = [[k] for k in reversed(order) if k > 1]
            groups[-1].append(1)
            held[1], after = lax.optimization_barrier((held[1], after))
        parts, following = {}, None
        for index, group in enumerate(groups):
            results = guests(held, group, after)
            after = results[0]
            parts.update(zip(group, results))
            if index == 0 and h + 1 < HALVES:
                following, after = spread(loaded[h + 1], after, nears[h + 1])
            if index == 0 and before is not None:
                back, after = gather_back(before, after)
                arrived.append(back)
        before, held = parts, following
    back, after = gather_back(before, after)
    arrived.append(back)

    turn = lax.axis_index("tp").reshape(1)
    terms, counts = [], []
    for h in range(HALVES):
        parts = [own[h], *arrived[h]]
        cuts = 1
        near, *aways, keep = project(
            turn, span_lengths, parts, out_weight, after, heads, h, members, cuts
        )
        near, sums = add_cores(near, aways, keep, members)
        if h + 1 == HALVES:
            near, *sums = lax.optimization_barrier((near, *sums))
        crossed = add_chips(sums, cuts, members)
        if h + 1 < HALVES:
            own[h + 1], near, after = lax.optimization_barrier((own[h + 1], near, sums[0]))
        if h + 1 == HALVES:
            keep, span_cache = lax.optimization_barrier((keep, span_cache))
        terms += [keep, near, *crossed]
        counts.append((len(crossed), cuts))
    projected = total_sums(terms, counts, some // members, out_weight.shape[1])

    push_shape = jax.ShapeDtypeStruct((2, push_cap, block_rows, head_dim), jnp.bfloat16)
    outgoing = pl.pallas_call(
        pack_kernel,
        out_shape=[push_shape] * peers,
        in_specs=[SMEM, SMEM, SMEM, VMEM],
        out_specs=[VMEM] * peers,
        scratch_shapes=[
            pltpu.VMEM((peers, *push_shape.shape), jnp.bfloat16),
            pltpu.SMEM((peers,), jnp.int32),
        ],
        compiler_params=params,
        name="pack_blocks",
    )(me, span_lengths, store_owners.reshape(-1), span_cache)
    incoming = [outgoing[0], *[exchange(outgoing[k], k) for k in range(1, peers)]]
    pushed_blocks = pl.pallas_call(
        unpack_kernel,
        out_shape=jax.ShapeDtypeStruct(
            (2, peers, push_cap, block_rows, head_dim), jnp.bfloat16
        ),
        in_specs=[SMEM] + [VMEM] * peers,
        out_specs=VMEM,
        compiler_params=params,
        name="unpack_blocks",
    )(me, *incoming).reshape(2, peers * push_cap, block_rows, head_dim)
    return (projected, pushed_blocks)


def solution(mesh):
    return jax.shard_map(
        shards,
        mesh=mesh,
        in_specs=(
            P(("pods", "inst"), "tp"),
            P(None, ("pods", "inst"), None, "tp"),
            P(None, ("pods", "inst"), "tp"),
            P("tp", None),
            P(("pods", "inst")),
            P(("pods", "inst")),
            P(("pods", "inst"), None, None),
            P(("pods", "inst"), None),
            P(("pods", "inst"), None, None),
        ),
        out_specs=(P(("pods", "inst", "tp"), None), P(None, ("pods", "inst"), None, "tp")),
        check_vma=False,
    )
```
